32 devices in a mesh: dp: 4 (over y, core), expert: 8 (over z, x).
Axes of the slice: x: 2, y: 2, z: 4, core: 2. Of those that a mesh axis runs over, the one named last changes fastest.
Arguments:
- tokens: bfloat16 [4096, 2048], P(('dp', 'expert')), may hold values from -6 to 6
- out_grad: bfloat16 [4096, 2048], P(('dp', 'expert')), may hold values from -6 to 6
- expert_ids: int32 [4096, 8], P(('dp', 'expert')), may hold values from 0 to 127, all different within a row; in each aligned block of 128 rows (0 to 127, 128 to 255, ...) at most 10 rows name the same one
- gates: bfloat16 [4096, 8], P(('dp', 'expert')), may hold values from 0.049804688 to 0.59765625
- expert_weights: bfloat16 [8, 3, 2048, 384], P('expert', None, 'dp'), may hold values from -0.125 to 0.125
Outputs:
- token_grads: bfloat16 [4096, 2048], P(('dp', 'expert'))
- weight_grads: float32 [8, 3, 2048, 384], P('expert', None, 'dp')
The draws below stay inside these ranges and needn't reach their ends.
Inputs may be any that keep to these rules, and one draw needn't show every extreme that they name: `expert_ids`: each row names 8 different experts; among the 128 rows of one device no expert is named more than 10 times, a bound that some block reaches.
All inputs are finite; a program needn't handle non-finite values.
Results may differ from the reference program's by a relative error of at most 0.0065.
Values may be sent and summed in bfloat16 or wider, within the bound.
No kernel may reach another device: no remote copies, remote signals or barrier semaphores. Data moves between devices by JAX's collectives and lax.ppermute only.
A program may use at most 64 MiB of HBM per device.

```python
import math
import jax
import jax.numpy as jnp
import numpy as np
from jax import lax

D = 2048
EXPERTS = 128
TOP = 8
FF = 384
TOK_DEV = 128
SLOTS = 10
WIN = 8
TOKENS = 4096
N_DP = 4
N_EXPERT = 8


def steps_of(key, extent, shards, low, top_value):
    loudness, own = 1.0, jax.random.fold_in(key, 6)
    for axis_at, blocks in shards:
        heights = jnp.exp(jax.random.uniform(jax.random.fold_in(own, axis_at), (blocks,), jnp.float32, low / len(shards), top_value / len(shards)))
        loudness = loudness * jnp.repeat(heights, extent[axis_at] // blocks).reshape([-1 if axis == axis_at else 1 for axis in range(len(extent))])
    return loudness


def routed_block(own_key, own, number, rows, amount, top, reach, slope):
    order = jax.random.permutation(own_key, amount)
    crowded, common = shares(amount, rows * top, reach, slope, True), shares(amount, rows * top, reach, slope, False)
    places = jnp.arange(amount)

    def named(lengths, offset_by):
        used = int((lengths > 0).sum())
        fixed = max(1, used // 4)
        passed = fixed + (places - fixed + offset_by * (used - fixed)) % max(1, amount - fixed)
        return jnp.zeros((amount,), jnp.int32).at[order[jnp.where(places < fixed, places, passed)]].set(jnp.asarray(lengths, jnp.int32))

    lengths = jnp.where(number % 4 == 0, named(crowded, number // 4), named(common, number - number // 4 - 1))
    mixed = jax.random.permutation(jax.random.fold_in(own, 3), amount)
    giver, receiver = mixed[0:amount // 2 * 2:2], mixed[1:amount // 2 * 2:2]
    margin = jnp.minimum(lengths[giver] - 1, reach - lengths[receiver]) // 2
    margin = jnp.where((giver == order[0]) | (receiver == order[0]) | (lengths[receiver] == 0), 0, jnp.maximum(margin, 0))
    passed = jax.random.randint(jax.random.fold_in(own, 4), (amount // 2,), 0, 1 << 20) % (margin + 1)
    lengths = lengths.at[giver].add(-passed).at[receiver].add(passed)
    labels = jnp.searchsorted(jnp.cumsum(lengths), jnp.arange(rows * top), side="right").astype(jnp.int32)
    listing = labels.reshape(top, rows).T
    listing = listing[jax.random.permutation(jax.random.fold_in(own, 1), rows)]
    offset_by = jax.random.randint(jax.random.fold_in(own, 2), (rows, 1), 0, top)
    return jnp.take_along_axis(listing, (jnp.arange(top)[None, :] + offset_by) % top, axis=1)


def shares(amount, total, limit, slope, full):
    loads = [(1 << 20) // math.isqrt(rank ** slope) + 1 for rank in range(1, amount + 1)]
    largest = limit if full else min(limit, max(-(-total // amount), total * loads[0] // sum(loads)))
    least = 1 if total - largest >= amount - 1 else 0
    given, spare = [largest] + [least] * (amount - 1), total - largest - least * (amount - 1)
    while spare > 0:
        free = [i for i in range(1, amount) if given[i] < largest] or [i for i in range(1, amount) if given[i] < limit]
        mass, budget = sum([loads[i] for i in free]), spare
        for i in free:
            extra = min(limit - given[i], max(1, budget * loads[i] // mass), spare)
            given[i] = given[i] + extra
            spare = spare - extra
    return np.array(given)


def gaussian(stream_key, extent, scale, limit, split=(), kind=jnp.bfloat16):
    values = scale * jax.random.normal(stream_key, extent, jnp.float32)
    if split:
        values = values * steps_of(stream_key, extent, split, -0.22, 0.18)
    return jnp.clip(values, -limit, limit).astype(kind)


def setup_inputs(seed: int = 0) -> dict:
    key_of = jax.random.split(jax.random.key(seed), 6)
    tokens = gaussian(key_of[0], (TOKENS, D), 1.0, 6.0, ((0, 32),))
    out_grad = gaussian(key_of[1], (TOKENS, D), 1.0, 6.0, ((0, 32),))
    expert_ids_keys = jax.random.split(jax.random.fold_in(key_of[2], 1), TOKENS // TOK_DEV)
    expert_ids_turns = jax.random.permutation(jax.random.fold_in(key_of[2], 3), TOKENS // TOK_DEV)
    expert_ids = jax.vmap(lambda own, number: routed_block(jax.random.fold_in(key_of[2], 2), own, number, TOK_DEV, EXPERTS, TOP, SLOTS, 2))(expert_ids_keys, expert_ids_turns).reshape((TOKENS, TOP))
    gates = jnp.clip(0.049804688 + 0.54785156 * jax.random.uniform(key_of[3], (TOKENS, TOP), jnp.float32) ** steps_of(key_of[3], (TOKENS, TOP), ((0, 32),), -0.2, 0.2), 0.049804688, 0.59765625).astype(jnp.bfloat16)
    expert_weights = gaussian(key_of[4], (WIN, 3, D, FF), D ** -0.5, 0.125, ((0, 8), (2, 4)))
    return {"tokens": tokens, "out_grad": out_grad, "expert_ids": expert_ids, "gates": gates, "expert_weights": expert_weights}


def route_tables(expert_ids, gates, window):
    token_rows, top_count = expert_ids.shape
    flat_ids = expert_ids.reshape(token_rows * top_count)
    onehot = (flat_ids[:, None] == jnp.arange(EXPERTS, dtype=jnp.int32)[None, :]).astype(jnp.int32)
    before = jnp.cumsum(onehot, axis=0) - onehot
    slot_index = jnp.sum(before * onehot, axis=1)
    target = jnp.where(flat_ids < window, flat_ids * SLOTS + slot_index, -1)
    picked = (target[None, :] == jnp.arange(window * SLOTS, dtype=jnp.int32)[:, None]).astype(jnp.float32)
    picked = picked.reshape(window * SLOTS, token_rows, top_count)
    token_table = jnp.sum(picked, axis=2).astype(jnp.bfloat16)
    gate_table = jnp.sum(picked * gates.astype(jnp.float32)[None, :, :], axis=2).astype(jnp.bfloat16)
    return token_table, gate_table


def expert_backward(expert_item):
    expert_rows, expert_grads, weights = expert_item
    w_gate, w_up, w_down = weights[0], weights[1], weights[2]
    gate_act = jnp.dot(expert_rows, w_gate, preferred_element_type=jnp.float32)
    up_act = jnp.dot(expert_rows, w_up, preferred_element_type=jnp.float32)
    logistic = jax.nn.sigmoid(gate_act)
    swish_out = gate_act * logistic
    hidden = (swish_out * up_act).astype(jnp.bfloat16)
    grad_hidden = jnp.dot(expert_grads, w_down, preferred_element_type=jnp.float32)
    grad_up = (grad_hidden * swish_out).astype(jnp.bfloat16)
    grad_gate = (grad_hidden * up_act * logistic * (1.0 + gate_act * (1.0 - logistic))).astype(jnp.bfloat16)
    expert_back = (jnp.dot(grad_gate, w_gate.T, preferred_element_type=jnp.float32)
                   + jnp.dot(grad_up, w_up.T, preferred_element_type=jnp.float32)).astype(jnp.bfloat16)
    gate_part = jnp.dot(expert_rows.T, grad_gate, preferred_element_type=jnp.float32).astype(jnp.bfloat16)
    up_part = jnp.dot(expert_rows.T, grad_up, preferred_element_type=jnp.float32).astype(jnp.bfloat16)
    down_part = jnp.dot(expert_grads.T, hidden, preferred_element_type=jnp.float32).astype(jnp.bfloat16)
    return expert_back, jnp.stack([gate_part, up_part, down_part])


def reference(tokens, out_grad, expert_ids, gates, expert_weights):
    window = N_EXPERT

    def group_step(grad_total, group_data):
        rows_group, grads_group, ids_group, gates_group = group_data

        def tables_of(block_ids, block_gates):
            return route_tables(block_ids, block_gates, window)

        token_tables, gate_tables = jax.vmap(tables_of)(ids_group, gates_group)
        sent_rows = jnp.einsum("jst,jtd->jsd", token_tables.astype(jnp.float32), rows_group.astype(jnp.float32)).astype(jnp.bfloat16)
        sent_grads = jnp.einsum("jst,jtd->jsd", gate_tables.astype(jnp.float32), grads_group.astype(jnp.float32)).astype(jnp.bfloat16)
        rows_by_expert = sent_rows.reshape(window, window, SLOTS, D).transpose(1, 0, 2, 3).reshape(window, window * SLOTS, D)
        grads_by_expert = sent_grads.reshape(window, window, SLOTS, D).transpose(1, 0, 2, 3).reshape(window, window * SLOTS, D)
        expert_back, parts = lax.map(expert_backward, (rows_by_expert, grads_by_expert, expert_weights))
        grad_total = grad_total + parts.astype(jnp.float32)
        returned = expert_back.reshape(window, window, SLOTS, D).transpose(1, 0, 2, 3).reshape(window, window * SLOTS, D)
        token_grads = jnp.einsum("jst,jsd->jtd", token_tables.astype(jnp.float32), returned.astype(jnp.float32)).astype(jnp.bfloat16)
        return grad_total, token_grads

    inputs = (tokens.reshape(N_DP, N_EXPERT, TOK_DEV, D), out_grad.reshape(N_DP, N_EXPERT, TOK_DEV, D),
              expert_ids.reshape(N_DP, N_EXPERT, TOK_DEV, TOP), gates.reshape(N_DP, N_EXPERT, TOK_DEV, TOP))
    grad_total, token_grads = lax.scan(group_step, jnp.zeros((window, 3, D, FF), jnp.float32), inputs)
    return token_grads.reshape(TOKENS, D), grad_total
```

```python
import jax
import jax.numpy as jnp
from jax import lax
from jax.sharding import PartitionSpec as P

EXPERTS = 128
SLOTS = 10
LANES = 128
BOTH = ("dp", "expert")


def route_tables(expert_ids, gates, window):
    token_rows, top_count = expert_ids.shape
    flat_ids = expert_ids.reshape(token_rows * top_count)
    onehot = (flat_ids[:, None] == jnp.arange(EXPERTS, dtype=jnp.int32)[None, :]).astype(jnp.int32)
    before = jnp.cumsum(onehot, axis=0) - onehot
    slot_index = jnp.sum(before * onehot, axis=1)
    target = jnp.where(flat_ids < window, flat_ids * SLOTS + slot_index, -1)
    picked = (target[None, :] == jnp.arange(window * SLOTS, dtype=jnp.int32)[:, None]).astype(
        jnp.float32
    )
    picked = picked.reshape(window * SLOTS, token_rows, top_count)
    token_table = jnp.sum(picked, axis=2).astype(jnp.bfloat16)
    gate_table = jnp.sum(picked * gates.astype(jnp.float32)[None, :, :], axis=2).astype(
        jnp.bfloat16
    )
    return (token_table, gate_table)


def inner_rows(first_op, second_op):
    return lax.dot_general(
        first_op, second_op, (((0,), (0,)), ((), ())), preferred_element_type=jnp.float32
    )


def inner_cols(first_op, second_op):
    return lax.dot_general(
        first_op, second_op, (((1,), (1,)), ((), ())), preferred_element_type=jnp.float32
    )


def swap(value, bit, groups):
    return lax.ppermute(value, "dp", [(i, i ^ bit) for i in range(groups)])


def on_device(tokens, out_grad, expert_ids, gates, expert_weights):
    window = lax.axis_size("expert")
    groups = lax.axis_size("dp")
    model_width = tokens.shape[1]
    hidden_units = expert_weights.shape[3]
    owned = model_width // groups
    chunks = owned // LANES
    devices = window * groups
    rows = devices * SLOTS
    bf16 = jnp.bfloat16
    token_table, gate_table = route_tables(expert_ids, gates, window)
    sent_rows = jnp.dot(token_table, tokens, preferred_element_type=jnp.float32).astype(bf16)
    sent_grads = jnp.dot(gate_table, out_grad, preferred_element_type=jnp.float32).astype(bf16)
    sent = jnp.stack([sent_rows, sent_grads]).reshape(2, window, SLOTS, groups, chunks, LANES)
    sent = sent.transpose(3, 1, 4, 0, 2, 5).reshape(devices, chunks * 2 * SLOTS, LANES)
    got = lax.all_to_all(sent, BOTH, split_axis=0, concat_axis=0, tiled=True)
    got = got.reshape(devices, chunks, 2, SLOTS, LANES).transpose(2, 0, 3, 1, 4)
    got = got.reshape(2, rows, owned)
    expert_rows, expert_grads = got[0], got[1]
    w_gate, w_up, w_down = expert_weights[0, 0], expert_weights[0, 1], expert_weights[0, 2]
    partial = jnp.stack(
        [
            jnp.dot(expert_rows, w_gate, preferred_element_type=jnp.float32),
            jnp.dot(expert_rows, w_up, preferred_element_type=jnp.float32),
            jnp.dot(expert_grads, w_down, preferred_element_type=jnp.float32),
        ]
    )
    half = rows // 2
    side = lax.axis_index("dp") % 2
    kept = lax.dynamic_slice_in_dim(partial, side * half, half, axis=1)
    given = lax.dynamic_slice_in_dim(partial, (1 - side) * half, half, axis=1)
    total = kept + swap(given.astype(bf16), 1, groups).astype(jnp.float32)
    bit = 2
    while bit < groups:
        total = total + swap(total.astype(bf16), bit, groups).astype(jnp.float32)
        bit *= 2
    gate_act, up_act, grad_hidden = total[0], total[1], total[2]
    logistic = jax.nn.sigmoid(gate_act)
    swish_out = gate_act * logistic
    hidden = swish_out * up_act
    grad_up = grad_hidden * swish_out
    grad_gate = grad_hidden * up_act * logistic * (1.0 + gate_act * (1.0 - logistic))
    mine = jnp.stack([grad_gate, grad_up, hidden]).astype(bf16)
    other = swap(mine, 1, groups)
    first = jnp.where(side == 0, mine, other)
    second = jnp.where(side == 0, other, mine)
    full = jnp.concatenate([first, second], axis=1)
    grad_gate, grad_up, hidden = full[0], full[1], full[2]
    expert_back = (inner_cols(grad_gate, w_gate) + inner_cols(grad_up, w_up)).astype(bf16)
    back = expert_back.reshape(devices, SLOTS, chunks, LANES).transpose(0, 2, 1, 3)
    back = back.reshape(devices, chunks * SLOTS, LANES)
    returned = lax.all_to_all(back, BOTH, split_axis=0, concat_axis=0, tiled=True)
    returned = returned.reshape(groups, window, chunks, SLOTS, LANES).transpose(1, 3, 0, 2, 4)
    returned = returned.reshape(window * SLOTS, model_width)
    token_grads = inner_rows(token_table, returned).astype(bf16)
    weight_grads = jnp.stack(
        [
            inner_rows(expert_rows, grad_gate),
            inner_rows(expert_rows, grad_up),
            inner_rows(expert_grads, hidden),
        ]
    )
    return (token_grads, weight_grads[None])


def solution(mesh):
    return jax.shard_map(
        on_device,
        mesh=mesh,
        in_specs=(
            P(("dp", "expert"), None),
            P(("dp", "expert"), None),
            P(("dp", "expert"), None),
            P(("dp", "expert"), None),
            P("expert", None, "dp", None),
        ),
        out_specs=(P(("dp", "expert"), None), P("expert", None, "dp", None)),
        check_vma=False,
    )
```

```python
import jax
import jax.numpy as jnp
from jax import lax
from jax.sharding import PartitionSpec as P

EXPERTS = 128
SLOTS = 10
LANES = 256


def route_tables(expert_ids, gates, window, me):
    token_rows, top_count = expert_ids.shape
    flat_ids = expert_ids.reshape(token_rows * top_count)
    onehot = (flat_ids[:, None] == jnp.arange(EXPERTS, dtype=jnp.int32)[None, :]).astype(jnp.int32)
    before = jnp.cumsum(onehot, axis=0) - onehot
    slot_index = jnp.sum(before * onehot, axis=1)
    target = jnp.where(flat_ids < window, (flat_ids ^ me) * SLOTS + slot_index, -1)
    picked = (target[None, :] == jnp.arange(window * SLOTS, dtype=jnp.int32)[:, None]).astype(
        jnp.float32
    )
    picked = picked.reshape(window * SLOTS, token_rows, top_count)
    token_table = jnp.sum(picked, axis=2).astype(jnp.bfloat16)
    gate_table = jnp.sum(picked * gates.astype(jnp.float32)[None, :, :], axis=2).astype(
        jnp.bfloat16
    )
    return (token_table, gate_table)


def inner_rows(first_op, second_op):
    return lax.dot_general(
        first_op, second_op, (((0,), (0,)), ((), ())), preferred_element_type=jnp.float32
    )


def inner_cols(first_op, second_op):
    return lax.dot_general(
        first_op, second_op, (((1,), (1,)), ((), ())), preferred_element_type=jnp.float32
    )


def dot(first_op, second_op):
    return jnp.dot(first_op, second_op, preferred_element_type=jnp.float32)


def swap(value, axis, bit):
    return lax.ppermute(value, axis, [(i, i ^ bit) for i in range(lax.axis_size(axis))])


def pack(rows, window):
    parts, _, width = rows.shape
    chunks = width // LANES
    blocks = rows.reshape(parts, window, SLOTS, chunks, LANES).transpose(1, 0, 3, 2, 4)
    return blocks.reshape(window, parts * chunks * SLOTS, LANES)


def unpack(blocks, parts):
    window, _, _ = blocks.shape
    blocks = blocks.reshape(window, parts, -1, SLOTS, LANES).transpose(1, 0, 3, 2, 4)
    return blocks.reshape(parts, window * SLOTS, -1)


def exchange(blocks):
    window = blocks.shape[0]
    order = sorted(range(1, window), reverse=True)
    got = {0: blocks[0]}
    for k in order:
        got[k] = swap(blocks[k], "expert", k)
    return jnp.stack([got[k] for k in range(window)])


def on_device(tokens, out_grad, expert_ids, gates, expert_weights):
    window = lax.axis_size("expert")
    groups = lax.axis_size("dp")
    sides = groups // 2
    me = lax.axis_index("dp")
    model_width = tokens.shape[1]
    hidden_units = expert_weights.shape[3]
    owned = model_width // groups
    bf16 = jnp.bfloat16
    f32 = jnp.float32

    w_gate, w_up, w_down = expert_weights[0, 0], expert_weights[0, 1], expert_weights[0, 2]
    gates_of, ups_of = {0: w_gate}, {0: w_up}
    for b in range(2, groups, 2):
        gates_of[b] = swap(w_gate, "dp", b)
    for b in range(2, groups, 2):
        ups_of[b] = swap(w_up, "dp", b)
    for b in range(0, groups, 2):
        gates_of[b ^ 1] = swap(gates_of[b], "dp", 1)
        ups_of[b ^ 1] = swap(ups_of[b], "dp", 1)
    down_other = swap(w_down, "dp", 1)

    token_table, gate_table = route_tables(expert_ids, gates, window, lax.axis_index("expert"))
    sent_rows = dot(token_table, tokens).astype(bf16)
    sent_grads = dot(gate_table, out_grad).astype(bf16)
    rows_here = window * SLOTS
    expert_rows = unpack(exchange(pack(sent_rows[None], window)), 1)[0]

    side = me // 2
    part = model_width // sides

    def part_of(value, index, size):
        return lax.dynamic_slice_in_dim(value, index * size, size, axis=value.ndim - 1)

    by_side = [part_of(sent_grads, side, part)]
    for b in range(1, sides):
        by_side.append(swap(part_of(sent_grads, side ^ b, part), "dp", 2 * b))
    expert_grads = unpack(exchange(pack(jnp.stack(by_side), window)), sides)
    flat_grads = expert_grads.reshape(sides * rows_here, part)
    odd = me % 2
    hidden_part = dot(part_of(flat_grads, odd, owned), w_down) + dot(
        part_of(flat_grads, 1 - odd, owned), down_other
    )
    hidden_part = hidden_part.reshape(sides, rows_here, hidden_units)
    grad_hidden = hidden_part[0]
    for b in range(1, sides):
        grad_hidden = grad_hidden + swap(hidden_part[b].astype(bf16), "dp", 2 * b).astype(f32)

    slices = {b: part_of(expert_rows, me ^ b, owned) for b in range(groups)}
    gate_act = sum(dot(slices[b], gates_of[b]) for b in range(groups))
    up_act = sum(dot(slices[b], ups_of[b]) for b in range(groups))

    logistic = jax.nn.sigmoid(gate_act)
    swish_out = gate_act * logistic
    hidden = (swish_out * up_act).astype(bf16)
    grad_up = (grad_hidden * swish_out).astype(bf16)
    grad_gate = (grad_hidden * up_act * logistic * (1.0 + gate_act * (1.0 - logistic))).astype(bf16)

    back = jnp.zeros((rows_here, groups, owned), bf16)
    pieces = [
        (inner_cols(grad_gate, gates_of[b]) + inner_cols(grad_up, ups_of[b])).astype(bf16)
        for b in range(groups)
    ]
    back = jnp.stack([pieces[0]] * groups, axis=1)
    index = jnp.arange(groups)[None, :, None] ^ me
    for b in range(1, groups):
        back = jnp.where(index == b, pieces[b][:, None, :], back)
    back = back.reshape(rows_here, model_width)
    returned = unpack(exchange(pack(back[None], window)), 1)[0]
    token_grads = inner_rows(token_table, returned).astype(bf16)

    all_rows = [slices[0]] + [swap(slices[b], "dp", b) for b in range(1, groups)]
    grads_mine = part_of(expert_grads, odd, owned)
    grads_other = swap(part_of(expert_grads, 1 - odd, owned), "dp", 1)
    acts = jnp.stack([grad_gate, grad_up, hidden])
    all_acts = {0: acts}
    for b in range(2, groups, 2):
        all_acts[b] = swap(acts, "dp", b)
    for b in range(0, groups, 2):
        all_acts[b ^ 1] = swap(all_acts[b], "dp", 1)
    rows_cat = jnp.concatenate(all_rows)
    grads_cat = jnp.concatenate(
        [(grads_mine if b % 2 == 0 else grads_other)[b // 2] for b in range(groups)]
    )
    acts_cat = jnp.concatenate([all_acts[b] for b in range(groups)], axis=1)
    weight_grads = jnp.stack(
        [
            inner_rows(rows_cat, acts_cat[0]),
            inner_rows(rows_cat, acts_cat[1]),
            inner_rows(grads_cat, acts_cat[2]),
        ]
    )
    return (token_grads, weight_grads[None])


def solution(mesh):
    return jax.shard_map(
        on_device,
        mesh=mesh,
        in_specs=(
            P(("dp", "expert"), None),
            P(("dp", "expert"), None),
            P(("dp", "expert"), None),
            P(("dp", "expert"), None),
            P("expert", None, "dp", None),
        ),
        out_specs=(P(("dp", "expert"), None), P("expert", None, "dp", None)),
        check_vma=False,
    )
```

```python
import jax
import jax.numpy as jnp
import numpy as np
from jax import lax
from jax.experimental import pallas as pl
from jax.experimental.pallas import tpu as pltpu
from jax.sharding import Mesh, PartitionSpec as P

SLOTS = 10
LANES = 128
JOIN = 4
VMEM_LIMIT = 60 * 2**20
F32 = jnp.float32
BF16 = jnp.bfloat16


def dot(first_op, second_op):
    return jnp.dot(first_op, second_op, preferred_element_type=F32)


def dot_tn(first_op, second_op):
    return lax.dot_general(first_op, second_op, (((0,), (0,)), ((), ())), preferred_element_type=F32)


def dot_nt(first_op, second_op):
    return lax.dot_general(first_op, second_op, (((1,), (1,)), ((), ())), preferred_element_type=F32)


def swap(value, axis, bit):
    return lax.ppermute(value, axis, [(i, i ^ bit) for i in range(lax.axis_size(axis))])


def piece_rows(chunks):
    return -(-chunks * SLOTS // 8) * 8


def params():
    return pltpu.CompilerParams(vmem_limit_bytes=VMEM_LIMIT)


def cost(flops, moved):
    return pl.CostEstimate(flops=flops, bytes_accessed=moved, transcendentals=0)


def sort_matrix(parts, chunks):
    padded = piece_rows(chunks)
    matrix = np.zeros((parts * chunks * JOIN * SLOTS, JOIN * parts * padded), np.float32)
    for part in range(parts):
        for chunk in range(chunks):
            for source in range(JOIN):
                for slot in range(SLOTS):
                    matrix[
                        ((part * chunks + chunk) * JOIN + source) * SLOTS + slot,
                        (source * parts + part) * padded + chunk * SLOTS + slot,
                    ] = 1
    return matrix


def table_of(code, values, chunks, padded):
    window, token_rows = code.shape
    spots = lax.broadcasted_iota(jnp.int32, (padded, chunks * token_rows), 0).astype(F32)
    tables = []
    for expert in range(window):
        own = code[expert : expert + 1]
        wide = jnp.concatenate([own + float(SLOTS * c) for c in range(chunks)], axis=1)
        hit = spots == wide
        row = []
        for value in values:
            if value is None:
                row.append(jnp.where(hit, 1.0, 0.0))
            else:
                gate = jnp.concatenate([value[expert : expert + 1]] * chunks, axis=1)
                row.append(jnp.where(hit, gate, 0.0))
        tables.append(row)
    return [jnp.concatenate([t[i] for t in tables], axis=0) for i in range(len(values))]


def pack_kernel(groups, window, ids_ref, gates_ref, tokens_ref, grads_ref, sent_ref, code_ref):
    token_rows, model_width = tokens_ref.shape
    owned = model_width // groups
    chunks = owned // LANES
    padded = piece_rows(chunks)
    above = lax.broadcasted_iota(jnp.int32, (token_rows, token_rows), 0)
    along = lax.broadcasted_iota(jnp.int32, (token_rows, token_rows), 1)
    eye = jnp.where(above == along, 1.0, 0.0).astype(BF16)
    earlier = jnp.where(above < along, 1.0, 0.0).astype(BF16)
    ids = dot_tn(ids_ref[...].astype(F32).astype(BF16), eye)
    gates = dot_tn(gates_ref[...], eye)
    members, chosen = [], []
    for expert in range(window):
        hit = ids == float(expert)
        members.append(jnp.sum(jnp.where(hit, 1.0, 0.0), axis=0, keepdims=True))
        chosen.append(jnp.sum(jnp.where(hit, gates, 0.0), axis=0, keepdims=True))
    members = jnp.concatenate(members, axis=0)
    chosen = jnp.concatenate(chosen, axis=0)
    code = jnp.where(members > 0.0, dot(members.astype(BF16), earlier), -1e6)
    code_ref[...] = code
    table, gated = table_of(code, [None, chosen], chunks, padded)

    def columns(ref):
        return jnp.concatenate(
            [
                jnp.concatenate(
                    [ref[:, d * owned + c * LANES : d * owned + (c + 1) * LANES] for d in range(groups)],
                    axis=1,
                )
                for c in range(chunks)
            ],
            axis=0,
        )

    rows = dot(table.astype(BF16), columns(tokens_ref))
    grads = dot(gated.astype(BF16), columns(grads_ref))
    for d in range(groups):
        lanes = slice(d * LANES, (d + 1) * LANES)
        for expert in range(window):
            lines = slice(expert * padded, (expert + 1) * padded)
            block = jnp.concatenate([rows[lines, lanes], grads[lines, lanes]], axis=0)
            sent_ref[d * window + expert] = block.astype(BF16)


def table_kernel(chunks, code_ref, table_ref):
    (table,) = table_of(code_ref[...], [None], chunks, piece_rows(chunks))
    table_ref[...] = table.T.astype(BF16)


def partial_kernel(got_ref, sort_ref, weights_ref, rows_ref, grads_ref, out_ref):
    sources, height, _ = got_ref.shape
    owned, hidden_units = weights_ref.shape[1:]
    chunks = owned // LANES
    joined = sources // JOIN
    tall = JOIN * SLOTS
    blocks = jnp.concatenate(
        [
            got_ref[q * JOIN : (q + 1) * JOIN].reshape(JOIN * height, LANES)
            for q in range(joined)
        ],
        axis=1,
    )
    lines = dot(sort_ref[...], blocks)

    def gathered(part):
        return jnp.concatenate(
            [
                jnp.concatenate(
                    [
                        lines[
                            (part * chunks + c) * tall : (part * chunks + c + 1) * tall,
                            q * LANES : (q + 1) * LANES,
                        ]
                        for c in range(chunks)
                    ],
                    axis=1,
                )
                for q in range(joined)
            ],
            axis=0,
        ).astype(BF16)

    rows, grads = gathered(0), gathered(1)
    rows_ref[...] = rows
    grads_ref[...] = grads
    out_ref[:, :hidden_units] = dot(rows, weights_ref[0])
    out_ref[:, hidden_units : 2 * hidden_units] = dot(rows, weights_ref[1])
    out_ref[:, 2 * hidden_units :] = dot(grads, weights_ref[2])


def acts_kernel(*refs):
    own_ref, out_ref = refs[0], refs[-1]
    total = own_ref[...]
    for ref in refs[1:-1]:
        total = total + ref[...].astype(F32)
    hidden_units = total.shape[1] // 3
    gate_act = total[:, :hidden_units]
    up_act = total[:, hidden_units : 2 * hidden_units]
    grad_hidden = total[:, 2 * hidden_units :]
    logistic = jax.nn.sigmoid(gate_act)
    swish_out = gate_act * logistic
    out_ref[:, 2 * hidden_units :] = (swish_out * up_act).astype(BF16)
    out_ref[:, hidden_units : 2 * hidden_units] = (grad_hidden * swish_out).astype(BF16)
    out_ref[:, :hidden_units] = (
        grad_hidden * up_act * logistic * (1.0 + gate_act * (1.0 - logistic))
    ).astype(BF16)


def back_kernel(*refs):
    own_ref, other_ref, unsort_ref, weights_ref = refs[:4]
    far_refs, out_ref = refs[4:-1], refs[-1]
    owned, hidden_units = weights_ref.shape[1:]
    chunks = owned // LANES
    padded = piece_rows(chunks)
    sides = len(far_refs) + 1
    core = lax.axis_index("core")
    own = own_ref[:, : 2 * hidden_units]
    other = other_ref[:, : 2 * hidden_units]
    acts = jnp.concatenate(
        [jnp.where(core == 0, own, other), jnp.where(core == 0, other, own)], axis=0
    )
    tall = JOIN * SLOTS
    joined = acts.shape[0] // tall
    backs = []
    for ref in (weights_ref,) + tuple(far_refs):
        both = jnp.concatenate([ref[0], ref[1]], axis=1)
        backs.append(dot_nt(acts, both))
    lines = jnp.concatenate(
        [
            jnp.concatenate(
                [
                    backs[b][q * tall : (q + 1) * tall, c * LANES : (c + 1) * LANES]
                    for b in range(sides)
                    for c in range(chunks)
                ],
                axis=0,
            )
            for q in range(joined)
        ],
        axis=1,
    ).astype(BF16)
    blocks = dot(unsort_ref[...], lines).astype(BF16)
    height = sides * padded
    for q in range(joined):
        for j in range(JOIN):
            out_ref[q * JOIN + j] = blocks[j * height : (j + 1) * height, q * LANES : (q + 1) * LANES]


def combine_kernel(returned_ref, table_ref, out_ref):
    token_rows, model_width = out_ref.shape
    columns, lines = table_ref.shape
    chunks = columns // token_rows
    padded = piece_rows(chunks)
    window = lines // padded
    sides = returned_ref.shape[1] // padded
    owned = chunks * LANES
    side = lax.axis_index("side")
    pieces = []
    for core in range(2):
        part = returned_ref[core * window : (core + 1) * window].astype(F32)
        for b in range(sides):
            piece = part[:, b * padded : (b + 1) * padded].reshape(lines, LANES)
            pieces.append((core, b, piece.astype(BF16)))
    spread = jnp.concatenate([piece for _, _, piece in pieces], axis=1)
    result = dot(table_ref[...], spread).astype(BF16)
    for at, (core, b, _) in enumerate(pieces):
        start = ((side ^ b) * 2 + core) * owned
        for c in range(chunks):
            out_ref[:, pl.ds(pl.multiple_of(start + c * LANES, LANES), LANES)] = result[
                c * token_rows : (c + 1) * token_rows, at * LANES : (at + 1) * LANES
            ]


def grads_kernel(*refs):
    rows_ref, grads_ref = refs[:2]
    acts_refs, out_ref, acts = refs[2:-2], refs[-2], refs[-1]
    hidden_units = out_ref.shape[3]
    per_group = acts_refs[0].shape[0]
    group = lax.axis_index("side") * 2 + lax.axis_index("core")
    for b, ref in enumerate(acts_refs):
        acts[pl.ds(pl.multiple_of((group ^ b) * per_group, 16), per_group), :] = ref[...]
    out_ref[0, 0] = dot_tn(rows_ref[...], acts[:, :hidden_units])
    out_ref[0, 1] = dot_tn(rows_ref[...], acts[:, hidden_units : 2 * hidden_units])
    out_ref[0, 2] = dot_tn(grads_ref[...], acts[:, 2 * hidden_units :])


def on_device(tokens, out_grad, expert_ids, gates, expert_weights):
    window = lax.axis_size("expert")
    sides = lax.axis_size("side")
    groups = sides * 2
    devices = groups * window
    token_rows, model_width = tokens.shape
    hidden_units = expert_weights.shape[3]
    owned = model_width // groups
    chunks = owned // LANES
    padded = piece_rows(chunks)
    rows_here = window * SLOTS
    weights = expert_weights[0]
    side, core = lax.axis_index("side"), lax.axis_index("core")

    far_weights = [swap(weights[:2], "side", b) for b in range(1, sides)]

    sent, code = pl.pallas_call(
        lambda *refs: pack_kernel(groups, window, *refs),
        out_shape=(
            jax.ShapeDtypeStruct((devices, 2 * padded, LANES), BF16),
            jax.ShapeDtypeStruct((window, token_rows), F32),
        ),
        compiler_params=params(),
    )(expert_ids, gates, tokens, out_grad)
    got = lax.all_to_all(sent, ("side", "core", "expert"), split_axis=0, concat_axis=0, tiled=True)
    table = pl.pallas_call(
        lambda *refs: table_kernel(chunks, *refs),
        out_shape=jax.ShapeDtypeStruct((chunks * token_rows, window * padded), BF16),
        compiler_params=params(),
    )(code)

    per = min(devices, 32)
    sort = jnp.asarray(sort_matrix(2, chunks), BF16)
    expert_rows, expert_grads, partial = pl.pallas_call(
        partial_kernel,
        grid=(devices // per,),
        in_specs=[
            pl.BlockSpec((per, 2 * padded, LANES), lambda i: (i, 0, 0)),
            pl.BlockSpec(sort.shape, lambda i: (0, 0)),
            pl.BlockSpec(weights.shape, lambda i: (0, 0, 0)),
        ],
        out_specs=[
            pl.BlockSpec((per * SLOTS, owned), lambda i: (i, 0)),
            pl.BlockSpec((per * SLOTS, owned), lambda i: (i, 0)),
            pl.BlockSpec((per * SLOTS, 3 * hidden_units), lambda i: (i, 0)),
        ],
        out_shape=(
            jax.ShapeDtypeStruct((devices * SLOTS, owned), BF16),
            jax.ShapeDtypeStruct((devices * SLOTS, owned), BF16),
            jax.ShapeDtypeStruct((devices * SLOTS, 3 * hidden_units), F32),
        ),
        compiler_params=params(),
    )(got, sort, weights)

    partial = partial.reshape(sides, 2, rows_here, 3 * hidden_units)
    kept = lax.dynamic_index_in_dim(partial, core, 1, keepdims=False)
    given = lax.dynamic_index_in_dim(partial, 1 - core, 1, keepdims=False)
    summed = kept + swap(given.astype(BF16), "core", 1).astype(F32)
    own = lax.dynamic_index_in_dim(summed, side, 0, keepdims=False)
    arrived = []
    for b in range(1, sides):
        leaving = lax.dynamic_index_in_dim(summed, side ^ b, 0, keepdims=False)
        arrived.append(swap(leaving.astype(BF16), "side", b))
    acts = pl.pallas_call(
        acts_kernel,
        out_shape=jax.ShapeDtypeStruct((rows_here, 3 * hidden_units), BF16),
        compiler_params=params(),
    )(own, *arrived)

    other = swap(acts, "core", 1)
    unsort = jnp.asarray(sort_matrix(sides, chunks).T, BF16)
    back = pl.pallas_call(
        back_kernel,
        out_shape=jax.ShapeDtypeStruct((2 * window, sides * padded, LANES), BF16),
        compiler_params=params(),
    )(acts, other, unsort, weights, *far_weights)
    returned = lax.all_to_all(back, ("core", "expert"), split_axis=0, concat_axis=0, tiled=True)

    all_acts = [acts, other]
    for b in range(1, sides):
        far = swap(acts, "side", b)
        all_acts += [far, swap(far, "core", 1)]
    weight_grads = pl.pallas_call(
        grads_kernel,
        out_shape=jax.ShapeDtypeStruct((1, 3, owned, hidden_units), F32),
        scratch_shapes=[pltpu.VMEM((groups * rows_here, 3 * hidden_units), BF16)],
        compiler_params=params(),
        cost_estimate=cost(6 * devices * SLOTS * owned * hidden_units, 12 * owned * hidden_units),
    )(expert_rows, expert_grads, *all_acts)

    token_grads = pl.pallas_call(
        combine_kernel,
        out_shape=jax.ShapeDtypeStruct((token_rows, model_width), BF16),
        compiler_params=params(),
    )(returned, table)
    return (token_grads, weight_grads)


def solution(mesh):
    groups, window = mesh.devices.shape
    split = Mesh(mesh.devices.reshape(groups // 2, 2, window), ("side", "core", "expert"))
    lines = P(("side", "core", "expert"), None)
    slabs = P("expert", None, ("side", "core"), None)
    return jax.shard_map(
        on_device,
        mesh=split,
        in_specs=(lines, lines, lines, lines, slabs),
        out_specs=(lines, slabs),
        check_vma=False,
    )
```

```python
import jax
import jax.numpy as jnp
from jax import lax
from jax.experimental import pallas as pl
from jax.experimental.pallas import tpu as pltpu
from jax.sharding import Mesh, PartitionSpec as P

SLOTS = 10
LANES = 128
VMEM_LIMIT = 32 * 2**20
F32 = jnp.float32
BF16 = jnp.bfloat16


def dot(first_op, second_op):
    return jnp.dot(first_op, second_op, preferred_element_type=F32)


def dot_tn(first_op, second_op):
    return lax.dot_general(first_op, second_op, (((0,), (0,)), ((), ())), preferred_element_type=F32)


def dot_nt(first_op, second_op):
    return lax.dot_general(first_op, second_op, (((1,), (1,)), ((), ())), preferred_element_type=F32)


def swap(value, axis, bit):
    return lax.ppermute(value, axis, [(i, i ^ bit) for i in range(lax.axis_size(axis))])


def piece_rows(chunks):
    return -(-chunks * SLOTS // 8) * 8


def params():
    return pltpu.CompilerParams(vmem_limit_bytes=VMEM_LIMIT)


def table_of(code, values, chunks, padded):
    window, token_rows = code.shape
    spots = lax.broadcasted_iota(jnp.int32, (padded, chunks * token_rows), 0).astype(F32)
    tables = []
    for expert in range(window):
        own = code[expert : expert + 1]
        wide = jnp.concatenate([own + float(SLOTS * c) for c in range(chunks)], axis=1)
        hit = spots == wide
        row = []
        for value in values:
            if value is None:
                row.append(jnp.where(hit, 1.0, 0.0))
            else:
                gate = jnp.concatenate([value[expert : expert + 1]] * chunks, axis=1)
                row.append(jnp.where(hit, gate, 0.0))
        tables.append(row)
    return [jnp.concatenate([t[i] for t in tables], axis=0) for i in range(len(values))]


def pack_kernel(groups, window, ids_ref, gates_ref, tokens_ref, grads_ref, sent_ref, code_ref):
    token_rows, model_width = tokens_ref.shape
    owned = model_width // groups
    chunks = owned // LANES
    padded = piece_rows(chunks)
    above = lax.broadcasted_iota(jnp.int32, (token_rows, token_rows), 0)
    along = lax.broadcasted_iota(jnp.int32, (token_rows, token_rows), 1)
    earlier = jnp.where(above < along, 1.0, 0.0).astype(BF16)
    ids = ids_ref[...]
    gates = gates_ref[...].astype(F32)
    members, chosen = [], []
    for expert in range(window):
        hit = ids == expert
        members.append(jnp.sum(jnp.where(hit, 1.0, 0.0), axis=0, keepdims=True))
        chosen.append(jnp.sum(jnp.where(hit, gates, 0.0), axis=0, keepdims=True))
    members = jnp.concatenate(members, axis=0)
    chosen = jnp.concatenate(chosen, axis=0)
    code = jnp.where(members > 0.0, dot(members.astype(BF16), earlier), -1e6)
    code_ref[...] = code
    table, gated = table_of(code, [None, chosen], chunks, padded)

    def columns(ref):
        return jnp.concatenate(
            [
                jnp.concatenate(
                    [ref[:, d * owned + c * LANES : d * owned + (c + 1) * LANES] for d in range(groups)],
                    axis=1,
                )
                for c in range(chunks)
            ],
            axis=0,
        )

    rows = dot(table.astype(BF16), columns(tokens_ref))
    grads = dot(gated.astype(BF16), columns(grads_ref))
    for d in range(groups):
        lanes = slice(d * LANES, (d + 1) * LANES)
        for expert in range(window):
            lines = slice(expert * padded, (expert + 1) * padded)
            block = jnp.concatenate([rows[lines, lanes], grads[lines, lanes]], axis=0)
            sent_ref[d * window + expert] = block.astype(BF16)


def on_device(tokens, out_grad, expert_ids, gates, expert_weights):
    window = lax.axis_size("expert")
    sides = lax.axis_size("side")
    groups = sides * 2
    devices = groups * window
    token_rows, model_width = tokens.shape
    hidden_units = expert_weights.shape[3]
    owned = model_width // groups
    chunks = owned // LANES
    used = chunks * SLOTS
    padded = piece_rows(chunks)
    rows_here = window * SLOTS
    side, core = lax.axis_index("side"), lax.axis_index("core")
    w_gate, w_up, w_down = expert_weights[0, 0], expert_weights[0, 1], expert_weights[0, 2]

    far_weights = [swap(expert_weights[0, :2], "side", b) for b in range(1, sides)]

    sent, code = pl.pallas_call(
        lambda *refs: pack_kernel(groups, window, *refs),
        out_shape=(
            jax.ShapeDtypeStruct((devices, 2 * padded, LANES), BF16),
            jax.ShapeDtypeStruct((window, token_rows), F32),
        ),
        compiler_params=params(),
    )(expert_ids.T, gates.T, tokens, out_grad)
    got = lax.all_to_all(sent, ("side", "core", "expert"), split_axis=0, concat_axis=0, tiled=True)
    slots = jnp.arange(SLOTS, dtype=F32)[None, :, None]
    token_table = (code[:, None, :] == slots).astype(BF16).reshape(rows_here, token_rows)
    got, far_weights = lax.optimization_barrier((got, far_weights))

    got = got.reshape(devices, 2, padded, LANES)[:, :, :used]
    got = got.reshape(devices, 2, chunks, SLOTS, LANES).transpose(1, 0, 3, 2, 4)
    got = got.reshape(2, devices * SLOTS, owned)
    expert_rows, expert_grads = got[0], got[1]
    partial = jnp.stack(
        [dot(expert_rows, w_gate), dot(expert_rows, w_up), dot(expert_grads, w_down)]
    )

    partial = partial.reshape(3, sides, 2, rows_here, hidden_units)
    kept = lax.dynamic_index_in_dim(partial, core, 2, keepdims=False)
    given = lax.dynamic_index_in_dim(partial, 1 - core, 2, keepdims=False)
    summed = kept + swap(given.astype(BF16), "core", 1).astype(F32)
    total = lax.dynamic_index_in_dim(summed, side, 1, keepdims=False)
    for b in range(1, sides):
        leaving = lax.dynamic_index_in_dim(summed, side ^ b, 1, keepdims=False)
        total = total + swap(leaving.astype(BF16), "side", b).astype(F32)
    gate_act, up_act, grad_hidden = total[0], total[1], total[2]
    logistic = jax.nn.sigmoid(gate_act)
    swish_out = gate_act * logistic
    hidden = swish_out * up_act
    grad_up = grad_hidden * swish_out
    grad_gate = grad_hidden * up_act * logistic * (1.0 + gate_act * (1.0 - logistic))
    acts = jnp.stack([grad_gate, grad_up, hidden]).astype(BF16)

    other = swap(acts, "core", 1)
    chip = jnp.stack([jnp.where(core == 0, acts, other), jnp.where(core == 0, other, acts)], axis=1)
    chip = chip.reshape(3, 2 * rows_here, hidden_units)
    backs = [
        (dot_nt(chip[0], gate) + dot_nt(chip[1], up)).astype(BF16)
        for gate, up in [(w_gate, w_up)] + [(far[0], far[1]) for far in far_weights]
    ]
    back = jnp.stack(backs).reshape(sides, 2 * window, SLOTS, chunks, LANES)
    back = back.transpose(1, 0, 3, 2, 4).reshape(2 * window, sides * used, LANES)
    returned = lax.all_to_all(back, ("core", "expert"), split_axis=0, concat_axis=0, tiled=True)

    near = chip.reshape(3, 2, rows_here, hidden_units)
    all_acts = jnp.zeros((3, sides, 2, rows_here, hidden_units), BF16)
    all_acts = lax.dynamic_update_index_in_dim(all_acts, near, side, 1)
    for b in range(1, sides):
        far = swap(acts, "side", b)
        far_other = swap(far, "core", 1)
        far = jnp.stack(
            [jnp.where(core == 0, far, far_other), jnp.where(core == 0, far_other, far)], axis=1
        )
        all_acts = lax.dynamic_update_index_in_dim(all_acts, far, side ^ b, 1)
    all_acts = all_acts.reshape(3, devices * SLOTS, hidden_units)
    weight_grads = jnp.stack(
        [
            dot_tn(expert_rows, all_acts[0]),
            dot_tn(expert_rows, all_acts[1]),
            dot_tn(expert_grads, all_acts[2]),
        ]
    )

    returned = returned.reshape(2, window, sides, chunks, SLOTS, LANES).transpose(1, 4, 2, 0, 3, 5)
    order = jnp.arange(sides) ^ side
    returned = jnp.take(returned, order, axis=2).reshape(rows_here, model_width)
    token_grads = dot_tn(token_table, returned).astype(BF16)
    return (token_grads, weight_grads[None])


def solution(mesh):
    groups, window = mesh.devices.shape
    split = Mesh(mesh.devices.reshape(groups // 2, 2, window), ("side", "core", "expert"))
    lines = P(("side", "core", "expert"), None)
    slabs = P("expert", None, ("side", "core"), None)
    return jax.shard_map(
        on_device,
        mesh=split,
        in_specs=(lines, lines, lines, lines, slabs),
        out_specs=(lines, slabs),
        check_vma=False,
    )
```

```python
import jax
import jax.numpy as jnp
from jax import lax
from jax.experimental import pallas as pl
from jax.experimental.pallas import tpu as pltpu
from jax.sharding import Mesh, PartitionSpec as P

SLOTS = 10
LANES = 128
JOIN = 4
F32 = jnp.float32
BF16 = jnp.bfloat16


def dot(first_op, second_op):
    return jnp.dot(first_op, second_op, preferred_element_type=F32)


def dot_tn(first_op, second_op):
    return lax.dot_general(first_op, second_op, (((0,), (0,)), ((), ())), preferred_element_type=F32)


def dot_nt(first_op, second_op):
    return lax.dot_general(first_op, second_op, (((1,), (1,)), ((), ())), preferred_element_type=F32)


def swap(value, axis, bit):
    return lax.ppermute(value, axis, [(i, i ^ bit) for i in range(lax.axis_size(axis))])


def piece_rows(chunks):
    return -(-chunks * SLOTS // 8) * 8


def params(arrays, scratch=0):
    moved = sum(a.size * a.dtype.itemsize for a in arrays) + scratch
    return pltpu.CompilerParams(vmem_limit_bytes=min(56 * 2**20, 12 * 2**20 + 3 * moved))


def cost(flops, moved):
    return pl.CostEstimate(flops=flops, bytes_accessed=moved, transcendentals=0)


def lower(value, by):
    return jnp.floor((value + 0.5) * (1.0 / by))


def sort_matrix(parts, chunks, transposed):
    padded = piece_rows(chunks)
    wide, tall = JOIN * parts * padded, parts * chunks * JOIN * SLOTS
    shape, axis = ((wide, tall), 0) if transposed else ((tall, wide), 1)
    line = (wide, 1) if transposed else (1, wide)
    place = lax.broadcasted_iota(jnp.int32, line, axis).astype(F32)
    block = lower(place, padded)
    inside = place - block * padded
    source = lower(block, parts)
    part = block - source * parts
    chunk = lower(inside, SLOTS)
    slot = inside - chunk * SLOTS
    target = ((part * chunks + chunk) * JOIN + source) * SLOTS + slot
    target = jnp.where(chunk < chunks, target, -1.0)
    spots = lax.broadcasted_iota(jnp.int32, shape, 1 - axis).astype(F32)
    return jnp.where(spots == target, 1.0, 0.0).astype(BF16)


def table_of(code, values, chunks, padded):
    window, token_rows = code.shape
    spots = lax.broadcasted_iota(jnp.int32, (padded, chunks * token_rows), 0).astype(F32)
    tables = []
    for expert in range(window):
        own = code[expert : expert + 1]
        wide = jnp.concatenate([own + float(SLOTS * c) for c in range(chunks)], axis=1)
        hit = spots == wide
        row = []
        for value in values:
            if value is None:
                row.append(jnp.where(hit, 1.0, 0.0))
            else:
                gate = jnp.concatenate([value[expert : expert + 1]] * chunks, axis=1)
                row.append(jnp.where(hit, gate, 0.0))
        tables.append(row)
    return [jnp.concatenate([t[i] for t in tables], axis=0) for i in range(len(values))]


def pack_kernel(
    groups, window, ids_in, gates_in, tokens_in, grads_in, sent_ref, code_ref, ids_ref, gates_ref, tokens_ref, grads_ref, sems
):
    copies = [
        pltpu.make_async_copy(source, target, sems.at[at])
        for at, (source, target) in enumerate(
            [(ids_in, ids_ref), (gates_in, gates_ref), (tokens_in, tokens_ref), (grads_in, grads_ref)]
        )
    ]
    for copy in copies:
        copy.start()
    token_rows, model_width = tokens_ref.shape
    owned = model_width // groups
    chunks = owned // LANES
    padded = piece_rows(chunks)
    above = lax.broadcasted_iota(jnp.int32, (token_rows, token_rows), 0)
    along = lax.broadcasted_iota(jnp.int32, (token_rows, token_rows), 1)
    earlier = jnp.where(above < along, 1.0, 0.0).astype(BF16)
    copies[0].wait()
    copies[1].wait()
    ids = ids_ref[...]
    gates = gates_ref[...].astype(F32)
    members, chosen = [], []
    for expert in range(window):
        hit = ids == expert
        members.append(jnp.sum(jnp.where(hit, 1.0, 0.0), axis=0, keepdims=True))
        chosen.append(jnp.sum(jnp.where(hit, gates, 0.0), axis=0, keepdims=True))
    members = jnp.concatenate(members, axis=0)
    chosen = jnp.concatenate(chosen, axis=0)
    code = jnp.where(members > 0.0, dot(members.astype(BF16), earlier), -1e6)
    code_ref[...] = code
    table, gated = table_of(code, [None, chosen], chunks, padded)

    def columns(ref):
        return jnp.concatenate(
            [
                jnp.concatenate(
                    [ref[:, d * owned + c * LANES : d * owned + (c + 1) * LANES] for d in range(groups)],
                    axis=1,
                )
                for c in range(chunks)
            ],
            axis=0,
        )

    copies[2].wait()
    rows = dot(table.astype(BF16), columns(tokens_ref))
    copies[3].wait()
    grads = dot(gated.astype(BF16), columns(grads_ref))
    for d in range(groups):
        lanes = slice(d * LANES, (d + 1) * LANES)
        for expert in range(window):
            lines = slice(expert * padded, (expert + 1) * padded)
            block = jnp.concatenate([rows[lines, lanes], grads[lines, lanes]], axis=0)
            sent_ref[d * window + expert] = block.astype(BF16)


def prep_kernel(*refs):
    weights_ref, far_refs, out_ref = refs[0], refs[1:-1], refs[-1]
    hidden_units = weights_ref.shape[2]
    for b, ref in enumerate((weights_ref,) + tuple(far_refs)):
        out_ref[b, :, :hidden_units] = ref[0]
        out_ref[b, :, hidden_units:] = ref[1]


def table_kernel(chunks, code_ref, table_ref):
    (table,) = table_of(code_ref[...], [None], chunks, piece_rows(chunks))
    table_ref[...] = table.T.astype(BF16)


def partial_kernel(got_ref, weights_in, rows_ref, grads_ref, kept_ref, given_ref, weights_ref, sems):
    @pl.when(pl.program_id(0) == 0)
    def _():
        copies = [
            pltpu.make_async_copy(weights_in.at[0, at], weights_ref.at[at], sems.at[at]) for at in range(3)
        ]
        for copy in copies:
            copy.start()

    sources, height, _ = got_ref.shape
    owned, hidden_units = weights_ref.shape[1:]
    chunks = owned // LANES
    joined = sources // JOIN
    tall = JOIN * SLOTS
    blocks = jnp.concatenate(
        [
            got_ref[q * JOIN : (q + 1) * JOIN].reshape(JOIN * height, LANES)
            for q in range(joined)
        ],
        axis=1,
    )
    lines = dot(sort_matrix(2, chunks, False), blocks)

    def gathered(part):
        return jnp.concatenate(
            [
                jnp.concatenate(
                    [
                        lines[
                            (part * chunks + c) * tall : (part * chunks + c + 1) * tall,
                            q * LANES : (q + 1) * LANES,
                        ]
                        for c in range(chunks)
                    ],
                    axis=1,
                )
                for q in range(joined)
            ],
            axis=0,
        ).astype(BF16)

    rows, grads = gathered(0), gathered(1)
    rows_ref[...] = rows
    grads_ref[...] = grads

    @pl.when(pl.program_id(0) == 0)
    def _():
        for at in range(3):
            pltpu.make_async_copy(weights_in.at[0, at], weights_ref.at[at], sems.at[at]).wait()

    core = lax.axis_index("core")
    per_group = rows.shape[0] // 2 // kept_ref.shape[0]
    for at, source in enumerate([rows, rows, grads]):
        lanes = slice(at * hidden_units, (at + 1) * hidden_units)
        part = dot(source, weights_ref[at])
        for side in range(kept_ref.shape[0]):
            first = part[2 * side * per_group : (2 * side + 1) * per_group]
            second = part[(2 * side + 1) * per_group : (2 * side + 2) * per_group]
            kept_ref[side, :, lanes] = jnp.where(core == 0, first, second)
            given_ref[side, :, lanes] = jnp.where(core == 0, second, first).astype(BF16)


def sum_kernel(kept_ref, arrived_ref, own_ref, leaving_ref):
    sides = kept_ref.shape[0]
    side = lax.axis_index("side")
    for b in range(sides):
        total = kept_ref[side ^ b] + arrived_ref[side ^ b].astype(F32)
        if b == 0:
            own_ref[...] = total
        else:
            leaving_ref[b - 1] = total.astype(BF16)


def acts_kernel(*refs):
    own_ref, out_ref = refs[0], refs[-1]
    total = own_ref[...]
    for ref in refs[1:-1]:
        total = total + ref[...].astype(F32)
    hidden_units = total.shape[1] // 3
    gate_act = total[:, :hidden_units]
    up_act = total[:, hidden_units : 2 * hidden_units]
    grad_hidden = total[:, 2 * hidden_units :]
    logistic = jax.nn.sigmoid(gate_act)
    swish_out = gate_act * logistic
    out_ref[:, 2 * hidden_units :] = (swish_out * up_act).astype(BF16)
    out_ref[:, hidden_units : 2 * hidden_units] = (grad_hidden * swish_out).astype(BF16)
    out_ref[:, :hidden_units] = (
        grad_hidden * up_act * logistic * (1.0 + gate_act * (1.0 - logistic))
    ).astype(BF16)


def back_kernel(*refs):
    own_ref, other_ref, weights_ref, out_ref = refs
    sides, owned, hidden_units = weights_ref.shape
    hidden_units //= 2
    chunks = owned // LANES
    padded = piece_rows(chunks)
    core = lax.axis_index("core")
    own = own_ref[:, : 2 * hidden_units]
    other = other_ref[:, : 2 * hidden_units]
    acts = jnp.concatenate(
        [jnp.where(core == 0, own, other), jnp.where(core == 0, other, own)], axis=0
    )
    tall = JOIN * SLOTS
    joined = acts.shape[0] // tall
    backs = [dot_nt(acts, weights_ref[b]) for b in range(sides)]
    lines = jnp.concatenate(
        [
            jnp.concatenate(
                [
                    backs[b][q * tall : (q + 1) * tall, c * LANES : (c + 1) * LANES]
                    for b in range(sides)
                    for c in range(chunks)
                ],
                axis=0,
            )
            for q in range(joined)
        ],
        axis=1,
    ).astype(BF16)
    blocks = dot(sort_matrix(sides, chunks, True), lines).astype(BF16)
    height = sides * padded
    for q in range(joined):
        for j in range(JOIN):
            out_ref[q * JOIN + j] = blocks[j * height : (j + 1) * height, q * LANES : (q + 1) * LANES]


def combine_kernel(returned_ref, table_ref, out_ref):
    token_rows, model_width = out_ref.shape
    columns, lines = table_ref.shape
    chunks = columns // token_rows
    padded = piece_rows(chunks)
    window = lines // padded
    sides = returned_ref.shape[1] // padded
    owned = chunks * LANES
    side = lax.axis_index("side")
    pieces = []
    for core in range(2):
        part = returned_ref[core * window : (core + 1) * window].astype(F32)
        for b in range(sides):
            piece = part[:, b * padded : (b + 1) * padded].reshape(lines, LANES)
            pieces.append((core, b, piece.astype(BF16)))
    spread = jnp.concatenate([piece for _, _, piece in pieces], axis=1)
    result = dot(table_ref[...], spread).astype(BF16)
    for at, (core, b, _) in enumerate(pieces):
        start = ((side ^ b) * 2 + core) * owned
        for c in range(chunks):
            out_ref[:, pl.ds(pl.multiple_of(start + c * LANES, LANES), LANES)] = result[
                c * token_rows : (c + 1) * token_rows, at * LANES : (at + 1) * LANES
            ]


def grads_kernel(*refs):
    rows_ref, grads_ref = refs[:2]
    acts_refs, out_ref, acts = refs[2:-2], refs[-2], refs[-1]
    hidden_units = out_ref.shape[3]
    per_group = acts_refs[0].shape[0]
    group = lax.axis_index("side") * 2 + lax.axis_index("core")
    for b, ref in enumerate(acts_refs):
        acts[pl.ds(pl.multiple_of((group ^ b) * per_group, 16), per_group), :] = ref[...]
    out_ref[0, 0] = dot_tn(rows_ref[...], acts[:, :hidden_units])
    out_ref[0, 1] = dot_tn(rows_ref[...], acts[:, hidden_units : 2 * hidden_units])
    out_ref[0, 2] = dot_tn(grads_ref[...], acts[:, 2 * hidden_units :])


def on_device(tokens, out_grad, expert_ids, gates, expert_weights):
    window = lax.axis_size("expert")
    sides = lax.axis_size("side")
    groups = sides * 2
    devices = groups * window
    token_rows, model_width = tokens.shape
    hidden_units = expert_weights.shape[3]
    owned = model_width // groups
    chunks = owned // LANES
    padded = piece_rows(chunks)
    rows_here = window * SLOTS
    weights = expert_weights[0]

    far_weights = [swap(expert_weights[0, :2], "side", b) for b in range(1, sides)]

    anywhere = pl.BlockSpec(memory_space=pl.ANY)
    ids_t, gates_t = expert_ids.T, gates.T
    sent, code = pl.pallas_call(
        lambda *refs: pack_kernel(groups, window, *refs),
        in_specs=[anywhere] * 4,
        out_shape=(
            jax.ShapeDtypeStruct((devices, 2 * padded, LANES), BF16),
            jax.ShapeDtypeStruct((window, token_rows), F32),
        ),
        scratch_shapes=[pltpu.VMEM(a.shape, a.dtype) for a in (ids_t, gates_t, tokens, out_grad)]
        + [pltpu.SemaphoreType.DMA((4,))],
        compiler_params=params((tokens, out_grad, tokens)),
    )(ids_t, gates_t, tokens, out_grad)
    got = lax.all_to_all(sent, ("side", "core", "expert"), split_axis=0, concat_axis=0, tiled=True)
    table = pl.pallas_call(
        lambda *refs: table_kernel(chunks, *refs),
        out_shape=jax.ShapeDtypeStruct((chunks * token_rows, window * padded), BF16),
        compiler_params=params(()),
        cost_estimate=cost(0, 4 * 2**20),
    )(code)
    both = pl.pallas_call(
        prep_kernel,
        out_shape=jax.ShapeDtypeStruct((sides, owned, 2 * hidden_units), BF16),
        compiler_params=params((expert_weights,) * 2),
        cost_estimate=cost(10**11, 10**8),
    )(expert_weights[0, :2], *far_weights)
    got, both, table = lax.optimization_barrier((got, both, table))

    wide = 3 * hidden_units
    expert_rows, expert_grads, kept, given = pl.pallas_call(
        partial_kernel,
        grid=(1,),
        in_specs=[pl.BlockSpec(got.shape, lambda i: (0, 0, 0)), anywhere],
        out_specs=[
            pl.BlockSpec((devices * SLOTS, owned), lambda i: (0, 0)),
            pl.BlockSpec((devices * SLOTS, owned), lambda i: (0, 0)),
            pl.BlockSpec((sides, rows_here, wide), lambda i: (0, 0, 0)),
            pl.BlockSpec((sides, rows_here, wide), lambda i: (0, 0, 0)),
        ],
        out_shape=(
            jax.ShapeDtypeStruct((devices * SLOTS, owned), BF16),
            jax.ShapeDtypeStruct((devices * SLOTS, owned), BF16),
            jax.ShapeDtypeStruct((sides, rows_here, wide), F32),
            jax.ShapeDtypeStruct((sides, rows_here, wide), BF16),
        ),
        scratch_shapes=[pltpu.VMEM(weights.shape, BF16), pltpu.SemaphoreType.DMA((3,))],
        compiler_params=params((got, got, expert_weights)),
    )(got, expert_weights)

    arrived = swap(given, "core", 1)
    own, leaving = pl.pallas_call(
        sum_kernel,
        out_shape=(
            jax.ShapeDtypeStruct((rows_here, wide), F32),
            jax.ShapeDtypeStruct((sides - 1, rows_here, wide), BF16),
        ),
        compiler_params=params((kept, given)),
    )(kept, arrived)
    acts = pl.pallas_call(
        acts_kernel,
        out_shape=jax.ShapeDtypeStruct((rows_here, wide), BF16),
        compiler_params=params((own,)),
    )(own, *[swap(leaving[b - 1], "side", b) for b in range(1, sides)])

    other = swap(acts, "core", 1)
    back = pl.pallas_call(
        back_kernel,
        out_shape=jax.ShapeDtypeStruct((2 * window, sides * padded, LANES), BF16),
        compiler_params=params((both, acts, acts)),
    )(acts, other, both)
    returned = lax.all_to_all(back, ("core", "expert"), split_axis=0, concat_axis=0, tiled=True)

    all_acts = [acts, other]
    for b in range(1, sides):
        all_acts.append(swap(acts, "side", b))
        all_acts.append(
            lax.ppermute(acts, ("side", "core"), [(i, i ^ (2 * b + 1)) for i in range(groups)])
        )
    weight_grads = pl.pallas_call(
        grads_kernel,
        out_shape=jax.ShapeDtypeStruct((1, 3, owned, hidden_units), F32),
        scratch_shapes=[pltpu.VMEM((groups * rows_here, wide), BF16)],
        compiler_params=params((expert_rows, expert_grads, expert_weights, expert_weights)),
        cost_estimate=cost(6 * devices * SLOTS * owned * hidden_units, 12 * owned * hidden_units),
    )(expert_rows, expert_grads, *all_acts)

    token_grads = pl.pallas_call(
        combine_kernel,
        out_shape=jax.ShapeDtypeStruct((token_rows, model_width), BF16),
        compiler_params=params((table, back)),
    )(returned, table)
    return (token_grads, weight_grads)


def solution(mesh):
    groups, window = mesh.devices.shape
    split = Mesh(mesh.devices.reshape(groups // 2, 2, window), ("side", "core", "expert"))
    lines = P(("side", "core", "expert"), None)
    slabs = P("expert", None, ("side", "core"), None)
    return jax.shard_map(
        on_device,
        mesh=split,
        in_specs=(lines, lines, lines, lines, slabs),
        out_specs=(lines, slabs),
        check_vma=False,
    )
```

```python
import jax
import jax.numpy as jnp
from jax import lax
from jax.experimental import pallas as pl
from jax.experimental.pallas import tpu as pltpu
from jax.sharding import Mesh, PartitionSpec as P

SLOTS = 10
LANES = 128
JOIN = 4
F32 = jnp.float32
BF16 = jnp.bfloat16


def dot(first_op, second_op):
    return jnp.dot(first_op, second_op, preferred_element_type=F32)


def dot_tn(first_op, second_op):
    return lax.dot_general(first_op, second_op, (((0,), (0,)), ((), ())), preferred_element_type=F32)


def dot_nt(first_op, second_op):
    return lax.dot_general(first_op, second_op, (((1,), (1,)), ((), ())), preferred_element_type=F32)


def swap(value, axis, bit):
    return lax.ppermute(value, axis, [(i, i ^ bit) for i in range(lax.axis_size(axis))])


def piece_rows(chunks):
    return -(-chunks * SLOTS // 8) * 8


def params(arrays, scratch=0):
    moved = sum(a.size * a.dtype.itemsize for a in arrays) + scratch
    return pltpu.CompilerParams(vmem_limit_bytes=min(56 * 2**20, 12 * 2**20 + 3 * moved))


def cost(flops, moved):
    return pl.CostEstimate(flops=flops, bytes_accessed=moved, transcendentals=0)


def lower(value, by):
    return jnp.floor((value + 0.5) * (1.0 / by))


def sort_matrix(parts, chunks, transposed):
    padded = piece_rows(chunks)
    wide, tall = JOIN * parts * padded, parts * chunks * JOIN * SLOTS
    shape, axis = ((wide, tall), 0) if transposed else ((tall, wide), 1)
    line = (wide, 1) if transposed else (1, wide)
    place = lax.broadcasted_iota(jnp.int32, line, axis).astype(F32)
    block = lower(place, padded)
    inside = place - block * padded
    source = lower(block, parts)
    part = block - source * parts
    chunk = lower(inside, SLOTS)
    slot = inside - chunk * SLOTS
    target = ((part * chunks + chunk) * JOIN + source) * SLOTS + slot
    target = jnp.where(chunk < chunks, target, -1.0)
    spots = lax.broadcasted_iota(jnp.int32, shape, 1 - axis).astype(F32)
    return jnp.where(spots == target, 1.0, 0.0).astype(BF16)


def table_of(code, values, chunks, padded):
    window, token_rows = code.shape
    spots = lax.broadcasted_iota(jnp.int32, (padded, chunks * token_rows), 0).astype(F32)
    tables = []
    for expert in range(window):
        own = code[expert : expert + 1]
        wide = jnp.concatenate([own + float(SLOTS * c) for c in range(chunks)], axis=1)
        hit = spots == wide
        row = []
        for value in values:
            if value is None:
                row.append(jnp.where(hit, 1.0, 0.0))
            else:
                gate = jnp.concatenate([value[expert : expert + 1]] * chunks, axis=1)
                row.append(jnp.where(hit, gate, 0.0))
        tables.append(row)
    return [jnp.concatenate([t[i] for t in tables], axis=0) for i in range(len(values))]


def pack_kernel(
    groups, window, ids_in, gates_in, tokens_in, grads_in, weights_in, sent_ref, code_ref, slices_ref, ids_ref, gates_ref, tokens_ref, grads_ref, sems
):
    copies = [
        pltpu.make_async_copy(source, target, sems.at[at])
        for at, (source, target) in enumerate(
            [
                (ids_in, ids_ref),
                (gates_in, gates_ref),
                (tokens_in, tokens_ref),
                (grads_in, grads_ref),
                (weights_in.at[0, pl.ds(0, 2)], slices_ref),
            ]
        )
    ]
    for copy in copies:
        copy.start()
    token_rows, model_width = tokens_ref.shape
    owned = model_width // groups
    chunks = owned // LANES
    padded = piece_rows(chunks)
    above = lax.broadcasted_iota(jnp.int32, (token_rows, token_rows), 0)
    along = lax.broadcasted_iota(jnp.int32, (token_rows, token_rows), 1)
    earlier = jnp.where(above < along, 1.0, 0.0).astype(BF16)
    copies[0].wait()
    copies[1].wait()
    ids = ids_ref[...]
    gates = gates_ref[...].astype(F32)
    members, chosen = [], []
    for expert in range(window):
        hit = ids == expert
        members.append(jnp.sum(jnp.where(hit, 1.0, 0.0), axis=0, keepdims=True))
        chosen.append(jnp.sum(jnp.where(hit, gates, 0.0), axis=0, keepdims=True))
    members = jnp.concatenate(members, axis=0)
    chosen = jnp.concatenate(chosen, axis=0)
    code = jnp.where(members > 0.0, dot(members.astype(BF16), earlier), -1e6)
    code_ref[...] = code
    table, gated = table_of(code, [None, chosen], chunks, padded)

    def columns(ref):
        return jnp.concatenate(
            [
                jnp.concatenate(
                    [ref[:, d * owned + c * LANES : d * owned + (c + 1) * LANES] for d in range(groups)],
                    axis=1,
                )
                for c in range(chunks)
            ],
            axis=0,
        )

    copies[2].wait()
    rows = dot(table.astype(BF16), columns(tokens_ref))
    copies[3].wait()
    grads = dot(gated.astype(BF16), columns(grads_ref))
    for d in range(groups):
        lanes = slice(d * LANES, (d + 1) * LANES)
        for expert in range(window):
            lines = slice(expert * padded, (expert + 1) * padded)
            block = jnp.concatenate([rows[lines, lanes], grads[lines, lanes]], axis=0)
            sent_ref[d * window + expert] = block.astype(BF16)
    copies[4].wait()


def anchor_kernel(*refs):
    pass


def table_kernel(chunks, code_ref, table_ref):
    (table,) = table_of(code_ref[...], [None], chunks, piece_rows(chunks))
    table_ref[...] = table.T.astype(BF16)


def partial_kernel(got_ref, weights_in, rows_ref, grads_ref, kept_ref, given_ref, weights_ref, sems):
    @pl.when(pl.program_id(0) == 0)
    def _():
        copies = [
            pltpu.make_async_copy(weights_in.at[0, at], weights_ref.at[at], sems.at[at]) for at in range(3)
        ]
        for copy in copies:
            copy.start()

    sources, height, _ = got_ref.shape
    owned, hidden_units = weights_ref.shape[1:]
    chunks = owned // LANES
    joined = sources // JOIN
    tall = JOIN * SLOTS
    blocks = jnp.concatenate(
        [
            got_ref[q * JOIN : (q + 1) * JOIN].reshape(JOIN * height, LANES)
            for q in range(joined)
        ],
        axis=1,
    )
    lines = dot(sort_matrix(2, chunks, False), blocks)

    def gathered(part):
        return jnp.concatenate(
            [
                jnp.concatenate(
                    [
                        lines[
                            (part * chunks + c) * tall : (part * chunks + c + 1) * tall,
                            q * LANES : (q + 1) * LANES,
                        ]
                        for c in range(chunks)
                    ],
                    axis=1,
                )
                for q in range(joined)
            ],
            axis=0,
        ).astype(BF16)

    rows, grads = gathered(0), gathered(1)
    rows_ref[...] = rows
    grads_ref[...] = grads

    @pl.when(pl.program_id(0) == 0)
    def _():
        for at in range(3):
            pltpu.make_async_copy(weights_in.at[0, at], weights_ref.at[at], sems.at[at]).wait()

    core = lax.axis_index("core")
    per_group = rows.shape[0] // 2 // kept_ref.shape[0]
    for at, source in enumerate([rows, rows, grads]):
        lanes = slice(at * hidden_units, (at + 1) * hidden_units)
        part = dot(source, weights_ref[at])
        for side in range(kept_ref.shape[0]):
            first = part[2 * side * per_group : (2 * side + 1) * per_group]
            second = part[(2 * side + 1) * per_group : (2 * side + 2) * per_group]
            kept_ref[side, :, lanes] = jnp.where(core == 0, first, second)
            given_ref[side, :, lanes] = jnp.where(core == 0, second, first).astype(BF16)


def sum_kernel(kept_ref, arrived_ref, own_ref, leaving_ref):
    sides = kept_ref.shape[0]
    side = lax.axis_index("side")
    for b in range(sides):
        total = kept_ref[side ^ b] + arrived_ref[side ^ b].astype(F32)
        if b == 0:
            own_ref[...] = total
        else:
            leaving_ref[b - 1] = total.astype(BF16)


def acts_kernel(*refs):
    own_ref, out_ref = refs[0], refs[-1]
    total = own_ref[...]
    for ref in refs[1:-1]:
        total = total + ref[...].astype(F32)
    hidden_units = total.shape[1] // 3
    gate_act = total[:, :hidden_units]
    up_act = total[:, hidden_units : 2 * hidden_units]
    grad_hidden = total[:, 2 * hidden_units :]
    logistic = jax.nn.sigmoid(gate_act)
    swish_out = gate_act * logistic
    out_ref[:, 2 * hidden_units :] = (swish_out * up_act).astype(BF16)
    out_ref[:, hidden_units : 2 * hidden_units] = (grad_hidden * swish_out).astype(BF16)
    out_ref[:, :hidden_units] = (
        grad_hidden * up_act * logistic * (1.0 + gate_act * (1.0 - logistic))
    ).astype(BF16)


def back_kernel(*refs):
    own_ref, other_ref, weights_refs, out_ref = refs[0], refs[1], refs[2:-1], refs[-1]
    sides = len(weights_refs)
    _, owned, hidden_units = weights_refs[0].shape
    chunks = owned // LANES
    padded = piece_rows(chunks)
    core = lax.axis_index("core")
    own = own_ref[:, : 2 * hidden_units]
    other = other_ref[:, : 2 * hidden_units]
    acts = jnp.concatenate(
        [jnp.where(core == 0, own, other), jnp.where(core == 0, other, own)], axis=0
    )
    tall = JOIN * SLOTS
    joined = acts.shape[0] // tall
    backs = [
        dot_nt(acts[:, :hidden_units], ref[0]) + dot_nt(acts[:, hidden_units:], ref[1])
        for ref in weights_refs
    ]
    lines = jnp.concatenate(
        [
            jnp.concatenate(
                [
                    backs[b][q * tall : (q + 1) * tall, c * LANES : (c + 1) * LANES]
                    for b in range(sides)
                    for c in range(chunks)
                ],
                axis=0,
            )
            for q in range(joined)
        ],
        axis=1,
    ).astype(BF16)
    blocks = dot(sort_matrix(sides, chunks, True), lines).astype(BF16)
    height = sides * padded
    for q in range(joined):
        for j in range(JOIN):
            out_ref[q * JOIN + j] = blocks[j * height : (j + 1) * height, q * LANES : (q + 1) * LANES]


def combine_kernel(returned_ref, table_ref, out_ref):
    token_rows, model_width = out_ref.shape
    columns, lines = table_ref.shape
    chunks = columns // token_rows
    padded = piece_rows(chunks)
    window = lines // padded
    sides = returned_ref.shape[1] // padded
    owned = chunks * LANES
    side = lax.axis_index("side")
    pieces = []
    for core in range(2):
        part = returned_ref[core * window : (core + 1) * window].astype(F32)
        for b in range(sides):
            piece = part[:, b * padded : (b + 1) * padded].reshape(lines, LANES)
            pieces.append((core, b, piece.astype(BF16)))
    spread = jnp.concatenate([piece for _, _, piece in pieces], axis=1)
    result = dot(table_ref[...], spread).astype(BF16)
    for at, (core, b, _) in enumerate(pieces):
        start = ((side ^ b) * 2 + core) * owned
        for c in range(chunks):
            out_ref[:, pl.ds(pl.multiple_of(start + c * LANES, LANES), LANES)] = result[
                c * token_rows : (c + 1) * token_rows, at * LANES : (at + 1) * LANES
            ]


def grads_kernel(*refs):
    rows_ref, grads_ref = refs[:2]
    acts_refs, out_ref, acts = refs[2:-2], refs[-2], refs[-1]
    hidden_units = out_ref.shape[3]
    per_group = acts_refs[0].shape[0]
    group = lax.axis_index("side") * 2 + lax.axis_index("core")
    for b, ref in enumerate(acts_refs):
        acts[pl.ds(pl.multiple_of((group ^ b) * per_group, 16), per_group), :] = ref[...]
    lanes = [slice(at * hidden_units, (at + 1) * hidden_units) for at in range(3)]
    sources = [rows_ref, rows_ref, grads_ref]
    total = rows_ref.shape[0]
    block = min(total, 640)
    if block == total:
        for at in range(3):
            out_ref[0, at] = dot_tn(sources[at][...], acts[:, lanes[at]])
    else:
        out_ref[...] = jnp.zeros_like(out_ref)

        @pl.loop(0, total // block)
        def _(step):
            lines = pl.ds(pl.multiple_of(step * block, 16), block)
            for at in range(3):
                out_ref[0, at] += dot_tn(sources[at][lines, :], acts[lines, lanes[at]])


def on_device(tokens, out_grad, expert_ids, gates, expert_weights):
    window = lax.axis_size("expert")
    sides = lax.axis_size("side")
    groups = sides * 2
    devices = groups * window
    token_rows, model_width = tokens.shape
    hidden_units = expert_weights.shape[3]
    owned = model_width // groups
    chunks = owned // LANES
    padded = piece_rows(chunks)
    rows_here = window * SLOTS
    weights = expert_weights[0]

    anywhere = pl.BlockSpec(memory_space=pl.ANY)
    ids_t, gates_t = expert_ids.T, gates.T
    sent, code, slices = pl.pallas_call(
        lambda *refs: pack_kernel(groups, window, *refs),
        in_specs=[anywhere] * 5,
        out_specs=(pl.BlockSpec(), pl.BlockSpec(), anywhere),
        out_shape=(
            jax.ShapeDtypeStruct((devices, 2 * padded, LANES), BF16),
            jax.ShapeDtypeStruct((window, token_rows), F32),
            jax.ShapeDtypeStruct((2, owned, hidden_units), BF16),
        ),
        scratch_shapes=[pltpu.VMEM(a.shape, a.dtype) for a in (ids_t, gates_t, tokens, out_grad)]
        + [pltpu.SemaphoreType.DMA((5,))],
        compiler_params=params((tokens, out_grad, tokens)),
    )(ids_t, gates_t, tokens, out_grad, expert_weights)
    far_weights = [swap(slices, "side", b) for b in range(1, sides)]
    got = lax.all_to_all(sent, ("side", "core", "expert"), split_axis=0, concat_axis=0, tiled=True)
    table = pl.pallas_call(
        lambda *refs: table_kernel(chunks, *refs),
        out_shape=jax.ShapeDtypeStruct((chunks * token_rows, window * padded), BF16),
        compiler_params=params(()),
        cost_estimate=cost(0, 4 * 2**20),
    )(code)
    far_weights = pl.pallas_call(
        anchor_kernel,
        in_specs=[anywhere] * (sides - 1),
        out_specs=[anywhere] * (sides - 1),
        out_shape=[jax.ShapeDtypeStruct(far.shape, BF16) for far in far_weights],
        input_output_aliases={b: b for b in range(sides - 1)},
        cost_estimate=cost(10**11, 10**8),
    )(*far_weights)
    got, far_weights, table = lax.optimization_barrier((got, far_weights, table))

    wide = 3 * hidden_units
    steps = sides if devices * SLOTS > 640 else 1
    expert_rows, expert_grads, kept, given = pl.pallas_call(
        partial_kernel,
        grid=(steps,),
        in_specs=[pl.BlockSpec((devices // steps,) + got.shape[1:], lambda i: (i, 0, 0)), anywhere],
        out_specs=[
            pl.BlockSpec((devices // steps * SLOTS, owned), lambda i: (i, 0)),
            pl.BlockSpec((devices // steps * SLOTS, owned), lambda i: (i, 0)),
            pl.BlockSpec((sides // steps, rows_here, wide), lambda i: (i, 0, 0)),
            pl.BlockSpec((sides // steps, rows_here, wide), lambda i: (i, 0, 0)),
        ],
        out_shape=(
            jax.ShapeDtypeStruct((devices * SLOTS, owned), BF16),
            jax.ShapeDtypeStruct((devices * SLOTS, owned), BF16),
            jax.ShapeDtypeStruct((sides, rows_here, wide), F32),
            jax.ShapeDtypeStruct((sides, rows_here, wide), BF16),
        ),
        scratch_shapes=[pltpu.VMEM(weights.shape, BF16), pltpu.SemaphoreType.DMA((3,))],
        compiler_params=params((got, got, expert_weights)),
    )(got, expert_weights)

    arrived = swap(given, "core", 1)
    own, leaving = pl.pallas_call(
        sum_kernel,
        out_shape=(
            jax.ShapeDtypeStruct((rows_here, wide), F32),
            jax.ShapeDtypeStruct((sides - 1, rows_here, wide), BF16),
        ),
        compiler_params=params((kept, given)),
    )(kept, arrived)
    acts = pl.pallas_call(
        acts_kernel,
        out_shape=jax.ShapeDtypeStruct((rows_here, wide), BF16),
        compiler_params=params((own,)),
    )(own, *[swap(leaving[b - 1], "side", b) for b in range(1, sides)])

    other = swap(acts, "core", 1)
    back = pl.pallas_call(
        back_kernel,
        out_shape=jax.ShapeDtypeStruct((2 * window, sides * padded, LANES), BF16),
        compiler_params=params((weights, weights, acts)),
    )(acts, other, slices, *far_weights)
    returned = lax.all_to_all(back, ("core", "expert"), split_axis=0, concat_axis=0, tiled=True)

    all_acts = [acts, other]
    for b in range(1, sides):
        all_acts.append(swap(acts, "side", b))
        all_acts.append(
            lax.ppermute(acts, ("side", "core"), [(i, i ^ (2 * b + 1)) for i in range(groups)])
        )
    weight_grads = pl.pallas_call(
        grads_kernel,
        out_shape=jax.ShapeDtypeStruct((1, 3, owned, hidden_units), F32),
        scratch_shapes=[pltpu.VMEM((groups * rows_here, wide), BF16)],
        compiler_params=params((expert_rows, expert_grads, expert_weights, expert_weights)),
        cost_estimate=cost(10**11, 10**8),
    )(expert_rows, expert_grads, *all_acts)

    token_grads = pl.pallas_call(
        combine_kernel,
        out_shape=jax.ShapeDtypeStruct((token_rows, model_width), BF16),
        compiler_params=params((table, back)),
    )(returned, table)
    return (token_grads, weight_grads)


def solution(mesh):
    groups, window = mesh.devices.shape
    split = Mesh(mesh.devices.reshape(groups // 2, 2, window), ("side", "core", "expert"))
    lines = P(("side", "core", "expert"), None)
    slabs = P("expert", None, ("side", "core"), None)
    return jax.shard_map(
        on_device,
        mesh=split,
        in_specs=(lines, lines, lines, lines, slabs),
        out_specs=(lines, slabs),
        check_vma=False,
    )
```

```python
import jax
import jax.numpy as jnp
from jax import lax
from jax.experimental import pallas as pl
from jax.experimental.pallas import tpu as pltpu
from jax.sharding import PartitionSpec as P

SLOTS = 10
WIDE = 512
JOIN = 4
F32 = jnp.float32
BF16 = jnp.bfloat16


def dot(first_op, second_op):
    return jnp.dot(first_op, second_op, preferred_element_type=F32)


def dot_tn(first_op, second_op):
    return lax.dot_general(first_op, second_op, (((0,), (0,)), ((), ())), preferred_element_type=F32)


def dot_nt(first_op, second_op):
    return lax.dot_general(first_op, second_op, (((1,), (1,)), ((), ())), preferred_element_type=F32)


def swap(value, bits):
    return lax.ppermute(value, "dp", [(i, i ^ bits) for i in range(lax.axis_size("dp"))])


def piece_rows(chunks):
    return -(-chunks * SLOTS // 8) * 8


def params(*arrays):
    moved = sum(a.size * a.dtype.itemsize for a in arrays)
    return pltpu.CompilerParams(vmem_limit_bytes=min(56 * 2**20, 12 * 2**20 + 3 * moved))


def cost(flops, moved):
    return pl.CostEstimate(flops=flops, bytes_accessed=moved, transcendentals=0)


def shape(*extent, kind=BF16):
    return jax.ShapeDtypeStruct(extent, kind)


def lower(value, by):
    return jnp.floor((value + 0.5) * (1.0 / by))


def sort_matrix(parts, chunks, transposed):
    padded = piece_rows(chunks)
    wide, tall = JOIN * parts * padded, parts * chunks * JOIN * SLOTS
    extent, axis = ((wide, tall), 0) if transposed else ((tall, wide), 1)
    line = (wide, 1) if transposed else (1, wide)
    place = lax.broadcasted_iota(jnp.int32, line, axis).astype(F32)
    block = lower(place, padded)
    inside = place - block * padded
    source = lower(block, parts)
    part = block - source * parts
    chunk = lower(inside, SLOTS)
    slot = inside - chunk * SLOTS
    target = ((part * chunks + chunk) * JOIN + source) * SLOTS + slot
    target = jnp.where(chunk < chunks, target, -1.0)
    spots = lax.broadcasted_iota(jnp.int32, extent, 1 - axis).astype(F32)
    return jnp.where(spots == target, 1.0, 0.0).astype(BF16)


def table_of(code, values, chunks, padded):
    window, token_rows = code.shape
    spots = lax.broadcasted_iota(jnp.int32, (padded, chunks * token_rows), 0).astype(F32)
    tables = []
    for expert in range(window):
        own = code[expert : expert + 1]
        hit = spots == jnp.concatenate([own + float(SLOTS * c) for c in range(chunks)], axis=1)
        row = []
        for value in values:
            if value is None:
                row.append(jnp.where(hit, 1.0, 0.0))
            else:
                gate = jnp.concatenate([value[expert : expert + 1]] * chunks, axis=1)
                row.append(jnp.where(hit, gate, 0.0))
        tables.append(row)
    return [jnp.concatenate([t[i] for t in tables], axis=0) for i in range(len(values))]


def pack_kernel(
    ids_in, gates_in, tokens_in, grads_in, weights_in,
    sent_ref, code_ref, pair_ref, down_ref,
    ids_ref, gates_ref, tokens_ref, grads_ref, sems,
):
    hidden_units = down_ref.shape[1]
    moves = [
        (ids_in, ids_ref),
        (gates_in, gates_ref),
        (tokens_in, tokens_ref),
        (grads_in, grads_ref),
        (weights_in.at[0, 0], pair_ref.at[:, pl.ds(0, hidden_units)]),
        (weights_in.at[0, 1], pair_ref.at[:, pl.ds(hidden_units, hidden_units)]),
        (weights_in.at[0, 2], down_ref),
    ]
    copies = [
        pltpu.make_async_copy(source, target, sems.at[at]) for at, (source, target) in enumerate(moves)
    ]
    for copy in copies:
        copy.start()
    token_rows, model_width = tokens_ref.shape
    window = code_ref.shape[0]
    chunks = model_width // WIDE
    padded = piece_rows(chunks)
    above = lax.broadcasted_iota(jnp.int32, (token_rows, token_rows), 0)
    along = lax.broadcasted_iota(jnp.int32, (token_rows, token_rows), 1)
    earlier = jnp.where(above < along, 1.0, 0.0).astype(BF16)
    copies[0].wait()
    copies[1].wait()
    ids = ids_ref[...]
    gates = gates_ref[...].astype(F32)
    members, chosen = [], []
    for expert in range(window):
        hit = ids == expert
        members.append(jnp.sum(jnp.where(hit, 1.0, 0.0), axis=0, keepdims=True))
        chosen.append(jnp.sum(jnp.where(hit, gates, 0.0), axis=0, keepdims=True))
    members = jnp.concatenate(members, axis=0)
    chosen = jnp.concatenate(chosen, axis=0)
    code = jnp.where(members > 0.0, dot(members.astype(BF16), earlier), -1e6)
    code_ref[...] = code
    table, gated = table_of(code, [None, chosen], chunks, padded)

    def columns(ref):
        return jnp.concatenate([ref[:, c * WIDE : (c + 1) * WIDE] for c in range(chunks)], axis=0)

    copies[2].wait()
    rows = dot(table.astype(BF16), columns(tokens_ref))
    copies[3].wait()
    grads = dot(gated.astype(BF16), columns(grads_ref))
    for expert in range(window):
        lines = slice(expert * padded, (expert + 1) * padded)
        sent_ref[expert] = jnp.concatenate([rows[lines], grads[lines]], axis=0).astype(BF16)
    for copy in copies[4:]:
        copy.wait()


def table_kernel(chunks, code_ref, table_ref):
    (table,) = table_of(code_ref[...], [None], chunks, piece_rows(chunks))
    table_ref[...] = table.T.astype(BF16)


def anchor_kernel(*refs):
    pass


def partial_kernel(groups, got_ref, *refs):
    pairs = [b for b in range(groups) if b % 2 == 0 or b == 1]
    count = len(pairs) + groups
    weights_in, refs = refs[:count], refs[count:]
    rows_ref, grads_ref, out_ref = refs[:3]
    slices_refs, refs = refs[3 : 3 + groups], refs[3 + groups :]
    pair_ref, down_ref, sems = refs
    copies = []
    for at, source in enumerate(weights_in):
        target = pair_ref.at[at] if at < len(pairs) else down_ref.at[at - len(pairs)]
        copies.append(pltpu.make_async_copy(source, target, sems.at[at]))
    for copy in copies:
        copy.start()
    sources, height, _ = got_ref.shape
    model_width = rows_ref.shape[1]
    chunks = model_width // WIDE
    owned = model_width // groups
    joined = sources // JOIN
    tall = JOIN * SLOTS
    blocks = jnp.concatenate(
        [got_ref[q * JOIN : (q + 1) * JOIN].reshape(JOIN * height, WIDE) for q in range(joined)],
        axis=1,
    )
    lines = dot(sort_matrix(2, chunks, False), blocks)

    def gathered(part):
        return jnp.concatenate(
            [
                jnp.concatenate(
                    [
                        lines[
                            (part * chunks + c) * tall : (part * chunks + c + 1) * tall,
                            q * WIDE : (q + 1) * WIDE,
                        ]
                        for c in range(chunks)
                    ],
                    axis=1,
                )
                for q in range(joined)
            ],
            axis=0,
        ).astype(BF16)

    rows_ref[...] = gathered(0)
    grads_ref[...] = gathered(1)
    me = lax.axis_index("dp")
    for copy in copies:
        copy.wait()
    wide = pair_ref.shape[2]
    pair_sum, down_sum = None, None
    for b in range(groups):
        lanes = pl.ds(pl.multiple_of((me ^ b) * owned, 128), owned)
        rows, grads = rows_ref[:, lanes], grads_ref[:, lanes]
        slices_refs[b][0] = rows
        slices_refs[b][1] = grads
        term = dot(grads, down_ref[b])
        down_sum = term if down_sum is None else down_sum + term
        if b in pairs:
            term = dot(rows, pair_ref[pairs.index(b)])
            pair_sum = term if pair_sum is None else pair_sum + term
    out_ref[:, :wide] = pair_sum
    out_ref[:, wide:] = down_sum


def back_kernel(groups, rows_ref, partial_ref, *refs):
    weights_in, (acts_ref, out_ref, back_ref, pair_ref, sems) = refs[:groups], refs[groups:]
    copies = [
        pltpu.make_async_copy(source, pair_ref.at[b], sems.at[b]) for b, source in enumerate(weights_in)
    ]
    late = [b for b in range(groups) if b % 2 == 1 and b != 1]
    order = late + [b for b in range(groups) if b not in late]
    for b in order:
        copies[b].start()
    me = lax.axis_index("dp")
    model_width = rows_ref.shape[1]
    owned = model_width // groups
    chunks = model_width // WIDE
    hidden_units = partial_ref.shape[1] // 3
    wide = 2 * hidden_units

    def lanes(b):
        return pl.ds(pl.multiple_of((me ^ b) * owned, 128), owned)

    both = partial_ref[:, :wide]
    for b in late:
        copies[b].wait()
        both = both + dot(rows_ref[:, lanes(b)], pair_ref[b])
    gate_act, up_act = both[:, :hidden_units], both[:, hidden_units:]
    grad_hidden = partial_ref[:, wide:]
    logistic = jax.nn.sigmoid(gate_act)
    swish_out = gate_act * logistic
    hidden = (swish_out * up_act).astype(BF16)
    grad_up = (grad_hidden * swish_out).astype(BF16)
    grad_gate = (grad_hidden * up_act * logistic * (1.0 + gate_act * (1.0 - logistic))).astype(BF16)
    acts = jnp.concatenate([grad_gate, grad_up], axis=1)
    acts_ref[:, :wide] = acts
    acts_ref[:, wide:] = hidden
    for b in order:
        if b not in late:
            copies[b].wait()
        back_ref[:, lanes(b)] = dot_nt(acts, pair_ref[b])
    tall = JOIN * SLOTS
    joined = rows_ref.shape[0] // tall
    lines = jnp.concatenate(
        [
            jnp.concatenate(
                [
                    back_ref[q * tall : (q + 1) * tall, c * WIDE : (c + 1) * WIDE]
                    for c in range(chunks)
                ],
                axis=0,
            )
            for q in range(joined)
        ],
        axis=1,
    ).astype(BF16)
    blocks = dot(sort_matrix(1, chunks, True), lines)
    height = piece_rows(chunks)
    for q in range(joined):
        for j in range(JOIN):
            part = blocks[j * height : (j + 1) * height, q * WIDE : (q + 1) * WIDE]
            out_ref[q * JOIN + j] = part.astype(BF16)


def combine_kernel(returned_ref, table_ref, out_ref):
    token_rows, model_width = out_ref.shape
    window, height, _ = returned_ref.shape
    lines = returned_ref[...].astype(F32).reshape(window * height, WIDE).astype(BF16)
    result = dot(table_ref[...], lines).astype(BF16)
    for c in range(model_width // WIDE):
        out_ref[:, c * WIDE : (c + 1) * WIDE] = result[c * token_rows : (c + 1) * token_rows]


def grads_kernel(groups, *refs):
    slices_refs, acts_refs, out_ref = refs[:groups], refs[groups : 2 * groups], refs[-1]
    hidden_units = out_ref.shape[3]
    rows_here = acts_refs[0].shape[0]
    step = max(1, min(groups, 640 // rows_here))
    for at in range(3):
        lanes = slice(at * hidden_units, (at + 1) * hidden_units)
        kind = 0 if at < 2 else 1
        total = None
        for first in range(0, groups, step):
            some = range(first, first + step)
            rows = jnp.concatenate([slices_refs[b][kind] for b in some], axis=0)
            acts = jnp.concatenate([acts_refs[b][:, lanes] for b in some], axis=0)
            term = dot_tn(rows, acts)
            total = term if total is None else total + term
        out_ref[0, at] = total


def on_device(tokens, out_grad, expert_ids, gates, expert_weights):
    window = lax.axis_size("expert")
    groups = lax.axis_size("dp")
    token_rows, model_width = tokens.shape
    hidden_units = expert_weights.shape[3]
    owned = model_width // groups
    chunks = model_width // WIDE
    padded = piece_rows(chunks)
    rows_here = window * SLOTS
    wide = 2 * hidden_units
    anywhere = pl.BlockSpec(memory_space=pl.ANY)
    in_hbm = pl.BlockSpec(memory_space=pltpu.HBM)

    ids_t, gates_t = expert_ids.T, gates.T
    sent, code, pair, down = pl.pallas_call(
        pack_kernel,
        in_specs=[in_hbm] * 5,
        out_specs=(pl.BlockSpec(), pl.BlockSpec(), in_hbm, in_hbm),
        out_shape=(
            shape(window, 2 * padded, WIDE),
            shape(window, token_rows, kind=F32),
            shape(owned, wide),
            shape(owned, hidden_units),
        ),
        scratch_shapes=[pltpu.VMEM(a.shape, a.dtype) for a in (ids_t, gates_t, tokens, out_grad)]
        + [pltpu.SemaphoreType.DMA((7,))],
        compiler_params=params(tokens, out_grad, tokens),
    )(ids_t, gates_t, tokens, out_grad, expert_weights)

    far = list(range(2, groups, 2))
    pairs = {b: swap(pair, b) for b in far}
    downs = {b: swap(down, b) for b in far}
    pairs[1], downs[1] = swap(pair, 1), swap(down, 1)
    got = lax.all_to_all(sent, "expert", split_axis=0, concat_axis=0, tiled=True)
    table = pl.pallas_call(
        lambda *refs: table_kernel(chunks, *refs),
        out_shape=shape(chunks * token_rows, window * padded),
        compiler_params=params(),
        cost_estimate=cost(0, 4 * 2**20),
    )(code)

    def arrived(values):
        return pl.pallas_call(
            anchor_kernel,
            in_specs=[anywhere] * len(values),
            out_specs=[anywhere] * len(values),
            out_shape=[shape(*value.shape) for value in values],
            input_output_aliases={at: at for at in range(len(values))},
            cost_estimate=cost(10**11, 10**8),
        )(*values)

    downs.update(zip(far, arrived([downs[b] for b in far])))
    pairs.update(zip(far, arrived([pairs[b] for b in far])))
    downs[0], pairs[0] = down, pair
    for b in far:
        downs[b + 1] = swap(downs[b], 1)
        pairs[b + 1] = swap(pairs[b], 1)

    early = [pairs[b] for b in range(groups) if b % 2 == 0 or b == 1]
    early += [downs[b] for b in range(groups)]
    outs = pl.pallas_call(
        lambda *refs: partial_kernel(groups, *refs),
        in_specs=[pl.BlockSpec()] + [anywhere] * len(early),
        out_shape=[shape(rows_here, model_width)] * 2
        + [shape(rows_here, 3 * hidden_units, kind=F32)]
        + [shape(2, rows_here, owned)] * groups,
        scratch_shapes=[
            pltpu.VMEM((len(early) - groups, owned, wide), BF16),
            pltpu.VMEM((groups, owned, hidden_units), BF16),
            pltpu.SemaphoreType.DMA((len(early),)),
        ],
        compiler_params=params(got, *early),
    )(got, *early)
    rows, _, partial = outs[:3]
    slices = list(outs[3:])

    acts, back = pl.pallas_call(
        lambda *refs: back_kernel(groups, *refs),
        in_specs=[pl.BlockSpec()] * 2 + [anywhere] * groups,
        out_shape=(shape(rows_here, 3 * hidden_units), shape(window, padded, WIDE)),
        scratch_shapes=[
            pltpu.VMEM((rows_here, model_width), F32),
            pltpu.VMEM((groups, owned, wide), BF16),
            pltpu.SemaphoreType.DMA((groups,)),
        ],
        compiler_params=params(rows, rows, *[pair] * groups),
    )(rows, partial, *[pairs[b] for b in range(groups)])
    returned = lax.all_to_all(back, "expert", split_axis=0, concat_axis=0, tiled=True)

    every = [slices[0]] + [swap(slices[b], b) for b in range(1, groups)]
    every += [acts] + [swap(acts, b) for b in range(1, groups)]
    weight_grads = pl.pallas_call(
        lambda *refs: grads_kernel(groups, *refs),
        out_shape=shape(1, 3, owned, hidden_units, kind=F32),
        compiler_params=params(*every, expert_weights, expert_weights),
        cost_estimate=cost(6 * groups * rows_here * owned * hidden_units, 12 * owned * hidden_units),
    )(*every)

    token_grads = pl.pallas_call(
        combine_kernel,
        out_shape=shape(token_rows, model_width),
        compiler_params=params(table, back, tokens),
    )(returned, table)
    return (token_grads, weight_grads)


def solution(mesh):
    lines = P(("dp", "expert"), None)
    slabs = P("expert", None, "dp", None)
    return jax.shard_map(
        on_device,
        mesh=mesh,
        in_specs=(lines, lines, lines, lines, slabs),
        out_specs=(lines, slabs),
        check_vma=False,
    )
```

```python
import jax
import jax.numpy as jnp
from jax import lax
from jax.experimental import pallas as pl
from jax.experimental.pallas import tpu as pltpu
from jax.sharding import PartitionSpec as P

SLOTS = 10
WIDE = 512
JOIN = 4
F32 = jnp.float32
BF16 = jnp.bfloat16


def dot(first_op, second_op):
    return jnp.dot(first_op, second_op, preferred_element_type=F32)


def dot_tn(first_op, second_op):
    return lax.dot_general(first_op, second_op, (((0,), (0,)), ((), ())), preferred_element_type=F32)


def dot_nt(first_op, second_op):
    return lax.dot_general(first_op, second_op, (((1,), (1,)), ((), ())), preferred_element_type=F32)


def swap(value, bits):
    return lax.ppermute(value, "dp", [(i, i ^ bits) for i in range(lax.axis_size("dp"))])


def piece_rows(chunks):
    return -(-chunks * SLOTS // 8) * 8


def params(*arrays):
    moved = sum(a.size * a.dtype.itemsize for a in arrays)
    return pltpu.CompilerParams(vmem_limit_bytes=min(56 * 2**20, 12 * 2**20 + 3 * moved))


def cost(flops, moved):
    return pl.CostEstimate(flops=flops, bytes_accessed=moved, transcendentals=0)


def shape(*extent, kind=BF16):
    return jax.ShapeDtypeStruct(extent, kind)


def lower(value, by):
    return jnp.floor((value + 0.5) * (1.0 / by))


def sort_matrix(parts, chunks, transposed):
    padded = piece_rows(chunks)
    wide, tall = JOIN * parts * padded, parts * chunks * JOIN * SLOTS
    extent, axis = ((wide, tall), 0) if transposed else ((tall, wide), 1)
    line = (wide, 1) if transposed else (1, wide)
    place = lax.broadcasted_iota(jnp.int32, line, axis).astype(F32)
    block = lower(place, padded)
    inside = place - block * padded
    source = lower(block, parts)
    part = block - source * parts
    chunk = lower(inside, SLOTS)
    slot = inside - chunk * SLOTS
    target = ((part * chunks + chunk) * JOIN + source) * SLOTS + slot
    target = jnp.where(chunk < chunks, target, -1.0)
    spots = lax.broadcasted_iota(jnp.int32, extent, 1 - axis).astype(F32)
    return jnp.where(spots == target, 1.0, 0.0).astype(BF16)


def table_of(code, values, chunks, padded):
    window, token_rows = code.shape
    spots = lax.broadcasted_iota(jnp.int32, (padded, chunks * token_rows), 0).astype(F32)
    tables = []
    for expert in range(window):
        own = code[expert : expert + 1]
        hit = spots == jnp.concatenate([own + float(SLOTS * c) for c in range(chunks)], axis=1)
        row = []
        for value in values:
            if value is None:
                row.append(jnp.where(hit, 1.0, 0.0))
            else:
                gate = jnp.concatenate([value[expert : expert + 1]] * chunks, axis=1)
                row.append(jnp.where(hit, gate, 0.0))
        tables.append(row)
    return [jnp.concatenate([t[i] for t in tables], axis=0) for i in range(len(values))]


def pack_kernel(
    ids_in, gates_in, tokens_in, grads_in, weights_in,
    sent_ref, code_ref, pair_ref, down_ref,
    ids_ref, gates_ref, tokens_ref, grads_ref, sems,
):
    hidden_units = down_ref.shape[1]
    moves = [
        (ids_in, ids_ref),
        (gates_in, gates_ref),
        (tokens_in, tokens_ref),
        (grads_in, grads_ref),
        (weights_in.at[0, 0], pair_ref.at[:, pl.ds(0, hidden_units)]),
        (weights_in.at[0, 1], pair_ref.at[:, pl.ds(hidden_units, hidden_units)]),
        (weights_in.at[0, 2], down_ref),
    ]
    copies = [
        pltpu.make_async_copy(source, target, sems.at[at]) for at, (source, target) in enumerate(moves)
    ]
    for copy in copies:
        copy.start()
    token_rows, model_width = tokens_ref.shape
    window = code_ref.shape[0]
    chunks = model_width // WIDE
    padded = piece_rows(chunks)
    above = lax.broadcasted_iota(jnp.int32, (token_rows, token_rows), 0)
    along = lax.broadcasted_iota(jnp.int32, (token_rows, token_rows), 1)
    earlier = jnp.where(above < along, 1.0, 0.0).astype(BF16)
    copies[0].wait()
    copies[1].wait()
    ids = ids_ref[...]
    gates = gates_ref[...].astype(F32)
    members, chosen = [], []
    for expert in range(window):
        hit = ids == expert
        members.append(jnp.sum(jnp.where(hit, 1.0, 0.0), axis=0, keepdims=True))
        chosen.append(jnp.sum(jnp.where(hit, gates, 0.0), axis=0, keepdims=True))
    members = jnp.concatenate(members, axis=0)
    chosen = jnp.concatenate(chosen, axis=0)
    code = jnp.where(members > 0.0, dot(members.astype(BF16), earlier), -1e6)
    code_ref[...] = code
    table, gated = table_of(code, [None, chosen], chunks, padded)

    def columns(ref):
        return jnp.concatenate([ref[:, c * WIDE : (c + 1) * WIDE] for c in range(chunks)], axis=0)

    copies[2].wait()
    rows = dot(table.astype(BF16), columns(tokens_ref))
    copies[3].wait()
    grads = dot(gated.astype(BF16), columns(grads_ref))
    for expert in range(window):
        lines = slice(expert * padded, (expert + 1) * padded)
        sent_ref[expert] = jnp.concatenate([rows[lines], grads[lines]], axis=0).astype(BF16)
    for copy in copies[4:]:
        copy.wait()


def table_kernel(chunks, code_ref, table_ref):
    (table,) = table_of(code_ref[...], [None], chunks, piece_rows(chunks))
    table_ref[...] = table.T.astype(BF16)


def anchor_kernel(*refs):
    refs[-1][...] = jnp.zeros_like(refs[-1])


def keep_kernel(*refs):
    pass


def partial_kernel(groups, got_ref, *refs):
    count = groups + 2
    weights_in, refs = refs[:count], refs[count + 1 :]
    out_ref, grads_ref, token_ref, refs = refs[0], refs[1], refs[2], refs[3:]
    slices_refs, (rows_ref, pair_ref, down_ref, sems) = refs[:groups], refs[groups:]
    copies = []
    for at, source in enumerate(weights_in):
        target = pair_ref.at[at] if at < groups else down_ref.at[at - groups]
        copies.append(pltpu.make_async_copy(source, target, sems.at[at]))
    for copy in copies:
        copy.start()
    token_ref[...] = jnp.zeros_like(token_ref)
    sources, height, _ = got_ref.shape
    model_width = rows_ref.shape[1]
    chunks = model_width // WIDE
    owned = model_width // groups
    joined = sources // JOIN
    tall = JOIN * SLOTS
    blocks = jnp.concatenate(
        [got_ref[q * JOIN : (q + 1) * JOIN].reshape(JOIN * height, WIDE) for q in range(joined)],
        axis=1,
    )
    lines = dot(sort_matrix(2, chunks, False), blocks)

    def gathered(part):
        return jnp.concatenate(
            [
                jnp.concatenate(
                    [
                        lines[
                            (part * chunks + c) * tall : (part * chunks + c + 1) * tall,
                            q * WIDE : (q + 1) * WIDE,
                        ]
                        for c in range(chunks)
                    ],
                    axis=1,
                )
                for q in range(joined)
            ],
            axis=0,
        ).astype(BF16)

    rows_ref[...] = gathered(0)
    grads_ref[...] = gathered(1)
    me = lax.axis_index("dp")
    wide = pair_ref.shape[2]
    for copy in copies:
        copy.wait()
    pair_sum, down_sum = None, None
    for b in range(groups):
        lanes = pl.ds(pl.multiple_of((me ^ b) * owned, 128), owned)
        rows, grads = rows_ref[:, lanes], grads_ref[:, lanes]
        slices_refs[b][0] = rows
        slices_refs[b][1] = grads
        term = dot(rows, pair_ref[b])
        pair_sum = term if pair_sum is None else pair_sum + term
        if b < 2:
            term = dot(grads, down_ref[b])
            down_sum = term if down_sum is None else down_sum + term
    out_ref[:, :wide] = pair_sum
    out_ref[:, wide:] = down_sum


def back_kernel(groups, grads_ref, partial_ref, *refs):
    pair_refs, down_refs = refs[:groups], refs[groups : 2 * groups - 2]
    acts_ref, out_ref, back_ref = refs[2 * groups - 2 :]
    me = lax.axis_index("dp")
    model_width = grads_ref.shape[1]
    owned = model_width // groups
    chunks = model_width // WIDE
    hidden_units = partial_ref.shape[1] // 3
    wide = 2 * hidden_units

    def lanes(b):
        return pl.ds(pl.multiple_of((me ^ b) * owned, 128), owned)

    gate_act = partial_ref[:, :hidden_units]
    up_act = partial_ref[:, hidden_units:wide]
    grad_hidden = partial_ref[:, wide:]
    for b in range(2, groups):
        grad_hidden = grad_hidden + dot(grads_ref[:, lanes(b)], down_refs[b - 2][...])
    logistic = jax.nn.sigmoid(gate_act)
    swish_out = gate_act * logistic
    hidden = (swish_out * up_act).astype(BF16)
    grad_up = (grad_hidden * swish_out).astype(BF16)
    grad_gate = (grad_hidden * up_act * logistic * (1.0 + gate_act * (1.0 - logistic))).astype(BF16)
    acts = jnp.concatenate([grad_gate, grad_up], axis=1)
    acts_ref[:, :wide] = acts
    acts_ref[:, wide:] = hidden
    for b in range(groups):
        back_ref[:, lanes(b)] = dot_nt(acts, pair_refs[b][...])
    tall = JOIN * SLOTS
    joined = grads_ref.shape[0] // tall
    lines = jnp.concatenate(
        [
            jnp.concatenate(
                [
                    back_ref[q * tall : (q + 1) * tall, c * WIDE : (c + 1) * WIDE]
                    for c in range(chunks)
                ],
                axis=0,
            )
            for q in range(joined)
        ],
        axis=1,
    ).astype(BF16)
    blocks = dot(sort_matrix(1, chunks, True), lines)
    height = piece_rows(chunks)
    for q in range(joined):
        for j in range(JOIN):
            part = blocks[j * height : (j + 1) * height, q * WIDE : (q + 1) * WIDE]
            out_ref[q * JOIN + j] = part.astype(BF16)


def combine_kernel(returned_ref, table_ref, out_ref):
    token_rows, model_width = out_ref.shape
    window, height, _ = returned_ref.shape
    lines = returned_ref[...].astype(F32).reshape(window * height, WIDE).astype(BF16)
    result = dot(table_ref[...], lines).astype(BF16)
    for c in range(model_width // WIDE):
        out_ref[:, c * WIDE : (c + 1) * WIDE] = result[c * token_rows : (c + 1) * token_rows]


def grads_kernel(groups, *refs):
    slices_refs, acts_refs, out_ref = refs[:groups], refs[groups : 2 * groups], refs[-1]
    hidden_units = out_ref.shape[3]
    rows_here = acts_refs[0].shape[0]
    step = max(1, min(groups, 640 // rows_here))
    for at in range(3):
        lanes = slice(at * hidden_units, (at + 1) * hidden_units)
        kind = 0 if at < 2 else 1
        total = None
        for first in range(0, groups, step):
            some = range(first, first + step)
            rows = jnp.concatenate([slices_refs[b][kind] for b in some], axis=0)
            acts = jnp.concatenate([acts_refs[b][:, lanes] for b in some], axis=0)
            term = dot_tn(rows, acts)
            total = term if total is None else total + term
        out_ref[0, at] = total


def on_device(tokens, out_grad, expert_ids, gates, expert_weights):
    window = lax.axis_size("expert")
    groups = lax.axis_size("dp")
    token_rows, model_width = tokens.shape
    hidden_units = expert_weights.shape[3]
    owned = model_width // groups
    chunks = model_width // WIDE
    padded = piece_rows(chunks)
    rows_here = window * SLOTS
    wide = 2 * hidden_units
    anywhere = pl.BlockSpec(memory_space=pl.ANY)

    ids_t, gates_t = expert_ids.T, gates.T
    sent, code, pair, down = pl.pallas_call(
        pack_kernel,
        in_specs=[anywhere] * 5,
        out_specs=(pl.BlockSpec(), pl.BlockSpec(), anywhere, anywhere),
        out_shape=(
            shape(window, 2 * padded, WIDE),
            shape(window, token_rows, kind=F32),
            shape(owned, wide),
            shape(owned, hidden_units),
        ),
        scratch_shapes=[pltpu.VMEM(a.shape, a.dtype) for a in (ids_t, gates_t, tokens, out_grad)]
        + [pltpu.SemaphoreType.DMA((7,))],
    )(ids_t, gates_t, tokens, out_grad, expert_weights)

    far = list(range(2, groups, 2))
    pairs = {b: swap(pair, b) for b in far}
    downs = {b: swap(down, b) for b in far}
    pairs[1], downs[1] = swap(pair, 1), swap(down, 1)
    got = lax.all_to_all(sent, "expert", split_axis=0, concat_axis=0, tiled=True)
    table = pl.pallas_call(
        lambda *refs: table_kernel(chunks, *refs),
        out_shape=shape(chunks * token_rows, window * padded),
        compiler_params=params(),
        cost_estimate=cost(0, 4 * 2**20),
    )(code)

    def arrived(values):
        return pl.pallas_call(
            anchor_kernel,
            in_specs=[anywhere] * len(values),
            out_shape=shape(8, 128, kind=F32),
            cost_estimate=cost(10**11, 10**8),
        )(*values)

    here = arrived([pairs[b] for b in far])
    pairs[0] = pair
    for b in far:
        pairs[b + 1] = swap(pairs[b], 1)
    pairs = [pairs[b] for b in range(groups)]
    early = pairs + [down, downs[1]]
    outs = pl.pallas_call(
        lambda *refs: partial_kernel(groups, *refs),
        in_specs=[pl.BlockSpec()] + [anywhere] * len(early) + [pl.BlockSpec()],
        out_shape=[
            shape(rows_here, 3 * hidden_units, kind=F32),
            shape(rows_here, model_width),
            shape(8, 128, kind=F32),
        ]
        + [shape(2, rows_here, owned)] * groups,
        scratch_shapes=[
            pltpu.VMEM((rows_here, model_width), BF16),
            pltpu.VMEM((groups, owned, wide), BF16),
            pltpu.VMEM((2, owned, hidden_units), BF16),
            pltpu.SemaphoreType.DMA((len(early),)),
        ],
    )(got, *early, here)
    partial, grads, token = outs[:3]
    slices = list(outs[3:])
    slices = slices[:1] + [swap(slices[b], b) for b in range(1, groups)]

    later = pl.pallas_call(
        keep_kernel,
        in_specs=[anywhere] * (len(far) + 1),
        out_specs=[anywhere] * len(far),
        out_shape=[shape(owned, hidden_units)] * len(far),
        input_output_aliases={at + 1: at for at in range(len(far))},
        cost_estimate=cost(10**11, 10**8),
    )(token, *[downs[b] for b in far])
    downs = [value for down in later for value in (down, swap(down, 1))]

    acts, back = pl.pallas_call(
        lambda *refs: back_kernel(groups, *refs),
        out_shape=(shape(rows_here, 3 * hidden_units), shape(window, padded, WIDE)),
        scratch_shapes=[pltpu.VMEM((rows_here, model_width), F32)],
        compiler_params=params(grads, partial, *pairs, *downs),
        cost_estimate=cost(10**6, 10**5),
    )(grads, partial, *pairs, *downs)
    returned = lax.all_to_all(back, "expert", split_axis=0, concat_axis=0, tiled=True)

    every = slices + [acts] + [swap(acts, b) for b in range(1, groups)]
    weight_grads = pl.pallas_call(
        lambda *refs: grads_kernel(groups, *refs),
        out_shape=shape(1, 3, owned, hidden_units, kind=F32),
        compiler_params=params(*every, expert_weights, expert_weights),
        cost_estimate=cost(6 * groups * rows_here * owned * hidden_units, 12 * owned * hidden_units),
    )(*every)

    token_grads = pl.pallas_call(
        combine_kernel,
        out_shape=shape(token_rows, model_width),
        compiler_params=params(table, back, tokens),
    )(returned, table)
    return (token_grads, weight_grads)


def solution(mesh):
    lines = P(("dp", "expert"), None)
    slabs = P("expert", None, "dp", None)
    return jax.shard_map(
        on_device,
        mesh=mesh,
        in_specs=(lines, lines, lines, lines, slabs),
        out_specs=(lines, slabs),
        check_vma=False,
    )
```

```python
import jax
import jax.numpy as jnp
from jax import lax
from jax.experimental import pallas as pl
from jax.experimental.pallas import tpu as pltpu
from jax.sharding import PartitionSpec as P

SLOTS = 10
WIDE = 512
JOIN = 4
F32 = jnp.float32
BF16 = jnp.bfloat16


def dot(first_op, second_op):
    return jnp.dot(first_op, second_op, preferred_element_type=F32)


def dot_tn(first_op, second_op):
    return lax.dot_general(first_op, second_op, (((0,), (0,)), ((), ())), preferred_element_type=F32)


def dot_nt(first_op, second_op):
    return lax.dot_general(first_op, second_op, (((1,), (1,)), ((), ())), preferred_element_type=F32)


def swap(value, bits):
    return lax.ppermute(value, "dp", [(i, i ^ bits) for i in range(lax.axis_size("dp"))])


def piece_rows(chunks):
    return -(-chunks * SLOTS // 8) * 8


def params(*arrays):
    moved = sum(a.size * a.dtype.itemsize for a in arrays)
    return pltpu.CompilerParams(vmem_limit_bytes=min(56 * 2**20, 12 * 2**20 + 3 * moved))


def cost(flops, moved):
    return pl.CostEstimate(flops=flops, bytes_accessed=moved, transcendentals=0)


def shape(*extent, kind=BF16):
    return jax.ShapeDtypeStruct(extent, kind)


def lower(value, by):
    return jnp.floor((value + 0.5) * (1.0 / by))


def sort_matrix(parts, chunks, transposed):
    padded = piece_rows(chunks)
    wide, tall = JOIN * parts * padded, parts * chunks * JOIN * SLOTS
    extent, axis = ((wide, tall), 0) if transposed else ((tall, wide), 1)
    line = (wide, 1) if transposed else (1, wide)
    place = lax.broadcasted_iota(jnp.int32, line, axis).astype(F32)
    block = lower(place, padded)
    inside = place - block * padded
    source = lower(block, parts)
    part = block - source * parts
    chunk = lower(inside, SLOTS)
    slot = inside - chunk * SLOTS
    target = ((part * chunks + chunk) * JOIN + source) * SLOTS + slot
    target = jnp.where(chunk < chunks, target, -1.0)
    spots = lax.broadcasted_iota(jnp.int32, extent, 1 - axis).astype(F32)
    return jnp.where(spots == target, 1.0, 0.0).astype(BF16)


def table_of(code, values, chunks, padded):
    window, token_rows = code.shape
    spots = lax.broadcasted_iota(jnp.int32, (padded, chunks * token_rows), 0).astype(F32)
    tables = []
    for expert in range(window):
        own = code[expert : expert + 1]
        hit = spots == jnp.concatenate([own + float(SLOTS * c) for c in range(chunks)], axis=1)
        row = []
        for value in values:
            if value is None:
                row.append(jnp.where(hit, 1.0, 0.0))
            else:
                gate = jnp.concatenate([value[expert : expert + 1]] * chunks, axis=1)
                row.append(jnp.where(hit, gate, 0.0))
        tables.append(row)
    return [jnp.concatenate([t[i] for t in tables], axis=0) for i in range(len(values))]


def pack_kernel(
    ids_in, gates_in, tokens_in, grads_in, weights_in,
    sent_ref, code_ref, pair_out, down_out,
    ids_ref, gates_ref, tokens_ref, grads_ref, pair_ref, down_ref, sems,
):
    hidden_units = down_ref.shape[1]
    moves = [
        (ids_in, ids_ref),
        (gates_in, gates_ref),
        (tokens_in, tokens_ref),
        (grads_in, grads_ref),
        (weights_in.at[0, 0], pair_ref.at[:, pl.ds(0, hidden_units)]),
        (weights_in.at[0, 1], pair_ref.at[:, pl.ds(hidden_units, hidden_units)]),
        (weights_in.at[0, 2], down_ref),
    ]
    moves += [(pair_ref, pair_out), (down_ref, down_out)]
    copies = [
        pltpu.make_async_copy(source, target, sems.at[at]) for at, (source, target) in enumerate(moves)
    ]
    for copy in copies[:7]:
        copy.start()
    token_rows, model_width = tokens_ref.shape
    window = code_ref.shape[0]
    chunks = model_width // WIDE
    padded = piece_rows(chunks)
    above = lax.broadcasted_iota(jnp.int32, (token_rows, token_rows), 0)
    along = lax.broadcasted_iota(jnp.int32, (token_rows, token_rows), 1)
    earlier = jnp.where(above < along, 1.0, 0.0).astype(BF16)
    copies[0].wait()
    copies[1].wait()
    ids = ids_ref[...]
    gates = gates_ref[...].astype(F32)
    members, chosen = [], []
    for expert in range(window):
        hit = ids == expert
        members.append(jnp.sum(jnp.where(hit, 1.0, 0.0), axis=0, keepdims=True))
        chosen.append(jnp.sum(jnp.where(hit, gates, 0.0), axis=0, keepdims=True))
    members = jnp.concatenate(members, axis=0)
    chosen = jnp.concatenate(chosen, axis=0)
    code = jnp.where(members > 0.0, dot(members.astype(BF16), earlier), -1e6)
    code_ref[...] = code
    table, gated = table_of(code, [None, chosen], chunks, padded)

    def columns(ref):
        return jnp.concatenate([ref[:, c * WIDE : (c + 1) * WIDE] for c in range(chunks)], axis=0)

    for copy in copies[4:7]:
        copy.wait()
    for copy in copies[7:]:
        copy.start()
    copies[2].wait()
    rows = dot(table.astype(BF16), columns(tokens_ref))
    copies[3].wait()
    grads = dot(gated.astype(BF16), columns(grads_ref))
    for expert in range(window):
        lines = slice(expert * padded, (expert + 1) * padded)
        sent_ref[expert] = jnp.concatenate([rows[lines], grads[lines]], axis=0).astype(BF16)
    for copy in copies[7:]:
        copy.wait()


def table_kernel(chunks, code_ref, table_ref):
    (table,) = table_of(code_ref[...], [None], chunks, piece_rows(chunks))
    table_ref[...] = table.T.astype(BF16)


def anchor_kernel(*refs):
    refs[-1][...] = jnp.zeros_like(refs[-1])


def keep_kernel(*refs):
    pass


def partial_kernel(groups, got_ref, *refs):
    count = groups + 2
    weights_in, refs = refs[:count], refs[count + 1 :]
    (out_ref, grads_ref, pair_ref, token_ref), refs = refs[:4], refs[4:]
    slices_refs, (rows_ref, down_ref, sems) = refs[:groups], refs[groups:]
    copies = []
    for at, source in enumerate(weights_in):
        target = pair_ref.at[at] if at < groups else down_ref.at[at - groups]
        copies.append(pltpu.make_async_copy(source, target, sems.at[at]))
    for copy in copies:
        copy.start()
    token_ref[...] = jnp.zeros_like(token_ref)
    sources, height, _ = got_ref.shape
    model_width = rows_ref.shape[1]
    chunks = model_width // WIDE
    owned = model_width // groups
    joined = sources // JOIN
    tall = JOIN * SLOTS
    blocks = jnp.concatenate(
        [got_ref[q * JOIN : (q + 1) * JOIN].reshape(JOIN * height, WIDE) for q in range(joined)],
        axis=1,
    )
    lines = dot(sort_matrix(2, chunks, False), blocks)

    def gathered(part):
        return jnp.concatenate(
            [
                jnp.concatenate(
                    [
                        lines[
                            (part * chunks + c) * tall : (part * chunks + c + 1) * tall,
                            q * WIDE : (q + 1) * WIDE,
                        ]
                        for c in range(chunks)
                    ],
                    axis=1,
                )
                for q in range(joined)
            ],
            axis=0,
        ).astype(BF16)

    rows_ref[...] = gathered(0)
    grads_ref[...] = gathered(1)
    me = lax.axis_index("dp")
    wide = pair_ref.shape[2]
    for copy in copies:
        copy.wait()
    pair_sum, down_sum = None, None
    for b in range(groups):
        lanes = pl.ds(pl.multiple_of((me ^ b) * owned, 128), owned)
        rows, grads = rows_ref[:, lanes], grads_ref[:, lanes]
        slices_refs[b][0] = rows
        slices_refs[b][1] = grads
        term = dot(rows, pair_ref[b])
        pair_sum = term if pair_sum is None else pair_sum + term
        if b < 2:
            term = dot(grads, down_ref[b])
            down_sum = term if down_sum is None else down_sum + term
    out_ref[:, :wide] = pair_sum
    out_ref[:, wide:] = down_sum


def back_kernel(groups, grads_ref, partial_ref, *refs):
    pair_ref, down_refs, (acts_ref, out_ref, back_ref) = refs[0], refs[1:-3], refs[-3:]
    me = lax.axis_index("dp")
    model_width = grads_ref.shape[1]
    owned = model_width // groups
    chunks = model_width // WIDE
    hidden_units = partial_ref.shape[1] // 3
    wide = 2 * hidden_units

    def lanes(b):
        return pl.ds(pl.multiple_of((me ^ b) * owned, 128), owned)

    gate_act = partial_ref[:, :hidden_units]
    up_act = partial_ref[:, hidden_units:wide]
    grad_hidden = partial_ref[:, wide:]
    for b in range(2, groups):
        grad_hidden = grad_hidden + dot(grads_ref[:, lanes(b)], down_refs[b - 2][...])
    logistic = jax.nn.sigmoid(gate_act)
    swish_out = gate_act * logistic
    hidden = (swish_out * up_act).astype(BF16)
    grad_up = (grad_hidden * swish_out).astype(BF16)
    grad_gate = (grad_hidden * up_act * logistic * (1.0 + gate_act * (1.0 - logistic))).astype(BF16)
    acts = jnp.concatenate([grad_gate, grad_up], axis=1)
    acts_ref[:, :wide] = acts
    acts_ref[:, wide:] = hidden
    for b in range(groups):
        back_ref[:, lanes(b)] = dot_nt(acts, pair_ref[b])
    tall = JOIN * SLOTS
    joined = grads_ref.shape[0] // tall
    lines = jnp.concatenate(
        [
            jnp.concatenate(
                [
                    back_ref[q * tall : (q + 1) * tall, c * WIDE : (c + 1) * WIDE]
                    for c in range(chunks)
                ],
                axis=0,
            )
            for q in range(joined)
        ],
        axis=1,
    ).astype(BF16)
    blocks = dot(sort_matrix(1, chunks, True), lines)
    height = piece_rows(chunks)
    for q in range(joined):
        for j in range(JOIN):
            part = blocks[j * height : (j + 1) * height, q * WIDE : (q + 1) * WIDE]
            out_ref[q * JOIN + j] = part.astype(BF16)


def combine_kernel(returned_ref, table_ref, out_ref):
    token_rows, model_width = out_ref.shape
    window, height, _ = returned_ref.shape
    lines = returned_ref[...].astype(F32).reshape(window * height, WIDE).astype(BF16)
    result = dot(table_ref[...], lines).astype(BF16)
    for c in range(model_width // WIDE):
        out_ref[:, c * WIDE : (c + 1) * WIDE] = result[c * token_rows : (c + 1) * token_rows]


def grads_kernel(groups, *refs):
    slices_refs, acts_refs, out_ref = refs[:groups], refs[groups : 2 * groups], refs[-1]
    hidden_units = out_ref.shape[3]
    rows_here = acts_refs[0].shape[0]
    step = max(1, min(groups, 640 // rows_here))
    for at in range(3):
        lanes = slice(at * hidden_units, (at + 1) * hidden_units)
        kind = 0 if at < 2 else 1
        total = None
        for first in range(0, groups, step):
            some = range(first, first + step)
            rows = jnp.concatenate([slices_refs[b][kind] for b in some], axis=0)
            acts = jnp.concatenate([acts_refs[b][:, lanes] for b in some], axis=0)
            term = dot_tn(rows, acts)
            total = term if total is None else total + term
        out_ref[0, at] = total


def on_device(tokens, out_grad, expert_ids, gates, expert_weights):
    window = lax.axis_size("expert")
    groups = lax.axis_size("dp")
    token_rows, model_width = tokens.shape
    hidden_units = expert_weights.shape[3]
    owned = model_width // groups
    chunks = model_width // WIDE
    padded = piece_rows(chunks)
    rows_here = window * SLOTS
    wide = 2 * hidden_units
    anywhere = pl.BlockSpec(memory_space=pl.ANY)

    ids_t, gates_t = expert_ids.T, gates.T
    sent, code, pair, down = pl.pallas_call(
        pack_kernel,
        in_specs=[anywhere] * 5,
        out_specs=(pl.BlockSpec(), pl.BlockSpec(), anywhere, anywhere),
        out_shape=(
            shape(window, 2 * padded, WIDE),
            shape(window, token_rows, kind=F32),
            shape(owned, wide),
            shape(owned, hidden_units),
        ),
        scratch_shapes=[pltpu.VMEM(a.shape, a.dtype) for a in (ids_t, gates_t, tokens, out_grad)]
        + [pltpu.VMEM((owned, wide), BF16), pltpu.VMEM((owned, hidden_units), BF16)]
        + [pltpu.SemaphoreType.DMA((9,))],
    )(ids_t, gates_t, tokens, out_grad, expert_weights)

    far = list(range(2, groups, 2))
    pairs = {b: swap(pair, b) for b in far}
    downs = {b: swap(down, b) for b in far}
    pairs[1], downs[1] = swap(pair, 1), swap(down, 1)
    got = lax.all_to_all(sent, "expert", split_axis=0, concat_axis=0, tiled=True)
    table = pl.pallas_call(
        lambda *refs: table_kernel(chunks, *refs),
        out_shape=shape(chunks * token_rows, window * padded),
        compiler_params=params(),
        cost_estimate=cost(10**11, 10**8),
    )(code)

    def arrived(values):
        return pl.pallas_call(
            anchor_kernel,
            in_specs=[anywhere] * len(values),
            out_shape=shape(8, 128, kind=F32),
            compiler_params=params(),
            cost_estimate=cost(10**11, 10**8),
        )(*values)

    here = arrived([pairs[b] for b in far])
    pairs[0] = pair
    for b in far:
        pairs[b + 1] = swap(pairs[b], 1)
    pairs = [pairs[b] for b in range(groups)]
    early = pairs + [down, downs[1]]
    outs = pl.pallas_call(
        lambda *refs: partial_kernel(groups, *refs),
        in_specs=[pl.BlockSpec()] + [anywhere] * len(early) + [pl.BlockSpec()],
        out_shape=[
            shape(rows_here, 3 * hidden_units, kind=F32),
            shape(rows_here, model_width),
            shape(groups, owned, wide),
            shape(8, 128, kind=F32),
        ]
        + [shape(2, rows_here, owned)] * groups,
        scratch_shapes=[
            pltpu.VMEM((rows_here, model_width), BF16),
            pltpu.VMEM((2, owned, hidden_units), BF16),
            pltpu.SemaphoreType.DMA((len(early),)),
        ],
        compiler_params=params(got, *early),
    )(got, *early, here)
    partial, grads, pairs, token = outs[:4]
    slices = list(outs[4:])
    slices = slices[:1] + [swap(slices[b], b) for b in range(1, groups)]

    later = pl.pallas_call(
        keep_kernel,
        in_specs=[anywhere] * (len(far) + 1),
        out_specs=[anywhere] * len(far),
        out_shape=[shape(owned, hidden_units)] * len(far),
        input_output_aliases={at + 1: at for at in range(len(far))},
        compiler_params=params(),
        cost_estimate=cost(10**11, 10**8),
    )(token, *[downs[b] for b in far])
    downs = [value for down in later for value in (down, swap(down, 1))]

    acts, back = pl.pallas_call(
        lambda *refs: back_kernel(groups, *refs),
        out_shape=(shape(rows_here, 3 * hidden_units), shape(window, padded, WIDE)),
        scratch_shapes=[pltpu.VMEM((rows_here, model_width), F32)],
        compiler_params=params(grads, partial, pairs, *downs),
        cost_estimate=cost(10**6, 10**5),
    )(grads, partial, pairs, *downs)
    returned = lax.all_to_all(back, "expert", split_axis=0, concat_axis=0, tiled=True)

    every = slices + [acts] + [swap(acts, b) for b in range(1, groups)]
    weight_grads = pl.pallas_call(
        lambda *refs: grads_kernel(groups, *refs),
        out_shape=shape(1, 3, owned, hidden_units, kind=F32),
        compiler_params=params(*every, expert_weights, expert_weights),
        cost_estimate=cost(6 * groups * rows_here * owned * hidden_units, 12 * owned * hidden_units),
    )(*every)

    token_grads = pl.pallas_call(
        combine_kernel,
        out_shape=shape(token_rows, model_width),
        compiler_params=params(table, back, tokens),
    )(returned, table)
    return (token_grads, weight_grads)


def solution(mesh):
    lines = P(("dp", "expert"), None)
    slabs = P("expert", None, "dp", None)
    return jax.shard_map(
        on_device,
        mesh=mesh,
        in_specs=(lines, lines, lines, lines, slabs),
        out_specs=(lines, slabs),
        check_vma=False,
    )
```

```python
import jax
import jax.numpy as jnp
from jax import lax
from jax.experimental import pallas as pl
from jax.experimental.pallas import tpu as pltpu
from jax.sharding import PartitionSpec as P

SLOTS = 10
WIDE = 512
JOIN = 4
F32 = jnp.float32
BF16 = jnp.bfloat16


def dot(first_op, second_op):
    return jnp.dot(first_op, second_op, preferred_element_type=F32)


def dot_tn(first_op, second_op):
    return lax.dot_general(first_op, second_op, (((0,), (0,)), ((), ())), preferred_element_type=F32)


def dot_nt(first_op, second_op):
    return lax.dot_general(first_op, second_op, (((1,), (1,)), ((), ())), preferred_element_type=F32)


def swap(value, bits):
    return lax.ppermute(value, "dp", [(i, i ^ bits) for i in range(lax.axis_size("dp"))])


def piece_rows(chunks):
    return -(-chunks * SLOTS // 8) * 8


def params(*arrays):
    moved = sum(a.size * a.dtype.itemsize for a in arrays)
    return pltpu.CompilerParams(vmem_limit_bytes=min(56 * 2**20, 12 * 2**20 + 3 * moved))


def cost(flops, moved):
    return pl.CostEstimate(flops=flops, bytes_accessed=moved, transcendentals=0)


def shape(*extent, kind=BF16):
    return jax.ShapeDtypeStruct(extent, kind)


def lower(value, by):
    return jnp.floor((value + 0.5) * (1.0 / by))


def sort_matrix(parts, chunks, transposed):
    padded = piece_rows(chunks)
    wide, tall = JOIN * parts * padded, parts * chunks * JOIN * SLOTS
    extent, axis = ((wide, tall), 0) if transposed else ((tall, wide), 1)
    line = (wide, 1) if transposed else (1, wide)
    place = lax.broadcasted_iota(jnp.int32, line, axis).astype(F32)
    block = lower(place, padded)
    inside = place - block * padded
    source = lower(block, parts)
    part = block - source * parts
    chunk = lower(inside, SLOTS)
    slot = inside - chunk * SLOTS
    target = ((part * chunks + chunk) * JOIN + source) * SLOTS + slot
    target = jnp.where(chunk < chunks, target, -1.0)
    spots = lax.broadcasted_iota(jnp.int32, extent, 1 - axis).astype(F32)
    return jnp.where(spots == target, 1.0, 0.0).astype(BF16)


def table_of(code, values, chunks, padded):
    window, token_rows = code.shape
    spots = lax.broadcasted_iota(jnp.int32, (padded, chunks * token_rows), 0).astype(F32)
    tables = []
    for expert in range(window):
        own = code[expert : expert + 1]
        hit = spots == jnp.concatenate([own + float(SLOTS * c) for c in range(chunks)], axis=1)
        row = []
        for value in values:
            if value is None:
                row.append(jnp.where(hit, 1.0, 0.0))
            else:
                gate = jnp.concatenate([value[expert : expert + 1]] * chunks, axis=1)
                row.append(jnp.where(hit, gate, 0.0))
        tables.append(row)
    return [jnp.concatenate([t[i] for t in tables], axis=0) for i in range(len(values))]


def pack_kernel(
    ids_in, gates_in, tokens_in, grads_in, sent_ref, code_ref, ids_ref, gates_ref, tokens_ref, grads_ref, sems
):
    moves = [
        (ids_in, ids_ref),
        (gates_in, gates_ref),
        (tokens_in, tokens_ref),
        (grads_in, grads_ref),
    ]
    copies = [
        pltpu.make_async_copy(source, target, sems.at[at]) for at, (source, target) in enumerate(moves)
    ]
    for copy in copies:
        copy.start()
    token_rows, model_width = tokens_ref.shape
    window = code_ref.shape[0]
    chunks = model_width // WIDE
    padded = piece_rows(chunks)
    above = lax.broadcasted_iota(jnp.int32, (token_rows, token_rows), 0)
    along = lax.broadcasted_iota(jnp.int32, (token_rows, token_rows), 1)
    earlier = jnp.where(above < along, 1.0, 0.0).astype(BF16)
    copies[0].wait()
    copies[1].wait()
    ids = ids_ref[...]
    gates = gates_ref[...].astype(F32)
    members, chosen = [], []
    for expert in range(window):
        hit = ids == expert
        members.append(jnp.sum(jnp.where(hit, 1.0, 0.0), axis=0, keepdims=True))
        chosen.append(jnp.sum(jnp.where(hit, gates, 0.0), axis=0, keepdims=True))
    members = jnp.concatenate(members, axis=0)
    chosen = jnp.concatenate(chosen, axis=0)
    code = jnp.where(members > 0.0, dot(members.astype(BF16), earlier), -1e6)
    code_ref[...] = code
    table, gated = table_of(code, [None, chosen], chunks, padded)

    def columns(ref):
        return jnp.concatenate([ref[:, c * WIDE : (c + 1) * WIDE] for c in range(chunks)], axis=0)

    copies[2].wait()
    rows = dot(table.astype(BF16), columns(tokens_ref))
    copies[3].wait()
    grads = dot(gated.astype(BF16), columns(grads_ref))
    for expert in range(window):
        lines = slice(expert * padded, (expert + 1) * padded)
        sent_ref[expert] = jnp.concatenate([rows[lines], grads[lines]], axis=0).astype(BF16)


def table_kernel(chunks, code_ref, table_ref):
    (table,) = table_of(code_ref[...], [None], chunks, piece_rows(chunks))
    table_ref[...] = table.T.astype(BF16)


def keep_kernel(*refs):
    pass


def place(source, pair_ref, down_ref, sems, at):
    hidden_units = down_ref.shape[1]
    moves = [
        (source.at[0], pair_ref.at[:, pl.ds(0, hidden_units)]),
        (source.at[1], pair_ref.at[:, pl.ds(hidden_units, hidden_units)]),
        (source.at[2], down_ref),
    ]
    return [
        pltpu.make_async_copy(start, end, sems.at[at, which]) for which, (start, end) in enumerate(moves)
    ]


def partial_kernel(groups, got_ref, own_in, near_in, *refs):
    (out_ref, rows_ref, grads_ref, pair_ref, token_ref), refs = refs[:5], refs[5:]
    slices_refs, (down_ref, sems) = refs[:groups], refs[groups:]
    copies = [
        copy
        for b, source in enumerate((own_in.at[0], near_in.at[0]))
        for copy in place(source, pair_ref.at[b], down_ref.at[b], sems, b)
    ]
    for copy in copies:
        copy.start()
    token_ref[...] = jnp.zeros_like(token_ref)
    sources, height, _ = got_ref.shape
    model_width = rows_ref.shape[1]
    chunks = model_width // WIDE
    owned = model_width // groups
    joined = sources // JOIN
    tall = JOIN * SLOTS
    blocks = jnp.concatenate(
        [got_ref[q * JOIN : (q + 1) * JOIN].reshape(JOIN * height, WIDE) for q in range(joined)],
        axis=1,
    )
    lines = dot(sort_matrix(2, chunks, False), blocks)

    def gathered(part):
        return jnp.concatenate(
            [
                jnp.concatenate(
                    [
                        lines[
                            (part * chunks + c) * tall : (part * chunks + c + 1) * tall,
                            q * WIDE : (q + 1) * WIDE,
                        ]
                        for c in range(chunks)
                    ],
                    axis=1,
                )
                for q in range(joined)
            ],
            axis=0,
        ).astype(BF16)

    rows_ref[...] = gathered(0)
    grads_ref[...] = gathered(1)
    me = lax.axis_index("dp")
    wide = pair_ref.shape[2]
    for copy in copies:
        copy.wait()
    pair_sum, down_sum = None, None
    for b in range(groups):
        lanes = pl.ds(pl.multiple_of((me ^ b) * owned, 128), owned)
        rows, grads = rows_ref[:, lanes], grads_ref[:, lanes]
        slices_refs[b][0] = rows
        slices_refs[b][1] = grads
        if b < 2:
            term = dot(rows, pair_ref[b])
            pair_sum = term if pair_sum is None else pair_sum + term
            term = dot(grads, down_ref[b])
            down_sum = term if down_sum is None else down_sum + term
    out_ref[:, :wide] = pair_sum
    out_ref[:, wide:] = down_sum


def lanes_of(owner, owned):
    return pl.ds(pl.multiple_of(owner * owned, 128), owned)


def far_kernel(groups, rows_ref, grads_ref, partial_ref, *refs):
    far = range(2, groups, 2)
    weights_in, (out_ref, pair_ref, down_ref, sems) = refs[: len(far)], refs[len(far) :]
    copies = [
        place(source.at[0], pair_ref.at[at], down_ref.at[at], sems, at)
        for at, source in enumerate(weights_in)
    ]
    for some in copies:
        for copy in some:
            copy.start()
    me = lax.axis_index("dp")
    owned, wide = pair_ref.shape[1:]
    pair_sum, down_sum = partial_ref[:, :wide], partial_ref[:, wide:]
    for at, b in enumerate(far):
        for copy in copies[at]:
            copy.wait()
        lanes = lanes_of(me ^ b, owned)
        pair_sum = pair_sum + dot(rows_ref[:, lanes], pair_ref[at])
        down_sum = down_sum + dot(grads_ref[:, lanes], down_ref[at])
    out_ref[:, :wide] = pair_sum
    out_ref[:, wide:] = down_sum


def back_kernel(groups, rows_ref, grads_ref, partial_ref, near_ref, far_ref, *refs):
    last_refs, (acts_ref, out_ref, back_ref) = refs[:-3], refs[-3:]
    me = lax.axis_index("dp")
    model_width = grads_ref.shape[1]
    owned = model_width // groups
    chunks = model_width // WIDE
    hidden_units = partial_ref.shape[1] // 3
    wide = 2 * hidden_units

    def lanes(b):
        return lanes_of(me ^ b, owned)

    gate_act = partial_ref[:, :hidden_units]
    up_act = partial_ref[:, hidden_units:wide]
    grad_hidden = partial_ref[:, wide:]
    for at, ref in enumerate(last_refs):
        here = lanes(2 * at + 3)
        gate_act = gate_act + dot(rows_ref[:, here], ref[0, 0])
        up_act = up_act + dot(rows_ref[:, here], ref[0, 1])
        grad_hidden = grad_hidden + dot(grads_ref[:, here], ref[0, 2])
    logistic = jax.nn.sigmoid(gate_act)
    swish_out = gate_act * logistic
    hidden = (swish_out * up_act).astype(BF16)
    grad_up = (grad_hidden * swish_out).astype(BF16)
    grad_gate = (grad_hidden * up_act * logistic * (1.0 + gate_act * (1.0 - logistic))).astype(BF16)
    acts = jnp.concatenate([grad_gate, grad_up], axis=1)
    acts_ref[:, :wide] = acts
    acts_ref[:, wide:] = hidden
    for b in range(groups):
        if b < 2:
            term = dot_nt(acts, near_ref[b])
        elif b % 2 == 0:
            term = dot_nt(acts, far_ref[b // 2 - 1])
        else:
            ref = last_refs[b // 2 - 1]
            term = dot_nt(grad_gate, ref[0, 0]) + dot_nt(grad_up, ref[0, 1])
        back_ref[:, lanes(b)] = term
    tall = JOIN * SLOTS
    joined = grads_ref.shape[0] // tall
    lines = jnp.concatenate(
        [
            jnp.concatenate(
                [
                    back_ref[q * tall : (q + 1) * tall, c * WIDE : (c + 1) * WIDE]
                    for c in range(chunks)
                ],
                axis=0,
            )
            for q in range(joined)
        ],
        axis=1,
    ).astype(BF16)
    blocks = dot(sort_matrix(1, chunks, True), lines)
    height = piece_rows(chunks)
    for q in range(joined):
        for j in range(JOIN):
            part = blocks[j * height : (j + 1) * height, q * WIDE : (q + 1) * WIDE]
            out_ref[q * JOIN + j] = part.astype(BF16)


def combine_kernel(returned_ref, table_ref, out_ref):
    token_rows, model_width = out_ref.shape
    window, height, _ = returned_ref.shape
    lines = returned_ref[...].astype(F32).reshape(window * height, WIDE).astype(BF16)
    result = dot(table_ref[...], lines).astype(BF16)
    for c in range(model_width // WIDE):
        out_ref[:, c * WIDE : (c + 1) * WIDE] = result[c * token_rows : (c + 1) * token_rows]


def grads_kernel(groups, *refs):
    slices_refs, acts_refs, out_ref = refs[:groups], refs[groups : 2 * groups], refs[-1]
    hidden_units = out_ref.shape[3]
    rows_here = acts_refs[0].shape[0]
    step = max(1, min(groups, 640 // rows_here))
    for at in range(3):
        lanes = slice(at * hidden_units, (at + 1) * hidden_units)
        kind = 0 if at < 2 else 1
        total = None
        for first in range(0, groups, step):
            some = range(first, first + step)
            rows = jnp.concatenate([slices_refs[b][kind] for b in some], axis=0)
            acts = jnp.concatenate([acts_refs[b][:, lanes] for b in some], axis=0)
            term = dot_tn(rows, acts)
            total = term if total is None else total + term
        out_ref[0, at] = total


def on_device(tokens, out_grad, expert_ids, gates, expert_weights):
    window = lax.axis_size("expert")
    groups = lax.axis_size("dp")
    token_rows, model_width = tokens.shape
    hidden_units = expert_weights.shape[3]
    owned = model_width // groups
    chunks = model_width // WIDE
    padded = piece_rows(chunks)
    rows_here = window * SLOTS
    wide = 2 * hidden_units
    anywhere = pl.BlockSpec(memory_space=pl.ANY)

    far = list(range(2, groups, 2))
    arriving = [swap(expert_weights, b) for b in far]
    near = swap(expert_weights, 1)

    ids_t, gates_t = expert_ids.T, gates.T
    sent, code = pl.pallas_call(
        pack_kernel,
        in_specs=[anywhere] * 4,
        out_shape=(
            shape(window, 2 * padded, WIDE),
            shape(window, token_rows, kind=F32),
        ),
        scratch_shapes=[pltpu.VMEM(a.shape, a.dtype) for a in (ids_t, gates_t, tokens, out_grad)]
        + [pltpu.SemaphoreType.DMA((4,))],
    )(ids_t, gates_t, tokens, out_grad)

    got = lax.all_to_all(sent, "expert", split_axis=0, concat_axis=0, tiled=True)
    table = pl.pallas_call(
        lambda *refs: table_kernel(chunks, *refs),
        out_shape=shape(chunks * token_rows, window * padded),
        compiler_params=params(),
        cost_estimate=cost(10**11, 10**8),
    )(code)

    outs = pl.pallas_call(
        lambda *refs: partial_kernel(groups, *refs),
        in_specs=[pl.BlockSpec()] + [anywhere] * 2,
        out_shape=[
            shape(rows_here, 3 * hidden_units, kind=F32),
            shape(rows_here, model_width),
            shape(rows_here, model_width),
            shape(2, owned, wide),
            shape(8, 128, kind=F32),
        ]
        + [shape(2, rows_here, owned)] * groups,
        scratch_shapes=[
            pltpu.VMEM((2, owned, hidden_units), BF16),
            pltpu.SemaphoreType.DMA((2, 3)),
        ],
        compiler_params=params(got, expert_weights, expert_weights),
    )(got, expert_weights, near)
    partial, rows, grads, near_pairs, token = outs[:5]
    slices = list(outs[5:])
    slices = slices[:1] + [swap(slices[b], b) for b in range(1, groups)]

    arrived = pl.pallas_call(
        keep_kernel,
        in_specs=[anywhere] * (len(far) + 1),
        out_specs=[anywhere] * len(far),
        out_shape=[shape(*expert_weights.shape)] * len(far),
        input_output_aliases={at + 1: at for at in range(len(far))},
        compiler_params=params(),
        cost_estimate=cost(10**11, 10**8),
    )(token, *arriving)
    last = [swap(value, 1) for value in arrived]
    partial, far_pairs = pl.pallas_call(
        lambda *refs: far_kernel(groups, *refs),
        in_specs=[pl.BlockSpec()] * 3 + [anywhere] * len(far),
        out_shape=(shape(rows_here, 3 * hidden_units, kind=F32), shape(len(far), owned, wide)),
        scratch_shapes=[
            pltpu.VMEM((len(far), owned, hidden_units), BF16),
            pltpu.SemaphoreType.DMA((len(far), 3)),
        ],
        compiler_params=params(rows, grads, *arrived, *arrived),
    )(rows, grads, partial, *arrived)

    acts, back = pl.pallas_call(
        lambda *refs: back_kernel(groups, *refs),
        out_shape=(shape(rows_here, 3 * hidden_units), shape(window, padded, WIDE)),
        scratch_shapes=[pltpu.VMEM((rows_here, model_width), F32)],
        compiler_params=params(rows, grads, partial, near_pairs, far_pairs, *last),
        cost_estimate=cost(10**6, 10**5),
    )(rows, grads, partial, near_pairs, far_pairs, *last)
    returned = lax.all_to_all(back, "expert", split_axis=0, concat_axis=0, tiled=True)

    every = slices + [acts] + [swap(acts, b) for b in range(1, groups)]
    weight_grads = pl.pallas_call(
        lambda *refs: grads_kernel(groups, *refs),
        out_shape=shape(1, 3, owned, hidden_units, kind=F32),
        compiler_params=params(*every, expert_weights, expert_weights),
        cost_estimate=cost(6 * groups * rows_here * owned * hidden_units, 12 * owned * hidden_units),
    )(*every)

    token_grads = pl.pallas_call(
        combine_kernel,
        out_shape=shape(token_rows, model_width),
        compiler_params=params(table, back, tokens),
    )(returned, table)
    return (token_grads, weight_grads)


def solution(mesh):
    lines = P(("dp", "expert"), None)
    slabs = P("expert", None, "dp", None)
    return jax.shard_map(
        on_device,
        mesh=mesh,
        in_specs=(lines, lines, lines, lines, slabs),
        out_specs=(lines, slabs),
        check_vma=False,
    )
```

```python
import jax
import jax.numpy as jnp
from jax import lax
from jax.experimental import pallas as pl
from jax.experimental.pallas import tpu as pltpu
from jax.sharding import PartitionSpec as P

SLOTS = 10
WIDE = 512
JOIN = 4
F32 = jnp.float32
BF16 = jnp.bfloat16


def dot(first_op, second_op):
    return jnp.dot(first_op, second_op, preferred_element_type=F32)


def dot_tn(first_op, second_op):
    return lax.dot_general(first_op, second_op, (((0,), (0,)), ((), ())), preferred_element_type=F32)


def dot_nt(first_op, second_op):
    return lax.dot_general(first_op, second_op, (((1,), (1,)), ((), ())), preferred_element_type=F32)


def swap(value, bits):
    return lax.ppermute(value, "dp", [(i, i ^ bits) for i in range(lax.axis_size("dp"))])


def piece_rows(chunks):
    return -(-chunks * SLOTS // 8) * 8


def params(*arrays):
    moved = sum(a.size * a.dtype.itemsize for a in arrays)
    return pltpu.CompilerParams(vmem_limit_bytes=min(56 * 2**20, 12 * 2**20 + 3 * moved))


def cost(flops, moved):
    return pl.CostEstimate(flops=flops, bytes_accessed=moved, transcendentals=0)


def shape(*extent, kind=BF16):
    return jax.ShapeDtypeStruct(extent, kind)


def lower(value, by):
    return jnp.floor((value + 0.5) * (1.0 / by))


def sort_matrix(parts, chunks, transposed):
    padded = piece_rows(chunks)
    wide, tall = JOIN * parts * padded, parts * chunks * JOIN * SLOTS
    extent, axis = ((wide, tall), 0) if transposed else ((tall, wide), 1)
    line = (wide, 1) if transposed else (1, wide)
    place = lax.broadcasted_iota(jnp.int32, line, axis).astype(F32)
    block = lower(place, padded)
    inside = place - block * padded
    source = lower(block, parts)
    part = block - source * parts
    chunk = lower(inside, SLOTS)
    slot = inside - chunk * SLOTS
    target = ((part * chunks + chunk) * JOIN + source) * SLOTS + slot
    target = jnp.where(chunk < chunks, target, -1.0)
    spots = lax.broadcasted_iota(jnp.int32, extent, 1 - axis).astype(F32)
    return jnp.where(spots == target, 1.0, 0.0).astype(BF16)


def table_of(code, values, chunks, padded):
    window, token_rows = code.shape
    spots = lax.broadcasted_iota(jnp.int32, (padded, chunks * token_rows), 0).astype(F32)
    tables = []
    for expert in range(window):
        own = code[expert : expert + 1]
        hit = spots == jnp.concatenate([own + float(SLOTS * c) for c in range(chunks)], axis=1)
        row = []
        for value in values:
            if value is None:
                row.append(jnp.where(hit, 1.0, 0.0))
            else:
                gate = jnp.concatenate([value[expert : expert + 1]] * chunks, axis=1)
                row.append(jnp.where(hit, gate, 0.0))
        tables.append(row)
    return [jnp.concatenate([t[i] for t in tables], axis=0) for i in range(len(values))]


def pack_kernel(ids_ref, gates_ref, tokens_ref, grads_ref, sent_ref, code_ref):
    token_rows, model_width = tokens_ref.shape
    window = code_ref.shape[0]
    chunks = model_width // WIDE
    padded = piece_rows(chunks)
    above = lax.broadcasted_iota(jnp.int32, (token_rows, token_rows), 0)
    along = lax.broadcasted_iota(jnp.int32, (token_rows, token_rows), 1)
    earlier = jnp.where(above < along, 1.0, 0.0).astype(BF16)
    ids = ids_ref[...]
    gates = gates_ref[...].astype(F32)
    members, chosen = [], []
    for expert in range(window):
        hit = ids == expert
        members.append(jnp.sum(jnp.where(hit, 1.0, 0.0), axis=0, keepdims=True))
        chosen.append(jnp.sum(jnp.where(hit, gates, 0.0), axis=0, keepdims=True))
    members = jnp.concatenate(members, axis=0)
    chosen = jnp.concatenate(chosen, axis=0)
    code = jnp.where(members > 0.0, dot(members.astype(BF16), earlier), -1e6)
    code_ref[...] = code
    table, gated = table_of(code, [None, chosen], chunks, padded)

    def columns(ref):
        return jnp.concatenate([ref[:, c * WIDE : (c + 1) * WIDE] for c in range(chunks)], axis=0)

    rows = dot(table.astype(BF16), columns(tokens_ref))
    grads = dot(gated.astype(BF16), columns(grads_ref))
    for expert in range(window):
        lines = slice(expert * padded, (expert + 1) * padded)
        sent_ref[expert] = jnp.concatenate([rows[lines], grads[lines]], axis=0).astype(BF16)


def table_kernel(chunks, code_ref, table_ref):
    (table,) = table_of(code_ref[...], [None], chunks, piece_rows(chunks))
    table_ref[...] = table.T.astype(BF16)


def keep_kernel(*refs):
    pass


def place(source, pair_ref, down_ref, sems, at):
    hidden_units = down_ref.shape[1]
    moves = [
        (source.at[0], pair_ref.at[:, pl.ds(0, hidden_units)]),
        (source.at[1], pair_ref.at[:, pl.ds(hidden_units, hidden_units)]),
        (source.at[2], down_ref),
    ]
    return [
        pltpu.make_async_copy(start, end, sems.at[at, which]) for which, (start, end) in enumerate(moves)
    ]


def partial_kernel(groups, got_ref, own_in, near_in, *refs):
    (out_ref, rows_ref, grads_ref, pair_ref, token_ref), refs = refs[:5], refs[5:]
    slices_refs, (down_ref, sems) = refs[: groups - 1], refs[groups - 1 :]
    copies = [
        copy
        for b, source in enumerate((own_in.at[0], near_in.at[0]))
        for copy in place(source, pair_ref.at[b], down_ref.at[b], sems, b)
    ]
    for copy in copies:
        copy.start()
    token_ref[...] = jnp.zeros_like(token_ref)
    sources, height, _ = got_ref.shape
    model_width = rows_ref.shape[1]
    chunks = model_width // WIDE
    owned = model_width // groups
    joined = sources // JOIN
    tall = JOIN * SLOTS
    blocks = jnp.concatenate(
        [got_ref[q * JOIN : (q + 1) * JOIN].reshape(JOIN * height, WIDE) for q in range(joined)],
        axis=1,
    )
    lines = dot(sort_matrix(2, chunks, False), blocks)

    def gathered(part):
        return jnp.concatenate(
            [
                jnp.concatenate(
                    [
                        lines[
                            (part * chunks + c) * tall : (part * chunks + c + 1) * tall,
                            q * WIDE : (q + 1) * WIDE,
                        ]
                        for c in range(chunks)
                    ],
                    axis=1,
                )
                for q in range(joined)
            ],
            axis=0,
        ).astype(BF16)

    rows_ref[...] = gathered(0)
    grads_ref[...] = gathered(1)
    me = lax.axis_index("dp")
    wide = pair_ref.shape[2]
    for copy in copies:
        copy.wait()
    pair_sum, down_sum = None, None
    for b in range(groups):
        lanes = pl.ds(pl.multiple_of((me ^ b) * owned, 128), owned)
        rows, grads = rows_ref[:, lanes], grads_ref[:, lanes]
        target, first = (slices_refs[0], 2) if b == 0 else (slices_refs[b - 1], 0)
        target[first] = rows
        target[first + 1] = grads
        if b < 2:
            term = dot(rows, pair_ref[b])
            pair_sum = term if pair_sum is None else pair_sum + term
            term = dot(grads, down_ref[b])
            down_sum = term if down_sum is None else down_sum + term
    out_ref[:, :wide] = pair_sum
    out_ref[:, wide:] = down_sum


def lanes_of(owner, owned):
    return pl.ds(pl.multiple_of(owner * owned, 128), owned)


def far_kernel(groups, rows_ref, grads_ref, partial_ref, *refs):
    far = range(2, groups, 2)
    weights_in, (out_ref, pair_ref, down_ref, sems) = refs[: len(far)], refs[len(far) :]
    copies = [
        place(source.at[0], pair_ref.at[at], down_ref.at[at], sems, at)
        for at, source in enumerate(weights_in)
    ]
    for some in copies:
        for copy in some:
            copy.start()
    me = lax.axis_index("dp")
    owned, wide = pair_ref.shape[1:]
    pair_sum, down_sum = partial_ref[:, :wide], partial_ref[:, wide:]
    for at, b in enumerate(far):
        for copy in copies[at]:
            copy.wait()
        lanes = lanes_of(me ^ b, owned)
        pair_sum = pair_sum + dot(rows_ref[:, lanes], pair_ref[at])
        down_sum = down_sum + dot(grads_ref[:, lanes], down_ref[at])
    out_ref[:, :wide] = pair_sum
    out_ref[:, wide:] = down_sum


def back_kernel(groups, rows_ref, grads_ref, partial_ref, near_ref, far_ref, *refs):
    last_refs, (acts_ref, out_ref, back_ref) = refs[:-3], refs[-3:]
    me = lax.axis_index("dp")
    model_width = grads_ref.shape[1]
    owned = model_width // groups
    chunks = model_width // WIDE
    hidden_units = partial_ref.shape[1] // 3
    wide = 2 * hidden_units

    def lanes(b):
        return lanes_of(me ^ b, owned)

    gate_act = partial_ref[:, :hidden_units]
    up_act = partial_ref[:, hidden_units:wide]
    grad_hidden = partial_ref[:, wide:]
    for at, ref in enumerate(last_refs):
        here = lanes(2 * at + 3)
        gate_act = gate_act + dot(rows_ref[:, here], ref[0, 0])
        up_act = up_act + dot(rows_ref[:, here], ref[0, 1])
        grad_hidden = grad_hidden + dot(grads_ref[:, here], ref[0, 2])
    logistic = jax.nn.sigmoid(gate_act)
    swish_out = gate_act * logistic
    hidden = (swish_out * up_act).astype(BF16)
    grad_up = (grad_hidden * swish_out).astype(BF16)
    grad_gate = (grad_hidden * up_act * logistic * (1.0 + gate_act * (1.0 - logistic))).astype(BF16)
    acts = jnp.concatenate([grad_gate, grad_up], axis=1)
    acts_ref[:, :wide] = acts
    acts_ref[:, wide:] = hidden
    for b in range(groups):
        if b < 2:
            term = dot_nt(acts, near_ref[b])
        elif b % 2 == 0:
            term = dot_nt(acts, far_ref[b // 2 - 1])
        else:
            ref = last_refs[b // 2 - 1]
            term = dot_nt(grad_gate, ref[0, 0]) + dot_nt(grad_up, ref[0, 1])
        back_ref[:, lanes(b)] = term
    tall = JOIN * SLOTS
    joined = grads_ref.shape[0] // tall
    lines = jnp.concatenate(
        [
            jnp.concatenate(
                [
                    back_ref[q * tall : (q + 1) * tall, c * WIDE : (c + 1) * WIDE]
                    for c in range(chunks)
                ],
                axis=0,
            )
            for q in range(joined)
        ],
        axis=1,
    ).astype(BF16)
    blocks = dot(sort_matrix(1, chunks, True), lines)
    height = piece_rows(chunks)
    for q in range(joined):
        for j in range(JOIN):
            part = blocks[j * height : (j + 1) * height, q * WIDE : (q + 1) * WIDE]
            out_ref[q * JOIN + j] = part.astype(BF16)


def combine_kernel(returned_ref, table_ref, out_ref):
    token_rows, model_width = out_ref.shape
    window, height, _ = returned_ref.shape
    lines = returned_ref[...].astype(F32).reshape(window * height, WIDE).astype(BF16)
    result = dot(table_ref[...], lines).astype(BF16)
    for c in range(model_width // WIDE):
        out_ref[:, c * WIDE : (c + 1) * WIDE] = result[c * token_rows : (c + 1) * token_rows]


def grads_kernel(groups, *refs):
    slices_refs, acts_refs, out_ref = refs[:groups], refs[groups : 2 * groups], refs[-1]
    hidden_units = out_ref.shape[3]
    rows_here = acts_refs[0].shape[0]
    step = max(1, min(groups, 640 // rows_here))
    for at in range(3):
        lanes = slice(at * hidden_units, (at + 1) * hidden_units)
        kind = 0 if at < 2 else 1
        places = [kind + 2 if b == 0 else kind for b in range(groups)]
        total = None
        for first in range(0, groups, step):
            some = range(first, first + step)
            rows = jnp.concatenate([slices_refs[b][places[b]] for b in some], axis=0)
            acts = jnp.concatenate([acts_refs[b][:, lanes] for b in some], axis=0)
            term = dot_tn(rows, acts)
            total = term if total is None else total + term
        out_ref[0, at] = total


def on_device(tokens, out_grad, expert_ids, gates, expert_weights):
    window = lax.axis_size("expert")
    groups = lax.axis_size("dp")
    token_rows, model_width = tokens.shape
    hidden_units = expert_weights.shape[3]
    owned = model_width // groups
    chunks = model_width // WIDE
    padded = piece_rows(chunks)
    rows_here = window * SLOTS
    wide = 2 * hidden_units
    anywhere = pl.BlockSpec(memory_space=pl.ANY)

    far = list(range(2, groups, 2))
    arriving = [swap(expert_weights, b) for b in far]
    near = swap(expert_weights, 1)

    ids_t, gates_t = expert_ids.T, gates.T
    sent, code = pl.pallas_call(
        pack_kernel,
        out_shape=(
            shape(window, 2 * padded, WIDE),
            shape(window, token_rows, kind=F32),
        ),
        compiler_params=params(tokens, out_grad),
    )(ids_t, gates_t, tokens, out_grad)

    got = lax.all_to_all(sent, "expert", split_axis=0, concat_axis=0, tiled=True)
    table = pl.pallas_call(
        lambda *refs: table_kernel(chunks, *refs),
        out_shape=shape(chunks * token_rows, window * padded),
        compiler_params=params(),
        cost_estimate=cost(10**11, 10**8),
    )(code)

    outs = pl.pallas_call(
        lambda *refs: partial_kernel(groups, *refs),
        in_specs=[pl.BlockSpec()] + [anywhere] * 2,
        out_shape=[
            shape(rows_here, 3 * hidden_units, kind=F32),
            shape(rows_here, model_width),
            shape(rows_here, model_width),
            shape(2, owned, wide),
            shape(8, 128, kind=F32),
        ]
        + [shape(4, rows_here, owned)]
        + [shape(2, rows_here, owned)] * (groups - 2),
        scratch_shapes=[
            pltpu.VMEM((2, owned, hidden_units), BF16),
            pltpu.SemaphoreType.DMA((2, 3)),
        ],
        compiler_params=params(got, expert_weights, expert_weights),
    )(got, expert_weights, near)
    partial, rows, grads, near_pairs, token = outs[:5]
    slices = list(outs[5:])
    slices = slices[:1] + [swap(slices[b - 1], b) for b in range(1, groups)]

    arrived = pl.pallas_call(
        keep_kernel,
        in_specs=[anywhere] * (len(far) + 1),
        out_specs=[anywhere] * len(far),
        out_shape=[shape(*expert_weights.shape)] * len(far),
        input_output_aliases={at + 1: at for at in range(len(far))},
        compiler_params=params(),
        cost_estimate=cost(10**11, 10**8),
    )(token, *arriving)
    last = [swap(value, 1) for value in arrived]
    partial, far_pairs = pl.pallas_call(
        lambda *refs: far_kernel(groups, *refs),
        in_specs=[pl.BlockSpec()] * 3 + [anywhere] * len(far),
        out_shape=(shape(rows_here, 3 * hidden_units, kind=F32), shape(len(far), owned, wide)),
        scratch_shapes=[
            pltpu.VMEM((len(far), owned, hidden_units), BF16),
            pltpu.SemaphoreType.DMA((len(far), 3)),
        ],
        compiler_params=params(rows, grads, *arrived, *arrived),
    )(rows, grads, partial, *arrived)

    acts, back = pl.pallas_call(
        lambda *refs: back_kernel(groups, *refs),
        out_shape=(shape(rows_here, 3 * hidden_units), shape(window, padded, WIDE)),
        scratch_shapes=[pltpu.VMEM((rows_here, model_width), F32)],
        compiler_params=params(rows, grads, partial, near_pairs, far_pairs, *last),
        cost_estimate=cost(10**6, 10**5),
    )(rows, grads, partial, near_pairs, far_pairs, *last)
    returned = lax.all_to_all(back, "expert", split_axis=0, concat_axis=0, tiled=True)

    every = slices + [acts] + [swap(acts, b) for b in range(1, groups)]
    weight_grads = pl.pallas_call(
        lambda *refs: grads_kernel(groups, *refs),
        out_shape=shape(1, 3, owned, hidden_units, kind=F32),
        compiler_params=params(*every, expert_weights, expert_weights),
        cost_estimate=cost(6 * groups * rows_here * owned * hidden_units, 12 * owned * hidden_units),
    )(*every)

    token_grads = pl.pallas_call(
        combine_kernel,
        out_shape=shape(token_rows, model_width),
        compiler_params=params(table, back, tokens),
    )(returned, table)
    return (token_grads, weight_grads)


def solution(mesh):
    lines = P(("dp", "expert"), None)
    slabs = P("expert", None, "dp", None)
    return jax.shard_map(
        on_device,
        mesh=mesh,
        in_specs=(lines, lines, lines, lines, slabs),
        out_specs=(lines, slabs),
        check_vma=False,
    )
```

```python
import jax
import jax.numpy as jnp
from jax import lax
from jax.experimental import pallas as pl
from jax.experimental.pallas import tpu as pltpu
from jax.sharding import PartitionSpec as P

SLOTS = 10
WIDE = 512
JOIN = 4
F32 = jnp.float32
BF16 = jnp.bfloat16


def dot(first_op, second_op):
    return jnp.dot(first_op, second_op, preferred_element_type=F32)


def dot_tn(first_op, second_op):
    return lax.dot_general(first_op, second_op, (((0,), (0,)), ((), ())), preferred_element_type=F32)


def dot_nt(first_op, second_op):
    return lax.dot_general(first_op, second_op, (((1,), (1,)), ((), ())), preferred_element_type=F32)


def swap(value, bits):
    return lax.ppermute(value, "dp", [(i, i ^ bits) for i in range(lax.axis_size("dp"))])


def piece_rows(chunks):
    return -(-chunks * SLOTS // 8) * 8


def params(*arrays):
    moved = sum(a.size * a.dtype.itemsize for a in arrays)
    return pltpu.CompilerParams(vmem_limit_bytes=min(56 * 2**20, 12 * 2**20 + 3 * moved))


def cost(flops, moved):
    return pl.CostEstimate(flops=flops, bytes_accessed=moved, transcendentals=0)


def shape(*extent, kind=BF16):
    return jax.ShapeDtypeStruct(extent, kind)


def lower(value, by):
    return jnp.floor((value + 0.5) * (1.0 / by))


def sort_matrix(parts, chunks, transposed):
    padded = piece_rows(chunks)
    wide, tall = JOIN * parts * padded, parts * chunks * JOIN * SLOTS
    extent, axis = ((wide, tall), 0) if transposed else ((tall, wide), 1)
    line = (wide, 1) if transposed else (1, wide)
    place = lax.broadcasted_iota(jnp.int32, line, axis).astype(F32)
    block = lower(place, padded)
    inside = place - block * padded
    source = lower(block, parts)
    part = block - source * parts
    chunk = lower(inside, SLOTS)
    slot = inside - chunk * SLOTS
    target = ((part * chunks + chunk) * JOIN + source) * SLOTS + slot
    target = jnp.where(chunk < chunks, target, -1.0)
    spots = lax.broadcasted_iota(jnp.int32, extent, 1 - axis).astype(F32)
    return jnp.where(spots == target, 1.0, 0.0).astype(BF16)


def table_of(code, values, chunks, padded):
    window, token_rows = code.shape
    spots = lax.broadcasted_iota(jnp.int32, (padded, chunks * token_rows), 0).astype(F32)
    tables = []
    for expert in range(window):
        own = code[expert : expert + 1]
        hit = spots == jnp.concatenate([own + float(SLOTS * c) for c in range(chunks)], axis=1)
        row = []
        for value in values:
            if value is None:
                row.append(jnp.where(hit, 1.0, 0.0))
            else:
                gate = jnp.concatenate([value[expert : expert + 1]] * chunks, axis=1)
                row.append(jnp.where(hit, gate, 0.0))
        tables.append(row)
    return [jnp.concatenate([t[i] for t in tables], axis=0) for i in range(len(values))]


def token_kernel(token_ref):
    token_ref[...] = jnp.zeros_like(token_ref)


def pack_kernel(ids_ref, gates_ref, tokens_ref, grads_ref, _, sent_ref, code_ref):
    token_rows, model_width = tokens_ref.shape
    window = code_ref.shape[0]
    chunks = model_width // WIDE
    padded = piece_rows(chunks)
    above = lax.broadcasted_iota(jnp.int32, (token_rows, token_rows), 0)
    along = lax.broadcasted_iota(jnp.int32, (token_rows, token_rows), 1)
    earlier = jnp.where(above < along, 1.0, 0.0).astype(BF16)
    ids = ids_ref[...]
    gates = gates_ref[...].astype(F32)
    members, chosen = [], []
    for expert in range(window):
        hit = ids == expert
        members.append(jnp.sum(jnp.where(hit, 1.0, 0.0), axis=0, keepdims=True))
        chosen.append(jnp.sum(jnp.where(hit, gates, 0.0), axis=0, keepdims=True))
    members = jnp.concatenate(members, axis=0)
    chosen = jnp.concatenate(chosen, axis=0)
    code = jnp.where(members > 0.0, dot(members.astype(BF16), earlier), -1e6)
    code_ref[...] = code
    table, gated = table_of(code, [None, chosen], chunks, padded)

    def columns(ref):
        return jnp.concatenate([ref[:, c * WIDE : (c + 1) * WIDE] for c in range(chunks)], axis=0)

    rows = dot(table.astype(BF16), columns(tokens_ref))
    grads = dot(gated.astype(BF16), columns(grads_ref))
    for expert in range(window):
        lines = slice(expert * padded, (expert + 1) * padded)
        sent_ref[expert] = jnp.concatenate([rows[lines], grads[lines]], axis=0).astype(BF16)


def table_kernel(chunks, code_ref, table_ref):
    (table,) = table_of(code_ref[...], [None], chunks, piece_rows(chunks))
    table_ref[...] = table.T.astype(BF16)


def keep_kernel(*refs):
    pass


def place(source, pair_ref, down_ref, sems, at):
    hidden_units = down_ref.shape[1]
    moves = [
        (source.at[0], pair_ref.at[:, pl.ds(0, hidden_units)]),
        (source.at[1], pair_ref.at[:, pl.ds(hidden_units, hidden_units)]),
        (source.at[2], down_ref),
    ]
    return [
        pltpu.make_async_copy(start, end, sems.at[at, which]) for which, (start, end) in enumerate(moves)
    ]


def partial_kernel(groups, got_ref, own_in, near_in, *refs):
    (out_ref, rows_ref, grads_ref, pair_ref, token_ref), refs = refs[:5], refs[5:]
    slices_refs, (down_ref, sems) = refs[: groups - 1], refs[groups - 1 :]
    copies = [
        copy
        for b, source in enumerate((own_in.at[0], near_in.at[0]))
        for copy in place(source, pair_ref.at[b], down_ref.at[b], sems, b)
    ]
    for copy in copies:
        copy.start()
    token_ref[...] = jnp.zeros_like(token_ref)
    sources, height, _ = got_ref.shape
    model_width = rows_ref.shape[1]
    chunks = model_width // WIDE
    owned = model_width // groups
    joined = sources // JOIN
    tall = JOIN * SLOTS
    blocks = jnp.concatenate(
        [got_ref[q * JOIN : (q + 1) * JOIN].reshape(JOIN * height, WIDE) for q in range(joined)],
        axis=1,
    )
    lines = dot(sort_matrix(2, chunks, False), blocks)

    def gathered(part):
        return jnp.concatenate(
            [
                jnp.concatenate(
                    [
                        lines[
                            (part * chunks + c) * tall : (part * chunks + c + 1) * tall,
                            q * WIDE : (q + 1) * WIDE,
                        ]
                        for c in range(chunks)
                    ],
                    axis=1,
                )
                for q in range(joined)
            ],
            axis=0,
        ).astype(BF16)

    rows_ref[...] = gathered(0)
    grads_ref[...] = gathered(1)
    me = lax.axis_index("dp")
    wide = pair_ref.shape[2]
    for copy in copies:
        copy.wait()
    pair_sum, down_sum = None, None
    for b in range(groups):
        lanes = pl.ds(pl.multiple_of((me ^ b) * owned, 128), owned)
        rows, grads = rows_ref[:, lanes], grads_ref[:, lanes]
        target, first = (slices_refs[0], 2) if b == 0 else (slices_refs[b - 1], 0)
        target[first] = rows
        target[first + 1] = grads
        if b < 2:
            term = dot(rows, pair_ref[b])
            pair_sum = term if pair_sum is None else pair_sum + term
            term = dot(grads, down_ref[b])
            down_sum = term if down_sum is None else down_sum + term
    out_ref[:, :wide] = pair_sum
    out_ref[:, wide:] = down_sum


def lanes_of(owner, owned):
    return pl.ds(pl.multiple_of(owner * owned, 128), owned)


def far_kernel(groups, rows_ref, grads_ref, partial_ref, *refs):
    far = range(2, groups, 2)
    weights_in, (out_ref, pair_ref, down_ref, sems) = refs[: len(far)], refs[len(far) :]
    copies = [
        place(source.at[0], pair_ref.at[at], down_ref.at[at], sems, at)
        for at, source in enumerate(weights_in)
    ]
    for some in copies:
        for copy in some:
            copy.start()
    me = lax.axis_index("dp")
    owned, wide = pair_ref.shape[1:]
    pair_sum, down_sum = partial_ref[:, :wide], partial_ref[:, wide:]
    for at, b in enumerate(far):
        for copy in copies[at]:
            copy.wait()
        lanes = lanes_of(me ^ b, owned)
        pair_sum = pair_sum + dot(rows_ref[:, lanes], pair_ref[at])
        down_sum = down_sum + dot(grads_ref[:, lanes], down_ref[at])
    out_ref[:, :wide] = pair_sum
    out_ref[:, wide:] = down_sum


def back_kernel(groups, rows_ref, grads_ref, partial_ref, near_ref, far_ref, *refs):
    last_refs, (acts_ref, out_ref, back_ref) = refs[:-3], refs[-3:]
    me = lax.axis_index("dp")
    model_width = grads_ref.shape[1]
    owned = model_width // groups
    chunks = model_width // WIDE
    hidden_units = partial_ref.shape[1] // 3
    wide = 2 * hidden_units

    def lanes(b):
        return lanes_of(me ^ b, owned)

    gate_act = partial_ref[:, :hidden_units]
    up_act = partial_ref[:, hidden_units:wide]
    grad_hidden = partial_ref[:, wide:]
    for at, ref in enumerate(last_refs):
        here = lanes(2 * at + 3)
        gate_act = gate_act + dot(rows_ref[:, here], ref[0, 0])
        up_act = up_act + dot(rows_ref[:, here], ref[0, 1])
        grad_hidden = grad_hidden + dot(grads_ref[:, here], ref[0, 2])
    logistic = jax.nn.sigmoid(gate_act)
    swish_out = gate_act * logistic
    hidden = (swish_out * up_act).astype(BF16)
    grad_up = (grad_hidden * swish_out).astype(BF16)
    grad_gate = (grad_hidden * up_act * logistic * (1.0 + gate_act * (1.0 - logistic))).astype(BF16)
    acts = jnp.concatenate([grad_gate, grad_up], axis=1)
    acts_ref[:, :wide] = acts
    acts_ref[:, wide:] = hidden
    for b in range(groups):
        if b < 2:
            term = dot_nt(acts, near_ref[b])
        elif b % 2 == 0:
            term = dot_nt(acts, far_ref[b // 2 - 1])
        else:
            ref = last_refs[b // 2 - 1]
            term = dot_nt(grad_gate, ref[0, 0]) + dot_nt(grad_up, ref[0, 1])
        back_ref[:, lanes(b)] = term
    tall = JOIN * SLOTS
    joined = grads_ref.shape[0] // tall
    lines = jnp.concatenate(
        [
            jnp.concatenate(
                [
                    back_ref[q * tall : (q + 1) * tall, c * WIDE : (c + 1) * WIDE]
                    for c in range(chunks)
                ],
                axis=0,
            )
            for q in range(joined)
        ],
        axis=1,
    ).astype(BF16)
    blocks = dot(sort_matrix(1, chunks, True), lines)
    height = piece_rows(chunks)
    for q in range(joined):
        for j in range(JOIN):
            part = blocks[j * height : (j + 1) * height, q * WIDE : (q + 1) * WIDE]
            out_ref[q * JOIN + j] = part.astype(BF16)


def combine_kernel(returned_ref, table_ref, out_ref):
    token_rows, model_width = out_ref.shape
    window, height, _ = returned_ref.shape
    lines = returned_ref[...].astype(F32).reshape(window * height, WIDE).astype(BF16)
    result = dot(table_ref[...], lines).astype(BF16)
    for c in range(model_width // WIDE):
        out_ref[:, c * WIDE : (c + 1) * WIDE] = result[c * token_rows : (c + 1) * token_rows]


def grads_kernel(groups, *refs):
    slices_refs, acts_refs, out_ref = refs[:groups], refs[groups : 2 * groups], refs[-1]
    hidden_units = out_ref.shape[3]
    rows_here = acts_refs[0].shape[0]
    step = max(1, min(groups, 640 // rows_here))
    for at in range(3):
        lanes = slice(at * hidden_units, (at + 1) * hidden_units)
        kind = 0 if at < 2 else 1
        places = [kind + 2 if b == 0 else kind for b in range(groups)]
        total = None
        for first in range(0, groups, step):
            some = range(first, first + step)
            rows = jnp.concatenate([slices_refs[b][places[b]] for b in some], axis=0)
            acts = jnp.concatenate([acts_refs[b][:, lanes] for b in some], axis=0)
            term = dot_tn(rows, acts)
            total = term if total is None else total + term
        out_ref[0, at] = total


def on_device(tokens, out_grad, expert_ids, gates, expert_weights):
    window = lax.axis_size("expert")
    groups = lax.axis_size("dp")
    token_rows, model_width = tokens.shape
    hidden_units = expert_weights.shape[3]
    owned = model_width // groups
    chunks = model_width // WIDE
    padded = piece_rows(chunks)
    rows_here = window * SLOTS
    wide = 2 * hidden_units
    anywhere = pl.BlockSpec(memory_space=pl.ANY)

    far = list(range(2, groups, 2))
    token = pl.pallas_call(
        token_kernel,
        out_shape=shape(8, 128, kind=F32),
        compiler_params=params(),
        cost_estimate=cost(10**11, 10**8),
    )()
    arriving = [swap(expert_weights, b) for b in far]
    near = swap(expert_weights, 1)

    ids_t, gates_t = expert_ids.T, gates.T
    sent, code = pl.pallas_call(
        pack_kernel,
        out_shape=(
            shape(window, 2 * padded, WIDE),
            shape(window, token_rows, kind=F32),
        ),
        compiler_params=params(tokens, out_grad),
    )(ids_t, gates_t, tokens, out_grad, token)

    got = lax.all_to_all(sent, "expert", split_axis=0, concat_axis=0, tiled=True)
    table = pl.pallas_call(
        lambda *refs: table_kernel(chunks, *refs),
        out_shape=shape(chunks * token_rows, window * padded),
        compiler_params=params(),
        cost_estimate=cost(10**11, 10**8),
    )(code)

    outs = pl.pallas_call(
        lambda *refs: partial_kernel(groups, *refs),
        in_specs=[pl.BlockSpec()] + [anywhere] * 2,
        out_shape=[
            shape(rows_here, 3 * hidden_units, kind=F32),
            shape(rows_here, model_width),
            shape(rows_here, model_width),
            shape(2, owned, wide),
            shape(8, 128, kind=F32),
        ]
        + [shape(4, rows_here, owned)]
        + [shape(2, rows_here, owned)] * (groups - 2),
        scratch_shapes=[
            pltpu.VMEM((2, owned, hidden_units), BF16),
            pltpu.SemaphoreType.DMA((2, 3)),
        ],
        compiler_params=params(got, expert_weights, expert_weights),
    )(got, expert_weights, near)
    partial, rows, grads, near_pairs, token = outs[:5]
    slices = list(outs[5:])
    slices = slices[:1] + [swap(slices[b - 1], b) for b in range(1, groups)]

    arrived = pl.pallas_call(
        keep_kernel,
        in_specs=[anywhere] * (len(far) + 1),
        out_specs=[anywhere] * len(far),
        out_shape=[shape(*expert_weights.shape)] * len(far),
        input_output_aliases={at + 1: at for at in range(len(far))},
        compiler_params=params(),
        cost_estimate=cost(10**11, 10**8),
    )(token, *arriving)
    last = [swap(value, 1) for value in arrived]
    partial, far_pairs = pl.pallas_call(
        lambda *refs: far_kernel(groups, *refs),
        in_specs=[pl.BlockSpec()] * 3 + [anywhere] * len(far),
        out_shape=(shape(rows_here, 3 * hidden_units, kind=F32), shape(len(far), owned, wide)),
        scratch_shapes=[
            pltpu.VMEM((len(far), owned, hidden_units), BF16),
            pltpu.SemaphoreType.DMA((len(far), 3)),
        ],
        compiler_params=params(rows, grads, *arrived, *arrived),
    )(rows, grads, partial, *arrived)

    acts, back = pl.pallas_call(
        lambda *refs: back_kernel(groups, *refs),
        out_shape=(shape(rows_here, 3 * hidden_units), shape(window, padded, WIDE)),
        scratch_shapes=[pltpu.VMEM((rows_here, model_width), F32)],
        compiler_params=params(rows, grads, partial, near_pairs, far_pairs, *last),
        cost_estimate=cost(10**6, 10**5),
    )(rows, grads, partial, near_pairs, far_pairs, *last)
    returned = lax.all_to_all(back, "expert", split_axis=0, concat_axis=0, tiled=True)

    every = slices + [acts] + [swap(acts, b) for b in range(1, groups)]
    weight_grads = pl.pallas_call(
        lambda *refs: grads_kernel(groups, *refs),
        out_shape=shape(1, 3, owned, hidden_units, kind=F32),
        compiler_params=params(*every, expert_weights, expert_weights),
        cost_estimate=cost(6 * groups * rows_here * owned * hidden_units, 12 * owned * hidden_units),
    )(*every)

    token_grads = pl.pallas_call(
        combine_kernel,
        out_shape=shape(token_rows, model_width),
        compiler_params=params(table, back, tokens),
    )(returned, table)
    return (token_grads, weight_grads)


def solution(mesh):
    lines = P(("dp", "expert"), None)
    slabs = P("expert", None, "dp", None)
    return jax.shard_map(
        on_device,
        mesh=mesh,
        in_specs=(lines, lines, lines, lines, slabs),
        out_specs=(lines, slabs),
        check_vma=False,
    )
```

```python
import jax
import jax.numpy as jnp
from jax import lax
from jax.experimental import pallas as pl
from jax.experimental.pallas import tpu as pltpu
from jax.sharding import PartitionSpec as P

SLOTS = 10
WIDE = 512
JOIN = 4
F32 = jnp.float32
BF16 = jnp.bfloat16


def dot(first_op, second_op):
    return jnp.dot(first_op, second_op, preferred_element_type=F32)


def dot_tn(first_op, second_op):
    return lax.dot_general(first_op, second_op, (((0,), (0,)), ((), ())), preferred_element_type=F32)


def dot_nt(first_op, second_op):
    return lax.dot_general(first_op, second_op, (((1,), (1,)), ((), ())), preferred_element_type=F32)


def swap(value, bits):
    return lax.ppermute(value, "dp", [(i, i ^ bits) for i in range(lax.axis_size("dp"))])


def piece_rows(chunks):
    return -(-chunks * SLOTS // 8) * 8


def params(*arrays):
    moved = sum(a.size * a.dtype.itemsize for a in arrays)
    return pltpu.CompilerParams(vmem_limit_bytes=min(56 * 2**20, 12 * 2**20 + 3 * moved))


def cost(flops, moved):
    return pl.CostEstimate(flops=flops, bytes_accessed=moved, transcendentals=0)


def ends_first(size):
    return [at // 2 if at % 2 == 0 else size - 1 - at // 2 for at in range(size)]


def trade(blocks):
    order = ends_first(lax.axis_size("expert"))
    return lax.all_to_all(
        blocks, "expert", split_axis=0, concat_axis=0, axis_index_groups=[order], tiled=True
    )


def shape(*extent, kind=BF16):
    return jax.ShapeDtypeStruct(extent, kind)


def lower(value, by):
    return jnp.floor((value + 0.5) * (1.0 / by))


def sort_matrix(parts, chunks, transposed):
    padded = piece_rows(chunks)
    wide, tall = JOIN * parts * padded, parts * chunks * JOIN * SLOTS
    extent, axis = ((wide, tall), 0) if transposed else ((tall, wide), 1)
    line = (wide, 1) if transposed else (1, wide)
    place = lax.broadcasted_iota(jnp.int32, line, axis).astype(F32)
    block = lower(place, padded)
    inside = place - block * padded
    source = lower(block, parts)
    part = block - source * parts
    chunk = lower(inside, SLOTS)
    slot = inside - chunk * SLOTS
    target = ((part * chunks + chunk) * JOIN + source) * SLOTS + slot
    target = jnp.where(chunk < chunks, target, -1.0)
    spots = lax.broadcasted_iota(jnp.int32, extent, 1 - axis).astype(F32)
    return jnp.where(spots == target, 1.0, 0.0).astype(BF16)


def table_of(code, values, chunks, padded):
    window, token_rows = code.shape
    spots = lax.broadcasted_iota(jnp.int32, (padded, chunks * token_rows), 0).astype(F32)
    tables = []
    for expert in range(window):
        own = code[expert : expert + 1]
        hit = spots == jnp.concatenate([own + float(SLOTS * c) for c in range(chunks)], axis=1)
        row = []
        for value in values:
            if value is None:
                row.append(jnp.where(hit, 1.0, 0.0))
            else:
                gate = jnp.concatenate([value[expert : expert + 1]] * chunks, axis=1)
                row.append(jnp.where(hit, gate, 0.0))
        tables.append(row)
    return [jnp.concatenate([t[i] for t in tables], axis=0) for i in range(len(values))]


def token_kernel(token_ref):
    token_ref[...] = jnp.zeros_like(token_ref)


def pack_kernel(ids_ref, gates_ref, tokens_ref, grads_ref, _, sent_ref, code_ref):
    token_rows, model_width = tokens_ref.shape
    window = code_ref.shape[0]
    chunks = model_width // WIDE
    padded = piece_rows(chunks)
    above = lax.broadcasted_iota(jnp.int32, (token_rows, token_rows), 0)
    along = lax.broadcasted_iota(jnp.int32, (token_rows, token_rows), 1)
    earlier = jnp.where(above < along, 1.0, 0.0).astype(BF16)
    ids = ids_ref[...]
    gates = gates_ref[...].astype(F32)
    members, chosen = [], []
    for expert in ends_first(window):
        hit = ids == expert
        members.append(jnp.sum(jnp.where(hit, 1.0, 0.0), axis=0, keepdims=True))
        chosen.append(jnp.sum(jnp.where(hit, gates, 0.0), axis=0, keepdims=True))
    members = jnp.concatenate(members, axis=0)
    chosen = jnp.concatenate(chosen, axis=0)
    code = jnp.where(members > 0.0, dot(members.astype(BF16), earlier), -1e6)
    code_ref[...] = code
    table, gated = table_of(code, [None, chosen], chunks, padded)

    def columns(ref):
        return jnp.concatenate([ref[:, c * WIDE : (c + 1) * WIDE] for c in range(chunks)], axis=0)

    rows = dot(table.astype(BF16), columns(tokens_ref))
    grads = dot(gated.astype(BF16), columns(grads_ref))
    for expert in range(window):
        lines = slice(expert * padded, (expert + 1) * padded)
        sent_ref[expert] = jnp.concatenate([rows[lines], grads[lines]], axis=0).astype(BF16)


def table_kernel(chunks, code_ref, table_ref):
    (table,) = table_of(code_ref[...], [None], chunks, piece_rows(chunks))
    table_ref[...] = table.T.astype(BF16)


def keep_kernel(*refs):
    pass


def place(source, pair_ref, down_ref, sems, at):
    hidden_units = down_ref.shape[1]
    moves = [
        (source.at[0], pair_ref.at[:, pl.ds(0, hidden_units)]),
        (source.at[1], pair_ref.at[:, pl.ds(hidden_units, hidden_units)]),
        (source.at[2], down_ref),
    ]
    return [
        pltpu.make_async_copy(start, end, sems.at[at, which]) for which, (start, end) in enumerate(moves)
    ]


def partial_kernel(groups, got_ref, own_in, near_in, *refs):
    (out_ref, rows_ref, grads_ref, pair_ref, token_ref), refs = refs[:5], refs[5:]
    slices_refs, (down_ref, sems) = refs[: groups - 1], refs[groups - 1 :]
    copies = [
        copy
        for b, source in enumerate((own_in.at[0], near_in.at[0]))
        for copy in place(source, pair_ref.at[b], down_ref.at[b], sems, b)
    ]
    for copy in copies:
        copy.start()
    token_ref[...] = jnp.zeros_like(token_ref)
    sources, height, _ = got_ref.shape
    model_width = rows_ref.shape[1]
    chunks = model_width // WIDE
    owned = model_width // groups
    joined = sources // JOIN
    tall = JOIN * SLOTS
    blocks = jnp.concatenate(
        [got_ref[q * JOIN : (q + 1) * JOIN].reshape(JOIN * height, WIDE) for q in range(joined)],
        axis=1,
    )
    lines = dot(sort_matrix(2, chunks, False), blocks)

    def gathered(part):
        return jnp.concatenate(
            [
                jnp.concatenate(
                    [
                        lines[
                            (part * chunks + c) * tall : (part * chunks + c + 1) * tall,
                            q * WIDE : (q + 1) * WIDE,
                        ]
                        for c in range(chunks)
                    ],
                    axis=1,
                )
                for q in range(joined)
            ],
            axis=0,
        ).astype(BF16)

    rows_ref[...] = gathered(0)
    grads_ref[...] = gathered(1)
    me = lax.axis_index("dp")
    wide = pair_ref.shape[2]
    for copy in copies:
        copy.wait()
    pair_sum, down_sum = None, None
    for b in range(groups):
        lanes = pl.ds(pl.multiple_of((me ^ b) * owned, 128), owned)
        rows, grads = rows_ref[:, lanes], grads_ref[:, lanes]
        target, first = (slices_refs[0], 2) if b == 0 else (slices_refs[b - 1], 0)
        target[first] = rows
        target[first + 1] = grads
        if b < 2:
            term = dot(rows, pair_ref[b])
            pair_sum = term if pair_sum is None else pair_sum + term
            term = dot(grads, down_ref[b])
            down_sum = term if down_sum is None else down_sum + term
    out_ref[:, :wide] = pair_sum
    out_ref[:, wide:] = down_sum


def lanes_of(owner, owned):
    return pl.ds(pl.multiple_of(owner * owned, 128), owned)


def far_kernel(groups, rows_ref, grads_ref, partial_ref, *refs):
    far = range(2, groups, 2)
    weights_in, (out_ref, pair_ref, down_ref, sems) = refs[: len(far)], refs[len(far) :]
    copies = [
        place(source.at[0], pair_ref.at[at], down_ref.at[at], sems, at)
        for at, source in enumerate(weights_in)
    ]
    for some in copies:
        for copy in some:
            copy.start()
    me = lax.axis_index("dp")
    owned, wide = pair_ref.shape[1:]
    pair_sum, down_sum = partial_ref[:, :wide], partial_ref[:, wide:]
    for at, b in enumerate(far):
        for copy in copies[at]:
            copy.wait()
        lanes = lanes_of(me ^ b, owned)
        pair_sum = pair_sum + dot(rows_ref[:, lanes], pair_ref[at])
        down_sum = down_sum + dot(grads_ref[:, lanes], down_ref[at])
    out_ref[:, :wide] = pair_sum
    out_ref[:, wide:] = down_sum


def back_kernel(groups, rows_ref, grads_ref, partial_ref, near_ref, far_ref, *refs):
    last_refs, (acts_ref, out_ref, back_ref) = refs[:-3], refs[-3:]
    me = lax.axis_index("dp")
    model_width = grads_ref.shape[1]
    owned = model_width // groups
    chunks = model_width // WIDE
    hidden_units = partial_ref.shape[1] // 3
    wide = 2 * hidden_units

    def lanes(b):
        return lanes_of(me ^ b, owned)

    gate_act = partial_ref[:, :hidden_units]
    up_act = partial_ref[:, hidden_units:wide]
    grad_hidden = partial_ref[:, wide:]
    for at, ref in enumerate(last_refs):
        here = lanes(2 * at + 3)
        gate_act = gate_act + dot(rows_ref[:, here], ref[0, 0])
        up_act = up_act + dot(rows_ref[:, here], ref[0, 1])
        grad_hidden = grad_hidden + dot(grads_ref[:, here], ref[0, 2])
    logistic = jax.nn.sigmoid(gate_act)
    swish_out = gate_act * logistic
    hidden = (swish_out * up_act).astype(BF16)
    grad_up = (grad_hidden * swish_out).astype(BF16)
    grad_gate = (grad_hidden * up_act * logistic * (1.0 + gate_act * (1.0 - logistic))).astype(BF16)
    acts = jnp.concatenate([grad_gate, grad_up], axis=1)
    acts_ref[:, :wide] = acts
    acts_ref[:, wide:] = hidden
    for b in range(groups):
        if b < 2:
            term = dot_nt(acts, near_ref[b])
        elif b % 2 == 0:
            term = dot_nt(acts, far_ref[b // 2 - 1])
        else:
            ref = last_refs[b // 2 - 1]
            term = dot_nt(grad_gate, ref[0, 0]) + dot_nt(grad_up, ref[0, 1])
        back_ref[:, lanes(b)] = term
    tall = JOIN * SLOTS
    joined = grads_ref.shape[0] // tall
    lines = jnp.concatenate(
        [
            jnp.concatenate(
                [
                    back_ref[q * tall : (q + 1) * tall, c * WIDE : (c + 1) * WIDE]
                    for c in range(chunks)
                ],
                axis=0,
            )
            for q in range(joined)
        ],
        axis=1,
    ).astype(BF16)
    blocks = dot(sort_matrix(1, chunks, True), lines)
    height = piece_rows(chunks)
    for q in range(joined):
        for j in range(JOIN):
            part = blocks[j * height : (j + 1) * height, q * WIDE : (q + 1) * WIDE]
            out_ref[q * JOIN + j] = part.astype(BF16)


def combine_kernel(returned_ref, table_ref, out_ref):
    token_rows, model_width = out_ref.shape
    window, height, _ = returned_ref.shape
    lines = returned_ref[...].astype(F32).reshape(window * height, WIDE).astype(BF16)
    result = dot(table_ref[...], lines).astype(BF16)
    for c in range(model_width // WIDE):
        out_ref[:, c * WIDE : (c + 1) * WIDE] = result[c * token_rows : (c + 1) * token_rows]


def grads_kernel(groups, *refs):
    slices_refs, acts_refs, out_ref = refs[:groups], refs[groups : 2 * groups], refs[-1]
    hidden_units = out_ref.shape[3]
    rows_here = acts_refs[0].shape[0]
    step = max(1, min(groups, 640 // rows_here))
    for at in range(3):
        lanes = slice(at * hidden_units, (at + 1) * hidden_units)
        kind = 0 if at < 2 else 1
        places = [kind + 2 if b == 0 else kind for b in range(groups)]
        total = None
        for first in range(0, groups, step):
            some = range(first, first + step)
            rows = jnp.concatenate([slices_refs[b][places[b]] for b in some], axis=0)
            acts = jnp.concatenate([acts_refs[b][:, lanes] for b in some], axis=0)
            term = dot_tn(rows, acts)
            total = term if total is None else total + term
        out_ref[0, at] = total


def on_device(tokens, out_grad, expert_ids, gates, expert_weights):
    window = lax.axis_size("expert")
    groups = lax.axis_size("dp")
    token_rows, model_width = tokens.shape
    hidden_units = expert_weights.shape[3]
    owned = model_width // groups
    chunks = model_width // WIDE
    padded = piece_rows(chunks)
    rows_here = window * SLOTS
    wide = 2 * hidden_units
    anywhere = pl.BlockSpec(memory_space=pl.ANY)

    far = list(range(2, groups, 2))
    token = pl.pallas_call(
        token_kernel,
        out_shape=shape(8, 128, kind=F32),
        compiler_params=params(),
        cost_estimate=cost(10**11, 10**8),
    )()
    arriving = [swap(expert_weights, b) for b in far]
    near = swap(expert_weights, 1)

    ids_t, gates_t = expert_ids.T, gates.T
    sent, code = pl.pallas_call(
        pack_kernel,
        out_shape=(
            shape(window, 2 * padded, WIDE),
            shape(window, token_rows, kind=F32),
        ),
        compiler_params=params(tokens, out_grad),
    )(ids_t, gates_t, tokens, out_grad, token)

    got = trade(sent)
    table = pl.pallas_call(
        lambda *refs: table_kernel(chunks, *refs),
        out_shape=shape(chunks * token_rows, window * padded),
        compiler_params=params(),
        cost_estimate=cost(10**11, 10**8),
    )(code)

    outs = pl.pallas_call(
        lambda *refs: partial_kernel(groups, *refs),
        in_specs=[pl.BlockSpec()] + [anywhere] * 2,
        out_shape=[
            shape(rows_here, 3 * hidden_units, kind=F32),
            shape(rows_here, model_width),
            shape(rows_here, model_width),
            shape(2, owned, wide),
            shape(8, 128, kind=F32),
        ]
        + [shape(4, rows_here, owned)]
        + [shape(2, rows_here, owned)] * (groups - 2),
        scratch_shapes=[
            pltpu.VMEM((2, owned, hidden_units), BF16),
            pltpu.SemaphoreType.DMA((2, 3)),
        ],
        compiler_params=params(got, expert_weights, expert_weights),
    )(got, expert_weights, near)
    partial, rows, grads, near_pairs, token = outs[:5]
    slices = list(outs[5:])
    slices = slices[:1] + [swap(slices[b - 1], b) for b in range(1, groups)]

    arrived = pl.pallas_call(
        keep_kernel,
        in_specs=[anywhere] * (len(far) + 1),
        out_specs=[anywhere] * len(far),
        out_shape=[shape(*expert_weights.shape)] * len(far),
        input_output_aliases={at + 1: at for at in range(len(far))},
        compiler_params=params(),
        cost_estimate=cost(10**11, 10**8),
    )(token, *arriving)
    last = [swap(value, 1) for value in arrived]
    partial, far_pairs = pl.pallas_call(
        lambda *refs: far_kernel(groups, *refs),
        in_specs=[pl.BlockSpec()] * 3 + [anywhere] * len(far),
        out_shape=(shape(rows_here, 3 * hidden_units, kind=F32), shape(len(far), owned, wide)),
        scratch_shapes=[
            pltpu.VMEM((len(far), owned, hidden_units), BF16),
            pltpu.SemaphoreType.DMA((len(far), 3)),
        ],
        compiler_params=params(rows, grads, *arrived, *arrived),
    )(rows, grads, partial, *arrived)

    acts, back = pl.pallas_call(
        lambda *refs: back_kernel(groups, *refs),
        out_shape=(shape(rows_here, 3 * hidden_units), shape(window, padded, WIDE)),
        scratch_shapes=[pltpu.VMEM((rows_here, model_width), F32)],
        compiler_params=params(rows, grads, partial, near_pairs, far_pairs, *last),
        cost_estimate=cost(10**6, 10**5),
    )(rows, grads, partial, near_pairs, far_pairs, *last)
    returned = trade(back)

    every = slices + [acts] + [swap(acts, b) for b in range(1, groups)]
    weight_grads = pl.pallas_call(
        lambda *refs: grads_kernel(groups, *refs),
        out_shape=shape(1, 3, owned, hidden_units, kind=F32),
        compiler_params=params(*every, expert_weights, expert_weights),
        cost_estimate=cost(6 * groups * rows_here * owned * hidden_units, 12 * owned * hidden_units),
    )(*every)

    token_grads = pl.pallas_call(
        combine_kernel,
        out_shape=shape(token_rows, model_width),
        compiler_params=params(table, back, tokens),
    )(returned, table)
    return (token_grads, weight_grads)


def solution(mesh):
    lines = P(("dp", "expert"), None)
    slabs = P("expert", None, "dp", None)
    return jax.shard_map(
        on_device,
        mesh=mesh,
        in_specs=(lines, lines, lines, lines, slabs),
        out_specs=(lines, slabs),
        check_vma=False,
    )
```

```python
import jax
import jax.numpy as jnp
from jax import lax
from jax.experimental import pallas as pl
from jax.experimental.pallas import tpu as pltpu
from jax.sharding import PartitionSpec as P

SLOTS = 10
WIDE = 512
JOIN = 4
F32 = jnp.float32
BF16 = jnp.bfloat16


def dot(first_op, second_op):
    return jnp.dot(first_op, second_op, preferred_element_type=F32)


def dot_tn(first_op, second_op):
    return lax.dot_general(first_op, second_op, (((0,), (0,)), ((), ())), preferred_element_type=F32)


def dot_nt(first_op, second_op):
    return lax.dot_general(first_op, second_op, (((1,), (1,)), ((), ())), preferred_element_type=F32)


def swap(value, bits):
    return lax.ppermute(value, "dp", [(i, i ^ bits) for i in range(lax.axis_size("dp"))])


def piece_rows(chunks):
    return -(-chunks * SLOTS // 8) * 8


def params(*arrays):
    moved = sum(a.size * a.dtype.itemsize for a in arrays)
    return pltpu.CompilerParams(vmem_limit_bytes=min(56 * 2**20, 6 * 2**20 + 3 * moved // 2))


def cost(flops, moved):
    return pl.CostEstimate(flops=flops, bytes_accessed=moved, transcendentals=0)


def shape(*extent, kind=BF16):
    return jax.ShapeDtypeStruct(extent, kind)


def lower(value, by):
    return jnp.floor((value + 0.5) * (1.0 / by))


def sort_matrix(parts, chunks, transposed):
    padded = piece_rows(chunks)
    wide, tall = JOIN * parts * padded, parts * chunks * JOIN * SLOTS
    extent, axis = ((wide, tall), 0) if transposed else ((tall, wide), 1)
    line = (wide, 1) if transposed else (1, wide)
    place = lax.broadcasted_iota(jnp.int32, line, axis).astype(F32)
    block = lower(place, padded)
    inside = place - block * padded
    source = lower(block, parts)
    part = block - source * parts
    chunk = lower(inside, SLOTS)
    slot = inside - chunk * SLOTS
    target = ((part * chunks + chunk) * JOIN + source) * SLOTS + slot
    target = jnp.where(chunk < chunks, target, -1.0)
    spots = lax.broadcasted_iota(jnp.int32, extent, 1 - axis).astype(F32)
    return jnp.where(spots == target, 1.0, 0.0).astype(BF16)


def table_of(code, values, chunks, padded):
    window, token_rows = code.shape
    spots = lax.broadcasted_iota(jnp.int32, (padded, chunks * token_rows), 0).astype(F32)
    tables = []
    for expert in range(window):
        own = code[expert : expert + 1]
        hit = spots == jnp.concatenate([own + float(SLOTS * c) for c in range(chunks)], axis=1)
        row = []
        for value in values:
            if value is None:
                row.append(jnp.where(hit, 1.0, 0.0))
            else:
                gate = jnp.concatenate([value[expert : expert + 1]] * chunks, axis=1)
                row.append(jnp.where(hit, gate, 0.0))
        tables.append(row)
    return [jnp.concatenate([t[i] for t in tables], axis=0) for i in range(len(values))]


def token_kernel(token_ref):
    token_ref[...] = jnp.zeros_like(token_ref)


def pack_kernel(ids_ref, gates_ref, tokens_ref, grads_ref, _, sent_ref, code_ref):
    token_rows, model_width = tokens_ref.shape
    window = code_ref.shape[0]
    chunks = model_width // WIDE
    padded = piece_rows(chunks)
    above = lax.broadcasted_iota(jnp.int32, (token_rows, token_rows), 0)
    along = lax.broadcasted_iota(jnp.int32, (token_rows, token_rows), 1)
    earlier = jnp.where(above < along, 1.0, 0.0).astype(BF16)
    ids = ids_ref[...]
    gates = gates_ref[...].astype(F32)
    members, chosen = [], []
    for expert in range(window):
        hit = ids == expert
        members.append(jnp.sum(jnp.where(hit, 1.0, 0.0), axis=0, keepdims=True))
        chosen.append(jnp.sum(jnp.where(hit, gates, 0.0), axis=0, keepdims=True))
    members = jnp.concatenate(members, axis=0)
    chosen = jnp.concatenate(chosen, axis=0)
    code = jnp.where(members > 0.0, dot(members.astype(BF16), earlier), -1e6)
    code_ref[...] = code
    table, gated = table_of(code, [None, chosen], chunks, padded)

    def columns(ref):
        return jnp.concatenate([ref[:, c * WIDE : (c + 1) * WIDE] for c in range(chunks)], axis=0)

    rows = dot(table.astype(BF16), columns(tokens_ref))
    grads = dot(gated.astype(BF16), columns(grads_ref))
    for expert in range(window):
        lines = slice(expert * padded, (expert + 1) * padded)
        sent_ref[expert] = jnp.concatenate([rows[lines], grads[lines]], axis=0).astype(BF16)


def table_kernel(chunks, code_ref, table_ref):
    (table,) = table_of(code_ref[...], [None], chunks, piece_rows(chunks))
    table_ref[...] = table.T.astype(BF16)


def keep_kernel(*refs):
    pass


def place(source, pair_ref, down_ref, sems, at):
    hidden_units = down_ref.shape[1]
    moves = [
        (source.at[0], pair_ref.at[:, pl.ds(0, hidden_units)]),
        (source.at[1], pair_ref.at[:, pl.ds(hidden_units, hidden_units)]),
        (source.at[2], down_ref),
    ]
    return [
        pltpu.make_async_copy(start, end, sems.at[at, which]) for which, (start, end) in enumerate(moves)
    ]


def partial_kernel(groups, got_ref, own_in, near_in, *refs):
    (out_ref, rows_ref, grads_ref, pair_ref, token_ref), refs = refs[:5], refs[5:]
    slices_refs, (down_ref, sems) = refs[: groups - 1], refs[groups - 1 :]
    copies = [
        copy
        for b, source in enumerate((own_in.at[0], near_in.at[0]))
        for copy in place(source, pair_ref.at[b], down_ref.at[b], sems, b)
    ]
    for copy in copies:
        copy.start()
    token_ref[...] = jnp.zeros_like(token_ref)
    sources, height, _ = got_ref.shape
    model_width = rows_ref.shape[1]
    chunks = model_width // WIDE
    owned = model_width // groups
    joined = sources // JOIN
    tall = JOIN * SLOTS
    blocks = jnp.concatenate(
        [got_ref[q * JOIN : (q + 1) * JOIN].reshape(JOIN * height, WIDE) for q in range(joined)],
        axis=1,
    )
    lines = dot(sort_matrix(2, chunks, False), blocks)

    def gathered(part):
        return jnp.concatenate(
            [
                jnp.concatenate(
                    [
                        lines[
                            (part * chunks + c) * tall : (part * chunks + c + 1) * tall,
                            q * WIDE : (q + 1) * WIDE,
                        ]
                        for c in range(chunks)
                    ],
                    axis=1,
                )
                for q in range(joined)
            ],
            axis=0,
        ).astype(BF16)

    rows_ref[...] = gathered(0)
    grads_ref[...] = gathered(1)
    me = lax.axis_index("dp")
    wide = pair_ref.shape[2]
    for copy in copies:
        copy.wait()
    pair_sum, down_sum = None, None
    for b in range(groups):
        lanes = pl.ds(pl.multiple_of((me ^ b) * owned, 128), owned)
        rows, grads = rows_ref[:, lanes], grads_ref[:, lanes]
        target, first = (slices_refs[0], 2) if b == 0 else (slices_refs[b - 1], 0)
        target[first] = rows
        target[first + 1] = grads
        if b < 2:
            term = dot(rows, pair_ref[b])
            pair_sum = term if pair_sum is None else pair_sum + term
            term = dot(grads, down_ref[b])
            down_sum = term if down_sum is None else down_sum + term
    out_ref[:, :wide] = pair_sum
    out_ref[:, wide:] = down_sum


def lanes_of(owner, owned):
    return pl.ds(pl.multiple_of(owner * owned, 128), owned)


def far_kernel(groups, rows_ref, grads_ref, partial_ref, *refs):
    far = range(2, groups, 2)
    weights_in, (out_ref, pair_ref, down_ref, sems) = refs[: len(far)], refs[len(far) :]
    copies = [
        place(source.at[0], pair_ref.at[at], down_ref.at[at], sems, at)
        for at, source in enumerate(weights_in)
    ]
    for some in copies:
        for copy in some:
            copy.start()
    me = lax.axis_index("dp")
    owned, wide = pair_ref.shape[1:]
    pair_sum, down_sum = partial_ref[:, :wide], partial_ref[:, wide:]
    for at, b in enumerate(far):
        for copy in copies[at]:
            copy.wait()
        lanes = lanes_of(me ^ b, owned)
        pair_sum = pair_sum + dot(rows_ref[:, lanes], pair_ref[at])
        down_sum = down_sum + dot(grads_ref[:, lanes], down_ref[at])
    out_ref[:, :wide] = pair_sum
    out_ref[:, wide:] = down_sum


def back_kernel(groups, rows_ref, grads_ref, partial_ref, near_ref, far_ref, *refs):
    last_refs, (acts_ref, out_ref, back_ref) = refs[:-3], refs[-3:]
    me = lax.axis_index("dp")
    model_width = grads_ref.shape[1]
    owned = model_width // groups
    chunks = model_width // WIDE
    hidden_units = partial_ref.shape[1] // 3
    wide = 2 * hidden_units

    def lanes(b):
        return lanes_of(me ^ b, owned)

    gate_act = partial_ref[:, :hidden_units]
    up_act = partial_ref[:, hidden_units:wide]
    grad_hidden = partial_ref[:, wide:]
    for at, ref in enumerate(last_refs):
        here = lanes(2 * at + 3)
        gate_act = gate_act + dot(rows_ref[:, here], ref[0, 0])
        up_act = up_act + dot(rows_ref[:, here], ref[0, 1])
        grad_hidden = grad_hidden + dot(grads_ref[:, here], ref[0, 2])
    logistic = jax.nn.sigmoid(gate_act)
    swish_out = gate_act * logistic
    hidden = (swish_out * up_act).astype(BF16)
    grad_up = (grad_hidden * swish_out).astype(BF16)
    grad_gate = (grad_hidden * up_act * logistic * (1.0 + gate_act * (1.0 - logistic))).astype(BF16)
    acts = jnp.concatenate([grad_gate, grad_up], axis=1)
    acts_ref[:, :wide] = acts
    acts_ref[:, wide:] = hidden
    for b in range(groups):
        if b < 2:
            term = dot_nt(acts, near_ref[b])
        elif b % 2 == 0:
            term = dot_nt(acts, far_ref[b // 2 - 1])
        else:
            ref = last_refs[b // 2 - 1]
            term = dot_nt(grad_gate, ref[0, 0]) + dot_nt(grad_up, ref[0, 1])
        back_ref[:, lanes(b)] = term
    tall = JOIN * SLOTS
    joined = grads_ref.shape[0] // tall
    lines = jnp.concatenate(
        [
            jnp.concatenate(
                [
                    back_ref[q * tall : (q + 1) * tall, c * WIDE : (c + 1) * WIDE]
                    for c in range(chunks)
                ],
                axis=0,
            )
            for q in range(joined)
        ],
        axis=1,
    ).astype(BF16)
    blocks = dot(sort_matrix(1, chunks, True), lines)
    height = piece_rows(chunks)
    for q in range(joined):
        for j in range(JOIN):
            part = blocks[j * height : (j + 1) * height, q * WIDE : (q + 1) * WIDE]
            out_ref[q * JOIN + j] = part.astype(BF16)


def combine_kernel(returned_ref, table_ref, out_ref):
    token_rows, model_width = out_ref.shape
    window, height, _ = returned_ref.shape
    lines = returned_ref[...].astype(F32).reshape(window * height, WIDE).astype(BF16)
    result = dot(table_ref[...], lines).astype(BF16)
    for c in range(model_width // WIDE):
        out_ref[:, c * WIDE : (c + 1) * WIDE] = result[c * token_rows : (c + 1) * token_rows]


def grads_kernel(groups, *refs):
    slices_refs, acts_refs, (out_ref, held_ref, sems) = refs[:groups], refs[groups : 2 * groups], refs[-3:]
    hidden_units = out_ref.shape[3]
    copies = [pltpu.make_async_copy(held_ref.at[at], out_ref.at[0, at], sems.at[at]) for at in range(3)]
    rows_here = acts_refs[0].shape[0]
    step = max(1, min(groups, 640 // rows_here))
    for at in range(3):
        lanes = slice(at * hidden_units, (at + 1) * hidden_units)
        kind = 0 if at < 2 else 1
        places = [kind + 2 if b == 0 else kind for b in range(groups)]
        total = None
        for first in range(0, groups, step):
            some = range(first, first + step)
            rows = jnp.concatenate([slices_refs[b][places[b]] for b in some], axis=0)
            acts = jnp.concatenate([acts_refs[b][:, lanes] for b in some], axis=0)
            term = dot_tn(rows, acts)
            total = term if total is None else total + term
        held_ref[at] = total
        copies[at].start()
    for copy in copies:
        copy.wait()


def on_device(tokens, out_grad, expert_ids, gates, expert_weights):
    window = lax.axis_size("expert")
    groups = lax.axis_size("dp")
    token_rows, model_width = tokens.shape
    hidden_units = expert_weights.shape[3]
    owned = model_width // groups
    chunks = model_width // WIDE
    padded = piece_rows(chunks)
    rows_here = window * SLOTS
    wide = 2 * hidden_units
    anywhere = pl.BlockSpec(memory_space=pl.ANY)

    far = list(range(2, groups, 2))
    token = pl.pallas_call(
        token_kernel,
        out_shape=shape(8, 128, kind=F32),
        compiler_params=params(),
        cost_estimate=cost(10**11, 10**8),
    )()
    arriving = [swap(expert_weights, b) for b in far]
    near = swap(expert_weights, 1)

    ids_t, gates_t = expert_ids.T, gates.T
    sent, code = pl.pallas_call(
        pack_kernel,
        out_shape=(
            shape(window, 2 * padded, WIDE),
            shape(window, token_rows, kind=F32),
        ),
        compiler_params=params(tokens, out_grad),
    )(ids_t, gates_t, tokens, out_grad, token)

    got = lax.all_to_all(sent, "expert", split_axis=0, concat_axis=0, tiled=True)
    table = pl.pallas_call(
        lambda *refs: table_kernel(chunks, *refs),
        out_shape=shape(chunks * token_rows, window * padded),
        compiler_params=params(),
        cost_estimate=cost(10**11, 10**8),
    )(code)

    outs = pl.pallas_call(
        lambda *refs: partial_kernel(groups, *refs),
        in_specs=[pl.BlockSpec()] + [anywhere] * 2,
        out_shape=[
            shape(rows_here, 3 * hidden_units, kind=F32),
            shape(rows_here, model_width),
            shape(rows_here, model_width),
            shape(2, owned, wide),
            shape(8, 128, kind=F32),
        ]
        + [shape(4, rows_here, owned)]
        + [shape(2, rows_here, owned)] * (groups - 2),
        scratch_shapes=[
            pltpu.VMEM((2, owned, hidden_units), BF16),
            pltpu.SemaphoreType.DMA((2, 3)),
        ],
        compiler_params=params(got, expert_weights, expert_weights),
    )(got, expert_weights, near)
    partial, rows, grads, near_pairs, token = outs[:5]
    slices = list(outs[5:])
    slices = slices[:1] + [swap(slices[b - 1], b) for b in range(1, groups)]

    arrived = pl.pallas_call(
        keep_kernel,
        in_specs=[anywhere] * (len(far) + 1),
        out_specs=[anywhere] * len(far),
        out_shape=[shape(*expert_weights.shape)] * len(far),
        input_output_aliases={at + 1: at for at in range(len(far))},
        compiler_params=params(),
        cost_estimate=cost(10**11, 10**8),
    )(token, *arriving)
    last = [swap(value, 1) for value in arrived]
    partial, far_pairs = pl.pallas_call(
        lambda *refs: far_kernel(groups, *refs),
        in_specs=[pl.BlockSpec()] * 3 + [anywhere] * len(far),
        out_shape=(shape(rows_here, 3 * hidden_units, kind=F32), shape(len(far), owned, wide)),
        scratch_shapes=[
            pltpu.VMEM((len(far), owned, hidden_units), BF16),
            pltpu.SemaphoreType.DMA((len(far), 3)),
        ],
        compiler_params=params(rows, grads, *arrived, *arrived),
    )(rows, grads, partial, *arrived)

    acts, back = pl.pallas_call(
        lambda *refs: back_kernel(groups, *refs),
        out_shape=(shape(rows_here, 3 * hidden_units), shape(window, padded, WIDE)),
        scratch_shapes=[pltpu.VMEM((rows_here, model_width), F32)],
        compiler_params=params(rows, grads, partial, near_pairs, far_pairs, *last),
        cost_estimate=cost(10**6, 10**5),
    )(rows, grads, partial, near_pairs, far_pairs, *last)
    returned = lax.all_to_all(back, "expert", split_axis=0, concat_axis=0, tiled=True)

    every = slices + [acts] + [swap(acts, b) for b in range(1, groups)]
    weight_grads = pl.pallas_call(
        lambda *refs: grads_kernel(groups, *refs),
        out_specs=anywhere,
        out_shape=shape(1, 3, owned, hidden_units, kind=F32),
        scratch_shapes=[
            pltpu.VMEM((3, owned, hidden_units), F32),
            pltpu.SemaphoreType.DMA((3,)),
        ],
        compiler_params=params(*every, expert_weights, expert_weights),
        cost_estimate=cost(6 * groups * rows_here * owned * hidden_units, 12 * owned * hidden_units),
    )(*every)

    token_grads = pl.pallas_call(
        combine_kernel,
        out_shape=shape(token_rows, model_width),
        compiler_params=params(table, back, tokens),
    )(returned, table)
    return (token_grads, weight_grads)


def solution(mesh):
    lines = P(("dp", "expert"), None)
    slabs = P("expert", None, "dp", None)
    return jax.shard_map(
        on_device,
        mesh=mesh,
        in_specs=(lines, lines, lines, lines, slabs),
        out_specs=(lines, slabs),
        check_vma=False,
    )
```

```python
import jax
import jax.numpy as jnp
from jax import lax
from jax.experimental import pallas as pl
from jax.experimental.pallas import tpu as pltpu
from jax.sharding import PartitionSpec as P

SLOTS = 10
WIDE = 512
JOIN = 4
F32 = jnp.float32
BF16 = jnp.bfloat16


def dot(first_op, second_op):
    return jnp.dot(first_op, second_op, preferred_element_type=F32)


def dot_tn(first_op, second_op):
    return lax.dot_general(first_op, second_op, (((0,), (0,)), ((), ())), preferred_element_type=F32)


def dot_nt(first_op, second_op):
    return lax.dot_general(first_op, second_op, (((1,), (1,)), ((), ())), preferred_element_type=F32)


def swap(value, bits):
    return lax.ppermute(value, "dp", [(i, i ^ bits) for i in range(lax.axis_size("dp"))])


def piece_rows(chunks):
    return -(-chunks * SLOTS // 8) * 8


def params(*arrays):
    moved = sum(a.size * a.dtype.itemsize for a in arrays)
    return pltpu.CompilerParams(vmem_limit_bytes=min(56 * 2**20, 6 * 2**20 + 3 * moved // 2))


def cost(flops, moved):
    return pl.CostEstimate(flops=flops, bytes_accessed=moved, transcendentals=0)


def shape(*extent, kind=BF16):
    return jax.ShapeDtypeStruct(extent, kind)


def lower(value, by):
    return jnp.floor((value + 0.5) * (1.0 / by))


def sort_matrix(parts, chunks, transposed):
    padded = piece_rows(chunks)
    wide, tall = JOIN * parts * padded, parts * chunks * JOIN * SLOTS
    extent, axis = ((wide, tall), 0) if transposed else ((tall, wide), 1)
    line = (wide, 1) if transposed else (1, wide)
    place = lax.broadcasted_iota(jnp.int32, line, axis).astype(F32)
    block = lower(place, padded)
    inside = place - block * padded
    source = lower(block, parts)
    part = block - source * parts
    chunk = lower(inside, SLOTS)
    slot = inside - chunk * SLOTS
    target = ((part * chunks + chunk) * JOIN + source) * SLOTS + slot
    target = jnp.where(chunk < chunks, target, -1.0)
    spots = lax.broadcasted_iota(jnp.int32, extent, 1 - axis).astype(F32)
    return jnp.where(spots == target, 1.0, 0.0).astype(BF16)


def table_of(code, values, chunks, padded):
    window, token_rows = code.shape
    spots = lax.broadcasted_iota(jnp.int32, (padded, chunks * token_rows), 0).astype(F32)
    tables = []
    for expert in range(window):
        own = code[expert : expert + 1]
        hit = spots == jnp.concatenate([own + float(SLOTS * c) for c in range(chunks)], axis=1)
        row = []
        for value in values:
            if value is None:
                row.append(jnp.where(hit, 1.0, 0.0))
            else:
                gate = jnp.concatenate([value[expert : expert + 1]] * chunks, axis=1)
                row.append(jnp.where(hit, gate, 0.0))
        tables.append(row)
    return [jnp.concatenate([t[i] for t in tables], axis=0) for i in range(len(values))]


def token_kernel(token_ref):
    token_ref[...] = jnp.zeros_like(token_ref)


def pack_kernel(ids_ref, gates_ref, tokens_ref, grads_ref, _, sent_ref, code_ref):
    token_rows, model_width = tokens_ref.shape
    window = code_ref.shape[0]
    chunks = model_width // WIDE
    padded = piece_rows(chunks)
    above = lax.broadcasted_iota(jnp.int32, (token_rows, token_rows), 0)
    along = lax.broadcasted_iota(jnp.int32, (token_rows, token_rows), 1)
    earlier = jnp.where(above < along, 1.0, 0.0).astype(BF16)
    ids = ids_ref[...]
    gates = gates_ref[...].astype(F32)
    members, chosen = [], []
    for expert in range(window):
        hit = ids == expert
        members.append(jnp.sum(jnp.where(hit, 1.0, 0.0), axis=0, keepdims=True))
        chosen.append(jnp.sum(jnp.where(hit, gates, 0.0), axis=0, keepdims=True))
    members = jnp.concatenate(members, axis=0)
    chosen = jnp.concatenate(chosen, axis=0)
    code = jnp.where(members > 0.0, dot(members.astype(BF16), earlier), -1e6)
    code_ref[...] = code
    table, gated = table_of(code, [None, chosen], chunks, padded)

    def columns(ref):
        return jnp.concatenate([ref[:, c * WIDE : (c + 1) * WIDE] for c in range(chunks)], axis=0)

    rows = dot(table.astype(BF16), columns(tokens_ref))
    grads = dot(gated.astype(BF16), columns(grads_ref))
    for expert in range(window):
        lines = slice(expert * padded, (expert + 1) * padded)
        sent_ref[expert] = jnp.concatenate([rows[lines], grads[lines]], axis=0).astype(BF16)


def table_kernel(chunks, code_ref, table_ref):
    (table,) = table_of(code_ref[...], [None], chunks, piece_rows(chunks))
    table_ref[...] = table.T.astype(BF16)


def keep_kernel(*refs):
    pass


def anchor_kernel(*refs):
    refs[-1][...] = jnp.zeros_like(refs[-1])


def partial_kernel(groups, got_ref, own_in, near_in, _, *refs):
    count = 2 * (groups - 2)
    sides_in, (out_ref, grads_ref, pair_ref, token_ref), refs = refs[:count], refs[count : count + 4], refs[count + 4 :]
    slices_refs, (rows_ref, down_ref, sems) = refs[: groups - 1], refs[groups - 1 :]
    hidden_units = down_ref.shape[2]
    sources = [(own_in.at[0, 0], own_in.at[0, 1]), (near_in.at[0, 0], near_in.at[0, 1])]
    sources += [(sides_in[2 * b], sides_in[2 * b + 1]) for b in range(groups - 2)]
    copies = []
    for b, pair in enumerate(sources):
        for at in range(2):
            target = pair_ref.at[b, :, pl.ds(at * hidden_units, hidden_units)]
            copies.append(pltpu.make_async_copy(pair[at], target, sems.at[b, at]))
    for b, source in enumerate((own_in, near_in)):
        copies.append(pltpu.make_async_copy(source.at[0, 2], down_ref.at[b], sems.at[b, 2]))
    for copy in copies:
        copy.start()
    token_ref[...] = jnp.zeros_like(token_ref)
    sources, height, _ = got_ref.shape
    model_width = rows_ref.shape[1]
    chunks = model_width // WIDE
    owned = model_width // groups
    joined = sources // JOIN
    tall = JOIN * SLOTS
    blocks = jnp.concatenate(
        [got_ref[q * JOIN : (q + 1) * JOIN].reshape(JOIN * height, WIDE) for q in range(joined)],
        axis=1,
    )
    lines = dot(sort_matrix(2, chunks, False), blocks)

    def gathered(part):
        return jnp.concatenate(
            [
                jnp.concatenate(
                    [
                        lines[
                            (part * chunks + c) * tall : (part * chunks + c + 1) * tall,
                            q * WIDE : (q + 1) * WIDE,
                        ]
                        for c in range(chunks)
                    ],
                    axis=1,
                )
                for q in range(joined)
            ],
            axis=0,
        ).astype(BF16)

    rows_ref[...] = gathered(0)
    grads_ref[...] = gathered(1)
    me = lax.axis_index("dp")
    wide = pair_ref.shape[2]
    for copy in copies:
        copy.wait()
    pair_sum, down_sum = None, None
    for b in range(groups):
        lanes = pl.ds(pl.multiple_of((me ^ b) * owned, 128), owned)
        rows, grads = rows_ref[:, lanes], grads_ref[:, lanes]
        target, first = (slices_refs[0], 2) if b == 0 else (slices_refs[b - 1], 0)
        target[first] = rows
        target[first + 1] = grads
        term = dot(rows, pair_ref[b])
        pair_sum = term if pair_sum is None else pair_sum + term
        if b < 2:
            term = dot(grads, down_ref[b])
            down_sum = term if down_sum is None else down_sum + term
    out_ref[:, :wide] = pair_sum
    out_ref[:, wide:] = down_sum


def lanes_of(owner, owned):
    return pl.ds(pl.multiple_of(owner * owned, 128), owned)


def far_kernel(groups, grads_ref, partial_ref, *refs):
    down_refs, out_ref = refs[:-1], refs[-1]
    me = lax.axis_index("dp")
    owned, hidden_units = down_refs[0].shape
    total = partial_ref[:, 2 * hidden_units :]
    for at, ref in enumerate(down_refs):
        total = total + dot(grads_ref[:, lanes_of(me ^ (2 * at + 2), owned)], ref[...])
    out_ref[...] = total


def back_kernel(groups, grads_ref, partial_ref, hidden_ref, pair_ref, *refs):
    down_refs, (acts_ref, out_ref, back_ref) = refs[:-3], refs[-3:]
    me = lax.axis_index("dp")
    model_width = grads_ref.shape[1]
    owned = model_width // groups
    chunks = model_width // WIDE
    hidden_units = partial_ref.shape[1] // 3
    wide = 2 * hidden_units

    def lanes(b):
        return lanes_of(me ^ b, owned)

    gate_act = partial_ref[:, :hidden_units]
    up_act = partial_ref[:, hidden_units:wide]
    grad_hidden = hidden_ref[...]
    for at, ref in enumerate(down_refs):
        grad_hidden = grad_hidden + dot(grads_ref[:, lanes(2 * at + 3)], ref[...])
    logistic = jax.nn.sigmoid(gate_act)
    swish_out = gate_act * logistic
    hidden = (swish_out * up_act).astype(BF16)
    grad_up = (grad_hidden * swish_out).astype(BF16)
    grad_gate = (grad_hidden * up_act * logistic * (1.0 + gate_act * (1.0 - logistic))).astype(BF16)
    acts = jnp.concatenate([grad_gate, grad_up], axis=1)
    acts_ref[:, :wide] = acts
    acts_ref[:, wide:] = hidden
    for b in range(groups):
        back_ref[:, lanes(b)] = dot_nt(acts, pair_ref[b])
    tall = JOIN * SLOTS
    joined = grads_ref.shape[0] // tall
    lines = jnp.concatenate(
        [
            jnp.concatenate(
                [
                    back_ref[q * tall : (q + 1) * tall, c * WIDE : (c + 1) * WIDE]
                    for c in range(chunks)
                ],
                axis=0,
            )
            for q in range(joined)
        ],
        axis=1,
    ).astype(BF16)
    blocks = dot(sort_matrix(1, chunks, True), lines)
    height = piece_rows(chunks)
    for q in range(joined):
        for j in range(JOIN):
            part = blocks[j * height : (j + 1) * height, q * WIDE : (q + 1) * WIDE]
            out_ref[q * JOIN + j] = part.astype(BF16)


def combine_kernel(returned_ref, table_ref, out_ref):
    token_rows, model_width = out_ref.shape
    window, height, _ = returned_ref.shape
    lines = returned_ref[...].astype(F32).reshape(window * height, WIDE).astype(BF16)
    result = dot(table_ref[...], lines).astype(BF16)
    for c in range(model_width // WIDE):
        out_ref[:, c * WIDE : (c + 1) * WIDE] = result[c * token_rows : (c + 1) * token_rows]


def grads_kernel(groups, *refs):
    slices_refs, acts_refs, (out_ref, held_ref, sems) = refs[:groups], refs[groups : 2 * groups], refs[-3:]
    hidden_units = out_ref.shape[3]
    copies = [pltpu.make_async_copy(held_ref.at[at], out_ref.at[0, at], sems.at[at]) for at in range(3)]
    rows_here = acts_refs[0].shape[0]
    step = max(1, min(groups, 640 // rows_here))
    for at in range(3):
        lanes = slice(at * hidden_units, (at + 1) * hidden_units)
        kind = 0 if at < 2 else 1
        places = [kind + 2 if b == 0 else kind for b in range(groups)]
        total = None
        for first in range(0, groups, step):
            some = range(first, first + step)
            rows = jnp.concatenate([slices_refs[b][places[b]] for b in some], axis=0)
            acts = jnp.concatenate([acts_refs[b][:, lanes] for b in some], axis=0)
            term = dot_tn(rows, acts)
            total = term if total is None else total + term
        held_ref[at] = total
        copies[at].start()
    for copy in copies:
        copy.wait()


def on_device(tokens, out_grad, expert_ids, gates, expert_weights):
    window = lax.axis_size("expert")
    groups = lax.axis_size("dp")
    token_rows, model_width = tokens.shape
    hidden_units = expert_weights.shape[3]
    owned = model_width // groups
    chunks = model_width // WIDE
    padded = piece_rows(chunks)
    rows_here = window * SLOTS
    wide = 2 * hidden_units
    anywhere = pl.BlockSpec(memory_space=pl.ANY)

    far = list(range(2, groups, 2))
    single = [expert_weights[0, 0]]
    rest, _ = lax.optimization_barrier((expert_weights, single[0]))
    single += [rest[0, 1], rest[0, 2]]
    gates_far = [swap(single[0], b) for b in far]
    ups_far = [swap(single[1], b) for b in far]
    downs_far = [swap(single[2], b) for b in far]
    near = swap(expert_weights, 1)

    token = pl.pallas_call(
        token_kernel,
        out_shape=shape(8, 128, kind=F32),
        compiler_params=params(),
        cost_estimate=cost(10**11, 10**8),
    )()

    ids_t, gates_t = expert_ids.T, gates.T
    sent, code = pl.pallas_call(
        pack_kernel,
        out_shape=(
            shape(window, 2 * padded, WIDE),
            shape(window, token_rows, kind=F32),
        ),
        compiler_params=params(tokens, out_grad),
    )(ids_t, gates_t, tokens, out_grad, token)

    got = lax.all_to_all(sent, "expert", split_axis=0, concat_axis=0, tiled=True)
    table = pl.pallas_call(
        lambda *refs: table_kernel(chunks, *refs),
        out_shape=shape(chunks * token_rows, window * padded),
        compiler_params=params(),
        cost_estimate=cost(10**11, 10**8),
    )(code)

    here = pl.pallas_call(
        anchor_kernel,
        in_specs=[anywhere] * (2 * len(far)),
        out_shape=shape(8, 128, kind=F32),
        compiler_params=params(),
        cost_estimate=cost(10**11, 10**8),
    )(*gates_far, *ups_far)
    sides = []
    for gate, up in zip(gates_far, ups_far):
        sides += [gate, up, swap(gate, 1), swap(up, 1)]
    outs = pl.pallas_call(
        lambda *refs: partial_kernel(groups, *refs),
        in_specs=[pl.BlockSpec()] + [anywhere] * (3 + len(sides)),
        out_shape=[
            shape(rows_here, 3 * hidden_units, kind=F32),
            shape(rows_here, model_width),
            shape(groups, owned, wide),
            shape(8, 128, kind=F32),
            shape(4, rows_here, owned),
        ]
        + [shape(2, rows_here, owned)] * (groups - 2),
        scratch_shapes=[
            pltpu.VMEM((rows_here, model_width), BF16),
            pltpu.VMEM((2, owned, hidden_units), BF16),
            pltpu.SemaphoreType.DMA((groups, 3)),
        ],
        compiler_params=params(got, *[expert_weights] * groups),
    )(got, expert_weights, near, here, *sides)
    partial, grads, pairs, token = outs[:4]
    slices = list(outs[4:])
    slices = slices[:1] + [swap(slices[b - 1], b) for b in range(1, groups)]

    arrived = pl.pallas_call(
        keep_kernel,
        in_specs=[anywhere] * (len(far) + 1),
        out_specs=[anywhere] * len(far),
        out_shape=[shape(owned, hidden_units)] * len(far),
        input_output_aliases={at + 1: at for at in range(len(far))},
        compiler_params=params(),
        cost_estimate=cost(10**11, 10**8),
    )(token, *downs_far)
    last = [swap(value, 1) for value in arrived]
    far_hidden = pl.pallas_call(
        lambda *refs: far_kernel(groups, *refs),
        out_shape=shape(rows_here, hidden_units, kind=F32),
        compiler_params=params(grads, partial, *arrived),
    )(grads, partial, *arrived)

    acts, back = pl.pallas_call(
        lambda *refs: back_kernel(groups, *refs),
        out_shape=(shape(rows_here, 3 * hidden_units), shape(window, padded, WIDE)),
        scratch_shapes=[pltpu.VMEM((rows_here, model_width), F32)],
        compiler_params=params(grads, partial, pairs, *last),
        cost_estimate=cost(10**6, 10**5),
    )(grads, partial, far_hidden, pairs, *last)
    returned = lax.all_to_all(back, "expert", split_axis=0, concat_axis=0, tiled=True)

    every = slices + [acts] + [swap(acts, b) for b in range(1, groups)]
    weight_grads = pl.pallas_call(
        lambda *refs: grads_kernel(groups, *refs),
        out_specs=anywhere,
        out_shape=shape(1, 3, owned, hidden_units, kind=F32),
        scratch_shapes=[
            pltpu.VMEM((3, owned, hidden_units), F32),
            pltpu.SemaphoreType.DMA((3,)),
        ],
        compiler_params=params(*every, expert_weights, expert_weights),
        cost_estimate=cost(6 * groups * rows_here * owned * hidden_units, 12 * owned * hidden_units),
    )(*every)

    token_grads = pl.pallas_call(
        combine_kernel,
        out_shape=shape(token_rows, model_width),
        compiler_params=params(table, back, tokens),
    )(returned, table)
    return (token_grads, weight_grads)


def solution(mesh):
    lines = P(("dp", "expert"), None)
    slabs = P("expert", None, "dp", None)
    return jax.shard_map(
        on_device,
        mesh=mesh,
        in_specs=(lines, lines, lines, lines, slabs),
        out_specs=(lines, slabs),
        check_vma=False,
    )
```

```python
import jax
import jax.numpy as jnp
from jax import lax
from jax.experimental import pallas as pl
from jax.experimental.pallas import tpu as pltpu
from jax.sharding import PartitionSpec as P

SLOTS = 10
WIDE = 512
JOIN = 4
F32 = jnp.float32
BF16 = jnp.bfloat16


def dot(first_op, second_op):
    return jnp.dot(first_op, second_op, preferred_element_type=F32)


def dot_tn(first_op, second_op):
    return lax.dot_general(first_op, second_op, (((0,), (0,)), ((), ())), preferred_element_type=F32)


def dot_nt(first_op, second_op):
    return lax.dot_general(first_op, second_op, (((1,), (1,)), ((), ())), preferred_element_type=F32)


def swap(value, bits):
    return lax.ppermute(value, "dp", [(i, i ^ bits) for i in range(lax.axis_size("dp"))])


def piece_rows(chunks):
    return -(-chunks * SLOTS // 8) * 8


def params(*arrays):
    moved = sum(a.size * a.dtype.itemsize for a in arrays)
    return pltpu.CompilerParams(vmem_limit_bytes=min(56 * 2**20, 6 * 2**20 + 3 * moved // 2))


def cost(flops, moved):
    return pl.CostEstimate(flops=flops, bytes_accessed=moved, transcendentals=0)


def shape(*extent, kind=BF16):
    return jax.ShapeDtypeStruct(extent, kind)


def lower(value, by):
    return jnp.floor((value + 0.5) * (1.0 / by))


def sort_matrix(parts, chunks, transposed):
    padded = piece_rows(chunks)
    wide, tall = JOIN * parts * padded, parts * chunks * JOIN * SLOTS
    extent, axis = ((wide, tall), 0) if transposed else ((tall, wide), 1)
    line = (wide, 1) if transposed else (1, wide)
    place = lax.broadcasted_iota(jnp.int32, line, axis).astype(F32)
    block = lower(place, padded)
    inside = place - block * padded
    source = lower(block, parts)
    part = block - source * parts
    chunk = lower(inside, SLOTS)
    slot = inside - chunk * SLOTS
    target = ((part * chunks + chunk) * JOIN + source) * SLOTS + slot
    target = jnp.where(chunk < chunks, target, -1.0)
    spots = lax.broadcasted_iota(jnp.int32, extent, 1 - axis).astype(F32)
    return jnp.where(spots == target, 1.0, 0.0).astype(BF16)


def table_of(code, values, chunks, padded):
    window, token_rows = code.shape
    spots = lax.broadcasted_iota(jnp.int32, (padded, chunks * token_rows), 0).astype(F32)
    tables = []
    for expert in range(window):
        own = code[expert : expert + 1]
        hit = spots == jnp.concatenate([own + float(SLOTS * c) for c in range(chunks)], axis=1)
        row = []
        for value in values:
            if value is None:
                row.append(jnp.where(hit, 1.0, 0.0))
            else:
                gate = jnp.concatenate([value[expert : expert + 1]] * chunks, axis=1)
                row.append(jnp.where(hit, gate, 0.0))
        tables.append(row)
    return [jnp.concatenate([t[i] for t in tables], axis=0) for i in range(len(values))]


def token_kernel(token_ref):
    token_ref[...] = jnp.zeros_like(token_ref)


def pack_kernel(ids_ref, gates_ref, tokens_ref, grads_ref, _, sent_ref, code_ref):
    token_rows, model_width = tokens_ref.shape
    window = code_ref.shape[0]
    chunks = model_width // WIDE
    padded = piece_rows(chunks)
    above = lax.broadcasted_iota(jnp.int32, (token_rows, token_rows), 0)
    along = lax.broadcasted_iota(jnp.int32, (token_rows, token_rows), 1)
    earlier = jnp.where(above < along, 1.0, 0.0).astype(BF16)
    ids = ids_ref[...]
    gates = gates_ref[...].astype(F32)
    members, chosen = [], []
    for expert in range(window):
        hit = ids == expert
        members.append(jnp.sum(jnp.where(hit, 1.0, 0.0), axis=0, keepdims=True))
        chosen.append(jnp.sum(jnp.where(hit, gates, 0.0), axis=0, keepdims=True))
    members = jnp.concatenate(members, axis=0)
    chosen = jnp.concatenate(chosen, axis=0)
    code = jnp.where(members > 0.0, dot(members.astype(BF16), earlier), -1e6)
    code_ref[...] = code
    table, gated = table_of(code, [None, chosen], chunks, padded)

    def columns(ref):
        return jnp.concatenate([ref[:, c * WIDE : (c + 1) * WIDE] for c in range(chunks)], axis=0)

    rows = dot(table.astype(BF16), columns(tokens_ref))
    grads = dot(gated.astype(BF16), columns(grads_ref))
    for expert in range(window):
        lines = slice(expert * padded, (expert + 1) * padded)
        sent_ref[expert] = jnp.concatenate([rows[lines], grads[lines]], axis=0).astype(BF16)


def table_kernel(chunks, code_ref, table_ref):
    (table,) = table_of(code_ref[...], [None], chunks, piece_rows(chunks))
    table_ref[...] = table.T.astype(BF16)


def keep_kernel(*refs):
    pass


def place(source, pair_ref, down_ref, sems, at):
    hidden_units = down_ref.shape[1]
    moves = [
        (source.at[0], pair_ref.at[:, pl.ds(0, hidden_units)]),
        (source.at[1], pair_ref.at[:, pl.ds(hidden_units, hidden_units)]),
        (source.at[2], down_ref),
    ]
    return [
        pltpu.make_async_copy(start, end, sems.at[at, which]) for which, (start, end) in enumerate(moves)
    ]


def partial_kernel(groups, got_ref, own_in, near_in, *refs):
    (out_ref, rows_ref, grads_ref, pair_ref, token_ref), refs = refs[:5], refs[5:]
    slices_refs, (down_ref, sems) = refs[: groups - 1], refs[groups - 1 :]
    copies = [
        copy
        for b, source in enumerate((own_in.at[0], near_in.at[0]))
        for copy in place(source, pair_ref.at[b], down_ref.at[b], sems, b)
    ]
    for copy in copies:
        copy.start()
    token_ref[...] = jnp.zeros_like(token_ref)
    sources, height, _ = got_ref.shape
    model_width = rows_ref.shape[1]
    chunks = model_width // WIDE
    owned = model_width // groups
    joined = sources // JOIN
    tall = JOIN * SLOTS
    blocks = jnp.concatenate(
        [got_ref[q * JOIN : (q + 1) * JOIN].reshape(JOIN * height, WIDE) for q in range(joined)],
        axis=1,
    )
    lines = dot(sort_matrix(2, chunks, False), blocks)

    def gathered(part):
        return jnp.concatenate(
            [
                jnp.concatenate(
                    [
                        lines[
                            (part * chunks + c) * tall : (part * chunks + c + 1) * tall,
                            q * WIDE : (q + 1) * WIDE,
                        ]
                        for c in range(chunks)
                    ],
                    axis=1,
                )
                for q in range(joined)
            ],
            axis=0,
        ).astype(BF16)

    rows_ref[...] = gathered(0)
    grads_ref[...] = gathered(1)
    me = lax.axis_index("dp")
    wide = pair_ref.shape[2]
    for copy in copies:
        copy.wait()
    pair_sum, down_sum = None, None
    for b in range(groups):
        lanes = pl.ds(pl.multiple_of((me ^ b) * owned, 128), owned)
        rows, grads = rows_ref[:, lanes], grads_ref[:, lanes]
        target, first = (slices_refs[0], 2) if b == 0 else (slices_refs[b - 1], 0)
        target[first] = rows
        target[first + 1] = grads
        if b < 2:
            term = dot(rows, pair_ref[b])
            pair_sum = term if pair_sum is None else pair_sum + term
            term = dot(grads, down_ref[b])
            down_sum = term if down_sum is None else down_sum + term
    out_ref[:, :wide] = pair_sum
    out_ref[:, wide:] = down_sum


def lanes_of(owner, owned):
    return pl.ds(pl.multiple_of(owner * owned, 128), owned)


def far_kernel(groups, rows_ref, grads_ref, partial_ref, *refs):
    far = range(2, groups, 2)
    weights_in, (out_ref, pair_ref, down_ref, sems) = refs[: len(far)], refs[len(far) :]
    copies = [
        place(source.at[0], pair_ref.at[at], down_ref.at[at], sems, at)
        for at, source in enumerate(weights_in)
    ]
    for some in copies:
        for copy in some:
            copy.start()
    me = lax.axis_index("dp")
    owned, wide = pair_ref.shape[1:]
    pair_sum, down_sum = partial_ref[:, :wide], partial_ref[:, wide:]
    for at, b in enumerate(far):
        for copy in copies[at]:
            copy.wait()
        lanes = lanes_of(me ^ b, owned)
        pair_sum = pair_sum + dot(rows_ref[:, lanes], pair_ref[at])
        down_sum = down_sum + dot(grads_ref[:, lanes], down_ref[at])
    out_ref[:, :wide] = pair_sum
    out_ref[:, wide:] = down_sum


def back_kernel(groups, rows_ref, grads_ref, partial_ref, near_ref, far_ref, *refs):
    last_refs, (acts_ref, out_ref, back_ref) = refs[:-3], refs[-3:]
    me = lax.axis_index("dp")
    model_width = grads_ref.shape[1]
    owned = model_width // groups
    chunks = model_width // WIDE
    hidden_units = partial_ref.shape[1] // 3
    wide = 2 * hidden_units

    def lanes(b):
        return lanes_of(me ^ b, owned)

    gate_act = partial_ref[:, :hidden_units]
    up_act = partial_ref[:, hidden_units:wide]
    grad_hidden = partial_ref[:, wide:]
    for at, ref in enumerate(last_refs):
        here = lanes(2 * at + 3)
        gate_act = gate_act + dot(rows_ref[:, here], ref[0, 0])
        up_act = up_act + dot(rows_ref[:, here], ref[0, 1])
        grad_hidden = grad_hidden + dot(grads_ref[:, here], ref[0, 2])
    logistic = jax.nn.sigmoid(gate_act)
    swish_out = gate_act * logistic
    hidden = (swish_out * up_act).astype(BF16)
    grad_up = (grad_hidden * swish_out).astype(BF16)
    grad_gate = (grad_hidden * up_act * logistic * (1.0 + gate_act * (1.0 - logistic))).astype(BF16)
    acts = jnp.concatenate([grad_gate, grad_up], axis=1)
    acts_ref[:, :wide] = acts
    acts_ref[:, wide:] = hidden
    for b in range(groups):
        if b < 2:
            term = dot_nt(acts, near_ref[b])
        elif b % 2 == 0:
            term = dot_nt(acts, far_ref[b // 2 - 1])
        else:
            ref = last_refs[b // 2 - 1]
            term = dot_nt(grad_gate, ref[0, 0]) + dot_nt(grad_up, ref[0, 1])
        back_ref[:, lanes(b)] = term
    tall = JOIN * SLOTS
    joined = grads_ref.shape[0] // tall
    lines = jnp.concatenate(
        [
            jnp.concatenate(
                [
                    back_ref[q * tall : (q + 1) * tall, c * WIDE : (c + 1) * WIDE]
                    for c in range(chunks)
                ],
                axis=0,
            )
            for q in range(joined)
        ],
        axis=1,
    ).astype(BF16)
    blocks = dot(sort_matrix(1, chunks, True), lines)
    height = piece_rows(chunks)
    for q in range(joined):
        for j in range(JOIN):
            part = blocks[j * height : (j + 1) * height, q * WIDE : (q + 1) * WIDE]
            out_ref[q * JOIN + j] = part.astype(BF16)


def combine_kernel(returned_ref, table_ref, out_ref, held_ref, sems):
    token_rows, model_width = held_ref.shape
    window, height, _ = returned_ref.shape
    lines = returned_ref[...].astype(F32).reshape(window * height, WIDE).astype(BF16)
    parts = sems.shape[0]
    chunks = model_width // WIDE // parts
    copies = []
    for part in range(parts):
        table = table_ref[part * chunks * token_rows : (part + 1) * chunks * token_rows]
        result = dot(table, lines).astype(BF16)
        for c in range(chunks):
            at = part * chunks + c
            held_ref[:, at * WIDE : (at + 1) * WIDE] = result[c * token_rows : (c + 1) * token_rows]
        lanes = pl.ds(part * chunks * WIDE, chunks * WIDE)
        copies.append(
            pltpu.make_async_copy(held_ref.at[:, lanes], out_ref.at[:, lanes], sems.at[part])
        )
        copies[-1].start()
    for copy in copies:
        copy.wait()


def grads_kernel(groups, *refs):
    slices_refs, acts_refs, (out_ref, held_ref, sems) = refs[:groups], refs[groups : 2 * groups], refs[-3:]
    hidden_units = out_ref.shape[3]
    copies = [pltpu.make_async_copy(held_ref.at[at], out_ref.at[0, at], sems.at[at]) for at in range(3)]
    rows_here = acts_refs[0].shape[0]
    step = max(1, min(groups, 640 // rows_here))
    for at in range(3):
        lanes = slice(at * hidden_units, (at + 1) * hidden_units)
        kind = 0 if at < 2 else 1
        places = [kind + 2 if b == 0 else kind for b in range(groups)]
        total = None
        for first in range(0, groups, step):
            some = range(first, first + step)
            rows = jnp.concatenate([slices_refs[b][places[b]] for b in some], axis=0)
            acts = jnp.concatenate([acts_refs[b][:, lanes] for b in some], axis=0)
            term = dot_tn(rows, acts)
            total = term if total is None else total + term
        held_ref[at] = total
        copies[at].start()
    for copy in copies:
        copy.wait()


def on_device(tokens, out_grad, expert_ids, gates, expert_weights):
    window = lax.axis_size("expert")
    groups = lax.axis_size("dp")
    token_rows, model_width = tokens.shape
    hidden_units = expert_weights.shape[3]
    owned = model_width // groups
    chunks = model_width // WIDE
    padded = piece_rows(chunks)
    rows_here = window * SLOTS
    wide = 2 * hidden_units
    anywhere = pl.BlockSpec(memory_space=pl.ANY)

    far = list(range(2, groups, 2))
    token = pl.pallas_call(
        token_kernel,
        out_shape=shape(8, 128, kind=F32),
        compiler_params=params(),
        cost_estimate=cost(10**11, 10**8),
    )()
    arriving = [swap(expert_weights, b) for b in far]
    near = swap(expert_weights, 1)

    ids_t, gates_t = expert_ids.T, gates.T
    sent, code = pl.pallas_call(
        pack_kernel,
        out_shape=(
            shape(window, 2 * padded, WIDE),
            shape(window, token_rows, kind=F32),
        ),
        compiler_params=params(tokens, out_grad),
    )(ids_t, gates_t, tokens, out_grad, token)

    got = lax.all_to_all(sent, "expert", split_axis=0, concat_axis=0, tiled=True)
    table = pl.pallas_call(
        lambda *refs: table_kernel(chunks, *refs),
        out_shape=shape(chunks * token_rows, window * padded),
        compiler_params=params(),
        cost_estimate=cost(10**11, 10**8),
    )(code)

    outs = pl.pallas_call(
        lambda *refs: partial_kernel(groups, *refs),
        in_specs=[pl.BlockSpec()] + [anywhere] * 2,
        out_shape=[
            shape(rows_here, 3 * hidden_units, kind=F32),
            shape(rows_here, model_width),
            shape(rows_here, model_width),
            shape(2, owned, wide),
            shape(8, 128, kind=F32),
        ]
        + [shape(4, rows_here, owned)]
        + [shape(2, rows_here, owned)] * (groups - 2),
        scratch_shapes=[
            pltpu.VMEM((2, owned, hidden_units), BF16),
            pltpu.SemaphoreType.DMA((2, 3)),
        ],
        compiler_params=params(got, expert_weights, expert_weights),
    )(got, expert_weights, near)
    partial, rows, grads, near_pairs, token = outs[:5]
    slices = list(outs[5:])
    slices = slices[:1] + [swap(slices[b - 1], b) for b in range(1, groups)]

    arrived = pl.pallas_call(
        keep_kernel,
        in_specs=[anywhere] * (len(far) + 1),
        out_specs=[anywhere] * len(far),
        out_shape=[shape(*expert_weights.shape)] * len(far),
        input_output_aliases={at + 1: at for at in range(len(far))},
        compiler_params=params(),
        cost_estimate=cost(10**11, 10**8),
    )(token, *arriving)
    last = [swap(value, 1) for value in arrived]
    partial, far_pairs = pl.pallas_call(
        lambda *refs: far_kernel(groups, *refs),
        in_specs=[pl.BlockSpec()] * 3 + [anywhere] * len(far),
        out_shape=(shape(rows_here, 3 * hidden_units, kind=F32), shape(len(far), owned, wide)),
        scratch_shapes=[
            pltpu.VMEM((len(far), owned, hidden_units), BF16),
            pltpu.SemaphoreType.DMA((len(far), 3)),
        ],
        compiler_params=params(rows, grads, *arrived, *arrived),
    )(rows, grads, partial, *arrived)

    acts, back = pl.pallas_call(
        lambda *refs: back_kernel(groups, *refs),
        out_shape=(shape(rows_here, 3 * hidden_units), shape(window, padded, WIDE)),
        scratch_shapes=[pltpu.VMEM((rows_here, model_width), F32)],
        compiler_params=params(rows, grads, partial, near_pairs, far_pairs, *last),
        cost_estimate=cost(10**6, 10**5),
    )(rows, grads, partial, near_pairs, far_pairs, *last)
    returned = lax.all_to_all(back, "expert", split_axis=0, concat_axis=0, tiled=True)

    every = slices + [acts] + [swap(acts, b) for b in range(1, groups)]
    weight_grads = pl.pallas_call(
        lambda *refs: grads_kernel(groups, *refs),
        out_specs=anywhere,
        out_shape=shape(1, 3, owned, hidden_units, kind=F32),
        scratch_shapes=[
            pltpu.VMEM((3, owned, hidden_units), F32),
            pltpu.SemaphoreType.DMA((3,)),
        ],
        compiler_params=params(*every, expert_weights, expert_weights),
        cost_estimate=cost(6 * groups * rows_here * owned * hidden_units, 12 * owned * hidden_units),
    )(*every)

    token_grads = pl.pallas_call(
        combine_kernel,
        out_specs=anywhere,
        out_shape=shape(token_rows, model_width),
        scratch_shapes=[pltpu.VMEM((token_rows, model_width), BF16), pltpu.SemaphoreType.DMA((2,))],
        compiler_params=params(table, back, tokens),
    )(returned, table)
    return (token_grads, weight_grads)


def solution(mesh):
    lines = P(("dp", "expert"), None)
    slabs = P("expert", None, "dp", None)
    return jax.shard_map(
        on_device,
        mesh=mesh,
        in_specs=(lines, lines, lines, lines, slabs),
        out_specs=(lines, slabs),
        check_vma=False,
    )
```

```python
import jax
import jax.numpy as jnp
from jax import lax
from jax.experimental import pallas as pl
from jax.experimental.pallas import tpu as pltpu
from jax.sharding import PartitionSpec as P

SLOTS = 10
WIDE = 512
JOIN = 4
F32 = jnp.float32
BF16 = jnp.bfloat16


def dot(first_op, second_op):
    return jnp.dot(first_op, second_op, preferred_element_type=F32)


def dot_tn(first_op, second_op):
    return lax.dot_general(first_op, second_op, (((0,), (0,)), ((), ())), preferred_element_type=F32)


def dot_nt(first_op, second_op):
    return lax.dot_general(first_op, second_op, (((1,), (1,)), ((), ())), preferred_element_type=F32)


def swap(value, bits):
    return lax.ppermute(value, "dp", [(i, i ^ bits) for i in range(lax.axis_size("dp"))])


def piece_rows(chunks):
    return -(-chunks * SLOTS // 8) * 8


def params(*arrays):
    moved = sum(a.size * a.dtype.itemsize for a in arrays)
    return pltpu.CompilerParams(vmem_limit_bytes=min(56 * 2**20, 6 * 2**20 + 3 * moved // 2))


def cost(flops, moved):
    return pl.CostEstimate(flops=flops, bytes_accessed=moved, transcendentals=0)


def shape(*extent, kind=BF16):
    return jax.ShapeDtypeStruct(extent, kind)


def lower(value, by):
    return jnp.floor((value + 0.5) * (1.0 / by))


def sort_matrix(parts, chunks, transposed):
    padded = piece_rows(chunks)
    wide, tall = JOIN * parts * padded, parts * chunks * JOIN * SLOTS
    extent, axis = ((wide, tall), 0) if transposed else ((tall, wide), 1)
    line = (wide, 1) if transposed else (1, wide)
    place = lax.broadcasted_iota(jnp.int32, line, axis).astype(F32)
    block = lower(place, padded)
    inside = place - block * padded
    source = lower(block, parts)
    part = block - source * parts
    chunk = lower(inside, SLOTS)
    slot = inside - chunk * SLOTS
    target = ((part * chunks + chunk) * JOIN + source) * SLOTS + slot
    target = jnp.where(chunk < chunks, target, -1.0)
    spots = lax.broadcasted_iota(jnp.int32, extent, 1 - axis).astype(F32)
    return jnp.where(spots == target, 1.0, 0.0).astype(BF16)


def table_of(code, values, chunks, padded):
    window, token_rows = code.shape
    spots = lax.broadcasted_iota(jnp.int32, (padded, chunks * token_rows), 0).astype(F32)
    tables = []
    for expert in range(window):
        own = code[expert : expert + 1]
        hit = spots == jnp.concatenate([own + float(SLOTS * c) for c in range(chunks)], axis=1)
        row = []
        for value in values:
            if value is None:
                row.append(jnp.where(hit, 1.0, 0.0))
            else:
                gate = jnp.concatenate([value[expert : expert + 1]] * chunks, axis=1)
                row.append(jnp.where(hit, gate, 0.0))
        tables.append(row)
    return [jnp.concatenate([t[i] for t in tables], axis=0) for i in range(len(values))]


def token_kernel(token_ref):
    token_ref[...] = jnp.zeros_like(token_ref)


def pack_kernel(ids_ref, gates_ref, tokens_ref, grads_ref, _, sent_ref, code_ref):
    token_rows, model_width = tokens_ref.shape
    window = code_ref.shape[0]
    chunks = model_width // WIDE
    padded = piece_rows(chunks)
    above = lax.broadcasted_iota(jnp.int32, (token_rows, token_rows), 0)
    along = lax.broadcasted_iota(jnp.int32, (token_rows, token_rows), 1)
    earlier = jnp.where(above < along, 1.0, 0.0).astype(BF16)
    ids = ids_ref[...]
    gates = gates_ref[...].astype(F32)
    members, chosen = [], []
    for expert in range(window):
        hit = ids == expert
        members.append(jnp.sum(jnp.where(hit, 1.0, 0.0), axis=0, keepdims=True))
        chosen.append(jnp.sum(jnp.where(hit, gates, 0.0), axis=0, keepdims=True))
    members = jnp.concatenate(members, axis=0)
    chosen = jnp.concatenate(chosen, axis=0)
    code = jnp.where(members > 0.0, dot(members.astype(BF16), earlier), -1e6)
    code_ref[...] = code
    table, gated = table_of(code, [None, chosen], chunks, padded)

    def columns(ref):
        return jnp.concatenate([ref[:, c * WIDE : (c + 1) * WIDE] for c in range(chunks)], axis=0)

    rows = dot(table.astype(BF16), columns(tokens_ref))
    grads = dot(gated.astype(BF16), columns(grads_ref))
    for expert in range(window):
        lines = slice(expert * padded, (expert + 1) * padded)
        sent_ref[expert] = jnp.concatenate([rows[lines], grads[lines]], axis=0).astype(BF16)


def table_kernel(chunks, code_ref, table_ref):
    (table,) = table_of(code_ref[...], [None], chunks, piece_rows(chunks))
    table_ref[...] = table.T.astype(BF16)


def part_kernel(acts_ref, *refs):
    hidden_units = acts_ref.shape[1] // 3
    for at, ref in enumerate(refs[-3:]):
        ref[...] = acts_ref[:, at * hidden_units : (at + 1) * hidden_units]


def keep_kernel(*refs):
    pass


def place(source, pair_ref, down_ref, sems, at):
    hidden_units = down_ref.shape[1]
    moves = [
        (source.at[0], pair_ref.at[:, pl.ds(0, hidden_units)]),
        (source.at[1], pair_ref.at[:, pl.ds(hidden_units, hidden_units)]),
        (source.at[2], down_ref),
    ]
    return [
        pltpu.make_async_copy(start, end, sems.at[at, which]) for which, (start, end) in enumerate(moves)
    ]


def partial_kernel(groups, got_ref, own_in, near_in, *refs):
    (out_ref, rows_ref, grads_ref, pair_ref, token_ref), refs = refs[:5], refs[5:]
    slices_refs, (down_ref, sems) = refs[: groups - 1], refs[groups - 1 :]
    copies = [
        copy
        for b, source in enumerate((own_in.at[0], near_in.at[0]))
        for copy in place(source, pair_ref.at[b], down_ref.at[b], sems, b)
    ]
    for copy in copies:
        copy.start()
    token_ref[...] = jnp.zeros_like(token_ref)
    sources, height, _ = got_ref.shape
    model_width = rows_ref.shape[1]
    chunks = model_width // WIDE
    owned = model_width // groups
    joined = sources // JOIN
    tall = JOIN * SLOTS
    blocks = jnp.concatenate(
        [got_ref[q * JOIN : (q + 1) * JOIN].reshape(JOIN * height, WIDE) for q in range(joined)],
        axis=1,
    )
    lines = dot(sort_matrix(2, chunks, False), blocks)

    def gathered(part):
        return jnp.concatenate(
            [
                jnp.concatenate(
                    [
                        lines[
                            (part * chunks + c) * tall : (part * chunks + c + 1) * tall,
                            q * WIDE : (q + 1) * WIDE,
                        ]
                        for c in range(chunks)
                    ],
                    axis=1,
                )
                for q in range(joined)
            ],
            axis=0,
        ).astype(BF16)

    rows_ref[...] = gathered(0)
    grads_ref[...] = gathered(1)
    me = lax.axis_index("dp")
    wide = pair_ref.shape[2]
    for copy in copies:
        copy.wait()
    pair_sum, down_sum = None, None
    for b in range(groups):
        lanes = pl.ds(pl.multiple_of((me ^ b) * owned, 128), owned)
        rows, grads = rows_ref[:, lanes], grads_ref[:, lanes]
        target, first = (slices_refs[0], 2) if b == 0 else (slices_refs[b - 1], 0)
        target[first] = rows
        target[first + 1] = grads
        if b < 2:
            term = dot(rows, pair_ref[b])
            pair_sum = term if pair_sum is None else pair_sum + term
            term = dot(grads, down_ref[b])
            down_sum = term if down_sum is None else down_sum + term
    out_ref[:, :wide] = pair_sum
    out_ref[:, wide:] = down_sum


def lanes_of(owner, owned):
    return pl.ds(pl.multiple_of(owner * owned, 128), owned)


def far_kernel(groups, rows_ref, grads_ref, partial_ref, *refs):
    far = range(2, groups, 2)
    weights_in, (out_ref, pair_ref, down_ref, sems) = refs[: len(far)], refs[len(far) :]
    copies = [
        place(source.at[0], pair_ref.at[at], down_ref.at[at], sems, at)
        for at, source in enumerate(weights_in)
    ]
    for some in copies:
        for copy in some:
            copy.start()
    me = lax.axis_index("dp")
    owned, wide = pair_ref.shape[1:]
    pair_sum, down_sum = partial_ref[:, :wide], partial_ref[:, wide:]
    for at, b in enumerate(far):
        for copy in copies[at]:
            copy.wait()
        lanes = lanes_of(me ^ b, owned)
        pair_sum = pair_sum + dot(rows_ref[:, lanes], pair_ref[at])
        down_sum = down_sum + dot(grads_ref[:, lanes], down_ref[at])
    out_ref[:, :wide] = pair_sum
    out_ref[:, wide:] = down_sum


def back_kernel(groups, rows_ref, grads_ref, partial_ref, near_ref, far_ref, *refs):
    last_refs, (acts_ref, out_ref, back_ref) = refs[:-3], refs[-3:]
    me = lax.axis_index("dp")
    model_width = grads_ref.shape[1]
    owned = model_width // groups
    chunks = model_width // WIDE
    hidden_units = partial_ref.shape[1] // 3
    wide = 2 * hidden_units

    def lanes(b):
        return lanes_of(me ^ b, owned)

    gate_act = partial_ref[:, :hidden_units]
    up_act = partial_ref[:, hidden_units:wide]
    grad_hidden = partial_ref[:, wide:]
    for at, ref in enumerate(last_refs):
        here = lanes(2 * at + 3)
        gate_act = gate_act + dot(rows_ref[:, here], ref[0, 0])
        up_act = up_act + dot(rows_ref[:, here], ref[0, 1])
        grad_hidden = grad_hidden + dot(grads_ref[:, here], ref[0, 2])
    logistic = jax.nn.sigmoid(gate_act)
    swish_out = gate_act * logistic
    hidden = (swish_out * up_act).astype(BF16)
    grad_up = (grad_hidden * swish_out).astype(BF16)
    grad_gate = (grad_hidden * up_act * logistic * (1.0 + gate_act * (1.0 - logistic))).astype(BF16)
    acts = jnp.concatenate([grad_gate, grad_up], axis=1)
    acts_ref[:, :wide] = acts
    acts_ref[:, wide:] = hidden
    for b in range(groups):
        if b < 2:
            term = dot_nt(acts, near_ref[b])
        elif b % 2 == 0:
            term = dot_nt(acts, far_ref[b // 2 - 1])
        else:
            ref = last_refs[b // 2 - 1]
            term = dot_nt(grad_gate, ref[0, 0]) + dot_nt(grad_up, ref[0, 1])
        back_ref[:, lanes(b)] = term
    tall = JOIN * SLOTS
    joined = grads_ref.shape[0] // tall
    lines = jnp.concatenate(
        [
            jnp.concatenate(
                [
                    back_ref[q * tall : (q + 1) * tall, c * WIDE : (c + 1) * WIDE]
                    for c in range(chunks)
                ],
                axis=0,
            )
            for q in range(joined)
        ],
        axis=1,
    ).astype(BF16)
    blocks = dot(sort_matrix(1, chunks, True), lines)
    height = piece_rows(chunks)
    for q in range(joined):
        for j in range(JOIN):
            part = blocks[j * height : (j + 1) * height, q * WIDE : (q + 1) * WIDE]
            out_ref[q * JOIN + j] = part.astype(BF16)


def combine_kernel(returned_ref, table_ref, out_ref, held_ref, sems):
    token_rows, model_width = held_ref.shape
    window, height, _ = returned_ref.shape
    lines = returned_ref[...].astype(F32).reshape(window * height, WIDE).astype(BF16)
    parts = sems.shape[0]
    chunks = model_width // WIDE // parts
    copies = []
    for part in range(parts):
        table = table_ref[part * chunks * token_rows : (part + 1) * chunks * token_rows]
        result = dot(table, lines).astype(BF16)
        for c in range(chunks):
            at = part * chunks + c
            held_ref[:, at * WIDE : (at + 1) * WIDE] = result[c * token_rows : (c + 1) * token_rows]
        lanes = pl.ds(part * chunks * WIDE, chunks * WIDE)
        copies.append(
            pltpu.make_async_copy(held_ref.at[:, lanes], out_ref.at[:, lanes], sems.at[part])
        )
        copies[-1].start()
    for copy in copies:
        copy.wait()


def grads_kernel(groups, *refs):
    slices_refs, acts_refs, (out_ref, held_ref, sems) = refs[:groups], refs[groups:-3], refs[-3:]
    hidden_units = out_ref.shape[3]
    copies = [pltpu.make_async_copy(held_ref.at[at], out_ref.at[0, at], sems.at[at]) for at in range(3)]
    rows_here = acts_refs[0].shape[0]
    step = max(1, min(groups, 640 // rows_here))
    for at in range(3):
        lanes = slice(at * hidden_units, (at + 1) * hidden_units)
        kind = 0 if at < 2 else 1
        places = [kind + 2 if b == 0 else kind for b in range(groups)]
        total = None
        for first in range(0, groups, step):
            some = range(first, first + step)
            rows = jnp.concatenate([slices_refs[b][places[b]] for b in some], axis=0)
            acts = jnp.concatenate(
                [
                    acts_refs[b][:, lanes] if b < 2 else acts_refs[2 + 3 * (b - 2) + at][...]
                    for b in some
                ],
                axis=0,
            )
            term = dot_tn(rows, acts)
            total = term if total is None else total + term
        held_ref[at] = total
        copies[at].start()
    for copy in copies:
        copy.wait()


def on_device(tokens, out_grad, expert_ids, gates, expert_weights):
    window = lax.axis_size("expert")
    groups = lax.axis_size("dp")
    token_rows, model_width = tokens.shape
    hidden_units = expert_weights.shape[3]
    owned = model_width // groups
    chunks = model_width // WIDE
    padded = piece_rows(chunks)
    rows_here = window * SLOTS
    wide = 2 * hidden_units
    anywhere = pl.BlockSpec(memory_space=pl.ANY)

    far = list(range(2, groups, 2))
    token = pl.pallas_call(
        token_kernel,
        out_shape=shape(8, 128, kind=F32),
        compiler_params=params(),
        cost_estimate=cost(10**11, 10**8),
    )()
    arriving = [swap(expert_weights, b) for b in far]
    near = swap(expert_weights, 1)

    ids_t, gates_t = expert_ids.T, gates.T
    sent, code = pl.pallas_call(
        pack_kernel,
        out_shape=(
            shape(window, 2 * padded, WIDE),
            shape(window, token_rows, kind=F32),
        ),
        compiler_params=params(tokens, out_grad),
    )(ids_t, gates_t, tokens, out_grad, token)

    got = lax.all_to_all(sent, "expert", split_axis=0, concat_axis=0, tiled=True)
    table = pl.pallas_call(
        lambda *refs: table_kernel(chunks, *refs),
        out_shape=shape(chunks * token_rows, window * padded),
        compiler_params=params(),
        cost_estimate=cost(10**6, 10**5),
    )(code)

    outs = pl.pallas_call(
        lambda *refs: partial_kernel(groups, *refs),
        in_specs=[pl.BlockSpec()] + [anywhere] * 2,
        out_shape=[
            shape(rows_here, 3 * hidden_units, kind=F32),
            shape(rows_here, model_width),
            shape(rows_here, model_width),
            shape(2, owned, wide),
            shape(8, 128, kind=F32),
        ]
        + [shape(4, rows_here, owned)]
        + [shape(2, rows_here, owned)] * (groups - 2),
        scratch_shapes=[
            pltpu.VMEM((2, owned, hidden_units), BF16),
            pltpu.SemaphoreType.DMA((2, 3)),
        ],
        compiler_params=params(got, expert_weights, expert_weights),
    )(got, expert_weights, near)
    partial, rows, grads, near_pairs, token = outs[:5]
    slices = list(outs[5:])
    slices = slices[:1] + [swap(slices[b - 1], b) for b in range(1, groups)]

    arrived = pl.pallas_call(
        keep_kernel,
        in_specs=[anywhere] * (len(far) + 1),
        out_specs=[anywhere] * len(far),
        out_shape=[shape(*expert_weights.shape)] * len(far),
        input_output_aliases={at + 1: at for at in range(len(far))},
        compiler_params=params(),
        cost_estimate=cost(10**11, 10**8),
    )(token, *arriving)
    last = [swap(value, 1) for value in arrived]
    partial, far_pairs = pl.pallas_call(
        lambda *refs: far_kernel(groups, *refs),
        in_specs=[pl.BlockSpec()] * 3 + [anywhere] * len(far),
        out_shape=(shape(rows_here, 3 * hidden_units, kind=F32), shape(len(far), owned, wide)),
        scratch_shapes=[
            pltpu.VMEM((len(far), owned, hidden_units), BF16),
            pltpu.SemaphoreType.DMA((len(far), 3)),
        ],
        compiler_params=params(rows, grads, *arrived, *arrived),
    )(rows, grads, partial, *arrived)

    acts, back = pl.pallas_call(
        lambda *refs: back_kernel(groups, *refs),
        out_shape=(shape(rows_here, 3 * hidden_units), shape(window, padded, WIDE)),
        scratch_shapes=[pltpu.VMEM((rows_here, model_width), F32)],
        compiler_params=params(rows, grads, partial, near_pairs, far_pairs, *last),
        cost_estimate=cost(10**6, 10**5),
    )(rows, grads, partial, near_pairs, far_pairs, *last)
    returned = lax.all_to_all(back, "expert", split_axis=0, concat_axis=0, tiled=True)

    later = pl.pallas_call(
        token_kernel,
        out_shape=shape(16, 128, kind=F32),
        compiler_params=params(),
        cost_estimate=cost(10**11, 10**8),
    )()
    parts = pl.pallas_call(
        part_kernel,
        in_specs=[pl.BlockSpec()] + [anywhere] * groups,
        out_shape=[shape(rows_here, hidden_units)] * 3,
        compiler_params=params(acts, acts),
        cost_estimate=cost(10**6, 10**5),
    )(acts, later, *slices[1:])
    every = slices + [acts, swap(acts, 1)]
    for b in far:
        over = [swap(part, b) for part in parts]
        every += over + [swap(part, 1) for part in over]
    weight_grads = pl.pallas_call(
        lambda *refs: grads_kernel(groups, *refs),
        out_specs=anywhere,
        out_shape=shape(1, 3, owned, hidden_units, kind=F32),
        scratch_shapes=[
            pltpu.VMEM((3, owned, hidden_units), F32),
            pltpu.SemaphoreType.DMA((3,)),
        ],
        compiler_params=params(*every, expert_weights, expert_weights),
        cost_estimate=cost(6 * groups * rows_here * owned * hidden_units, 12 * owned * hidden_units),
    )(*every)

    token_grads = pl.pallas_call(
        combine_kernel,
        out_specs=anywhere,
        out_shape=shape(token_rows, model_width),
        scratch_shapes=[pltpu.VMEM((token_rows, model_width), BF16), pltpu.SemaphoreType.DMA((2,))],
        compiler_params=params(table, back, tokens),
    )(returned, table)
    return (token_grads, weight_grads)


def solution(mesh):
    lines = P(("dp", "expert"), None)
    slabs = P("expert", None, "dp", None)
    return jax.shard_map(
        on_device,
        mesh=mesh,
        in_specs=(lines, lines, lines, lines, slabs),
        out_specs=(lines, slabs),
        check_vma=False,
    )
```

```python
import jax
import jax.numpy as jnp
from jax import lax
from jax.experimental import pallas as pl
from jax.experimental.pallas import tpu as pltpu
from jax.sharding import PartitionSpec as P

SLOTS = 10
WIDE = 512
JOIN = 4
F32 = jnp.float32
BF16 = jnp.bfloat16


def dot(first_op, second_op):
    return jnp.dot(first_op, second_op, preferred_element_type=F32)


def dot_tn(first_op, second_op):
    return lax.dot_general(first_op, second_op, (((0,), (0,)), ((), ())), preferred_element_type=F32)


def dot_nt(first_op, second_op):
    return lax.dot_general(first_op, second_op, (((1,), (1,)), ((), ())), preferred_element_type=F32)


def swap(value, bits):
    return lax.ppermute(value, "dp", [(i, i ^ bits) for i in range(lax.axis_size("dp"))])


def piece_rows(chunks):
    return -(-chunks * SLOTS // 8) * 8


def params(*arrays):
    moved = sum(a.size * a.dtype.itemsize for a in arrays)
    return pltpu.CompilerParams(vmem_limit_bytes=min(56 * 2**20, 6 * 2**20 + 3 * moved // 2))


def cost(flops, moved):
    return pl.CostEstimate(flops=flops, bytes_accessed=moved, transcendentals=0)


def shape(*extent, kind=BF16):
    return jax.ShapeDtypeStruct(extent, kind)


def lower(value, by):
    return jnp.floor((value + 0.5) * (1.0 / by))


def sort_matrix(parts, chunks, transposed):
    padded = piece_rows(chunks)
    wide, tall = JOIN * parts * padded, parts * chunks * JOIN * SLOTS
    extent, axis = ((wide, tall), 0) if transposed else ((tall, wide), 1)
    line = (wide, 1) if transposed else (1, wide)
    place = lax.broadcasted_iota(jnp.int32, line, axis).astype(F32)
    block = lower(place, padded)
    inside = place - block * padded
    source = lower(block, parts)
    part = block - source * parts
    chunk = lower(inside, SLOTS)
    slot = inside - chunk * SLOTS
    target = ((part * chunks + chunk) * JOIN + source) * SLOTS + slot
    target = jnp.where(chunk < chunks, target, -1.0)
    spots = lax.broadcasted_iota(jnp.int32, extent, 1 - axis).astype(F32)
    return jnp.where(spots == target, 1.0, 0.0).astype(BF16)


def table_of(code, values, chunks, padded):
    window, token_rows = code.shape
    spots = lax.broadcasted_iota(jnp.int32, (padded, chunks * token_rows), 0).astype(F32)
    tables = []
    for expert in range(window):
        own = code[expert : expert + 1]
        hit = spots == jnp.concatenate([own + float(SLOTS * c) for c in range(chunks)], axis=1)
        row = []
        for value in values:
            if value is None:
                row.append(jnp.where(hit, 1.0, 0.0))
            else:
                gate = jnp.concatenate([value[expert : expert + 1]] * chunks, axis=1)
                row.append(jnp.where(hit, gate, 0.0))
        tables.append(row)
    return [jnp.concatenate([t[i] for t in tables], axis=0) for i in range(len(values))]


def token_kernel(token_ref):
    token_ref[...] = jnp.zeros_like(token_ref)


def pack_kernel(ids_ref, gates_ref, tokens_ref, grads_ref, _, sent_ref, code_ref):
    token_rows, model_width = tokens_ref.shape
    window = code_ref.shape[0]
    chunks = model_width // WIDE
    padded = piece_rows(chunks)
    above = lax.broadcasted_iota(jnp.int32, (token_rows, token_rows), 0)
    along = lax.broadcasted_iota(jnp.int32, (token_rows, token_rows), 1)
    earlier = jnp.where(above < along, 1.0, 0.0).astype(BF16)
    ids = ids_ref[...]
    gates = gates_ref[...].astype(F32)
    members, chosen = [], []
    for expert in range(window):
        hit = ids == expert
        members.append(jnp.sum(jnp.where(hit, 1.0, 0.0), axis=0, keepdims=True))
        chosen.append(jnp.sum(jnp.where(hit, gates, 0.0), axis=0, keepdims=True))
    members = jnp.concatenate(members, axis=0)
    chosen = jnp.concatenate(chosen, axis=0)
    code = jnp.where(members > 0.0, dot(members.astype(BF16), earlier), -1e6)
    code_ref[...] = code
    table, gated = table_of(code, [None, chosen], chunks, padded)

    def columns(ref):
        return jnp.concatenate([ref[:, c * WIDE : (c + 1) * WIDE] for c in range(chunks)], axis=0)

    rows = dot(table.astype(BF16), columns(tokens_ref))
    grads = dot(gated.astype(BF16), columns(grads_ref))
    for expert in range(window):
        lines = slice(expert * padded, (expert + 1) * padded)
        sent_ref[expert] = jnp.concatenate([rows[lines], grads[lines]], axis=0).astype(BF16)


def table_kernel(chunks, code_ref, table_ref):
    (table,) = table_of(code_ref[...], [None], chunks, piece_rows(chunks))
    table_ref[...] = table.T.astype(BF16)


def part_kernel(acts_ref, *refs):
    wide = refs[-2].shape[1]
    refs[-2][...] = acts_ref[:, :wide]
    refs[-1][...] = acts_ref[:, wide:]


def keep_kernel(*refs):
    pass


def place(source, pair_ref, down_ref, sems, at):
    hidden_units = down_ref.shape[1]
    moves = [
        (source.at[0], pair_ref.at[:, pl.ds(0, hidden_units)]),
        (source.at[1], pair_ref.at[:, pl.ds(hidden_units, hidden_units)]),
        (source.at[2], down_ref),
    ]
    return [
        pltpu.make_async_copy(start, end, sems.at[at, which]) for which, (start, end) in enumerate(moves)
    ]


def partial_kernel(groups, got_ref, own_in, near_in, *refs):
    (out_ref, rows_ref, grads_ref, pair_ref, token_ref), refs = refs[:5], refs[5:]
    slices_refs, (down_ref, sems) = refs[: groups - 1], refs[groups - 1 :]
    copies = [
        copy
        for b, source in enumerate((own_in.at[0], near_in.at[0]))
        for copy in place(source, pair_ref.at[b], down_ref.at[b], sems, b)
    ]
    for copy in copies:
        copy.start()
    token_ref[...] = jnp.zeros_like(token_ref)
    sources, height, _ = got_ref.shape
    model_width = rows_ref.shape[1]
    chunks = model_width // WIDE
    owned = model_width // groups
    joined = sources // JOIN
    tall = JOIN * SLOTS
    blocks = jnp.concatenate(
        [got_ref[q * JOIN : (q + 1) * JOIN].reshape(JOIN * height, WIDE) for q in range(joined)],
        axis=1,
    )
    lines = dot(sort_matrix(2, chunks, False), blocks)

    def gathered(part):
        return jnp.concatenate(
            [
                jnp.concatenate(
                    [
                        lines[
                            (part * chunks + c) * tall : (part * chunks + c + 1) * tall,
                            q * WIDE : (q + 1) * WIDE,
                        ]
                        for c in range(chunks)
                    ],
                    axis=1,
                )
                for q in range(joined)
            ],
            axis=0,
        ).astype(BF16)

    rows_ref[...] = gathered(0)
    grads_ref[...] = gathered(1)
    me = lax.axis_index("dp")
    wide = pair_ref.shape[2]
    for copy in copies:
        copy.wait()
    pair_sum, down_sum = None, None
    for b in range(groups):
        lanes = pl.ds(pl.multiple_of((me ^ b) * owned, 128), owned)
        rows, grads = rows_ref[:, lanes], grads_ref[:, lanes]
        target, first = (slices_refs[0], 2) if b == 0 else (slices_refs[b - 1], 0)
        target[first] = rows
        target[first + 1] = grads
        if b < 2:
            term = dot(rows, pair_ref[b])
            pair_sum = term if pair_sum is None else pair_sum + term
            term = dot(grads, down_ref[b])
            down_sum = term if down_sum is None else down_sum + term
    out_ref[:, :wide] = pair_sum
    out_ref[:, wide:] = down_sum


def lanes_of(owner, owned):
    return pl.ds(pl.multiple_of(owner * owned, 128), owned)


def far_kernel(groups, rows_ref, grads_ref, partial_ref, *refs):
    far = range(2, groups, 2)
    weights_in, (out_ref, pair_ref, down_ref, sems) = refs[: len(far)], refs[len(far) :]
    copies = [
        place(source.at[0], pair_ref.at[at], down_ref.at[at], sems, at)
        for at, source in enumerate(weights_in)
    ]
    for some in copies:
        for copy in some:
            copy.start()
    me = lax.axis_index("dp")
    owned, wide = pair_ref.shape[1:]
    pair_sum, down_sum = partial_ref[:, :wide], partial_ref[:, wide:]
    for at, b in enumerate(far):
        for copy in copies[at]:
            copy.wait()
        lanes = lanes_of(me ^ b, owned)
        pair_sum = pair_sum + dot(rows_ref[:, lanes], pair_ref[at])
        down_sum = down_sum + dot(grads_ref[:, lanes], down_ref[at])
    out_ref[:, :wide] = pair_sum
    out_ref[:, wide:] = down_sum


def back_kernel(groups, rows_ref, grads_ref, partial_ref, near_ref, far_ref, *refs):
    last_refs, (acts_ref, out_ref, back_ref) = refs[:-3], refs[-3:]
    me = lax.axis_index("dp")
    model_width = grads_ref.shape[1]
    owned = model_width // groups
    chunks = model_width // WIDE
    hidden_units = partial_ref.shape[1] // 3
    wide = 2 * hidden_units

    def lanes(b):
        return lanes_of(me ^ b, owned)

    gate_act = partial_ref[:, :hidden_units]
    up_act = partial_ref[:, hidden_units:wide]
    grad_hidden = partial_ref[:, wide:]
    for at, ref in enumerate(last_refs):
        here = lanes(2 * at + 3)
        gate_act = gate_act + dot(rows_ref[:, here], ref[0, 0])
        up_act = up_act + dot(rows_ref[:, here], ref[0, 1])
        grad_hidden = grad_hidden + dot(grads_ref[:, here], ref[0, 2])
    logistic = jax.nn.sigmoid(gate_act)
    swish_out = gate_act * logistic
    hidden = (swish_out * up_act).astype(BF16)
    grad_up = (grad_hidden * swish_out).astype(BF16)
    grad_gate = (grad_hidden * up_act * logistic * (1.0 + gate_act * (1.0 - logistic))).astype(BF16)
    acts = jnp.concatenate([grad_gate, grad_up], axis=1)
    acts_ref[:, :wide] = acts
    acts_ref[:, wide:] = hidden
    for b in range(groups):
        if b < 2:
            term = dot_nt(acts, near_ref[b])
        elif b % 2 == 0:
            term = dot_nt(acts, far_ref[b // 2 - 1])
        else:
            ref = last_refs[b // 2 - 1]
            term = dot_nt(grad_gate, ref[0, 0]) + dot_nt(grad_up, ref[0, 1])
        back_ref[:, lanes(b)] = term
    tall = JOIN * SLOTS
    joined = grads_ref.shape[0] // tall
    lines = jnp.concatenate(
        [
            jnp.concatenate(
                [
                    back_ref[q * tall : (q + 1) * tall, c * WIDE : (c + 1) * WIDE]
                    for c in range(chunks)
                ],
                axis=0,
            )
            for q in range(joined)
        ],
        axis=1,
    ).astype(BF16)
    blocks = dot(sort_matrix(1, chunks, True), lines)
    height = piece_rows(chunks)
    for q in range(joined):
        for j in range(JOIN):
            part = blocks[j * height : (j + 1) * height, q * WIDE : (q + 1) * WIDE]
            out_ref[q * JOIN + j] = part.astype(BF16)


def combine_kernel(returned_ref, table_ref, out_ref, held_ref, sems):
    token_rows, model_width = held_ref.shape
    window, height, _ = returned_ref.shape
    lines = returned_ref[...].astype(F32).reshape(window * height, WIDE).astype(BF16)
    parts = sems.shape[0]
    chunks = model_width // WIDE // parts
    copies = []
    for part in range(parts):
        table = table_ref[part * chunks * token_rows : (part + 1) * chunks * token_rows]
        result = dot(table, lines).astype(BF16)
        for c in range(chunks):
            at = part * chunks + c
            held_ref[:, at * WIDE : (at + 1) * WIDE] = result[c * token_rows : (c + 1) * token_rows]
        lanes = pl.ds(part * chunks * WIDE, chunks * WIDE)
        copies.append(
            pltpu.make_async_copy(held_ref.at[:, lanes], out_ref.at[:, lanes], sems.at[part])
        )
        copies[-1].start()
    for copy in copies:
        copy.wait()


def grads_kernel(groups, *refs):
    slices_refs, acts_refs, (out_ref, held_ref, sems) = refs[:groups], refs[groups:-3], refs[-3:]
    hidden_units = out_ref.shape[3]
    copies = [pltpu.make_async_copy(held_ref.at[at], out_ref.at[0, at], sems.at[at]) for at in range(3)]
    rows_here = acts_refs[0].shape[0]
    step = max(1, min(groups, 640 // rows_here))
    for at in range(3):
        lanes = slice(at * hidden_units, (at + 1) * hidden_units)
        kind = 0 if at < 2 else 1
        places = [kind + 2 if b == 0 else kind for b in range(groups)]
        total = None
        for first in range(0, groups, step):
            some = range(first, first + step)
            rows = jnp.concatenate([slices_refs[b][places[b]] for b in some], axis=0)
            acts = jnp.concatenate(
                [
                    acts_refs[2 * b][:, lanes] if at < 2 else acts_refs[2 * b + 1][...]
                    for b in some
                ],
                axis=0,
            )
            term = dot_tn(rows, acts)
            total = term if total is None else total + term
        held_ref[at] = total
        copies[at].start()
    for copy in copies:
        copy.wait()


def on_device(tokens, out_grad, expert_ids, gates, expert_weights):
    window = lax.axis_size("expert")
    groups = lax.axis_size("dp")
    token_rows, model_width = tokens.shape
    hidden_units = expert_weights.shape[3]
    owned = model_width // groups
    chunks = model_width // WIDE
    padded = piece_rows(chunks)
    rows_here = window * SLOTS
    wide = 2 * hidden_units
    anywhere = pl.BlockSpec(memory_space=pl.ANY)

    far = list(range(2, groups, 2))
    token = pl.pallas_call(
        token_kernel,
        out_shape=shape(8, 128, kind=F32),
        compiler_params=params(),
        cost_estimate=cost(10**11, 10**8),
    )()
    arriving = [swap(expert_weights, b) for b in far]
    near = swap(expert_weights, 1)

    ids_t, gates_t = expert_ids.T, gates.T
    sent, code = pl.pallas_call(
        pack_kernel,
        out_shape=(
            shape(window, 2 * padded, WIDE),
            shape(window, token_rows, kind=F32),
        ),
        compiler_params=params(tokens, out_grad),
    )(ids_t, gates_t, tokens, out_grad, token)

    got = lax.all_to_all(sent, "expert", split_axis=0, concat_axis=0, tiled=True)
    table = pl.pallas_call(
        lambda *refs: table_kernel(chunks, *refs),
        out_shape=shape(chunks * token_rows, window * padded),
        compiler_params=params(),
        cost_estimate=cost(10**6, 10**5),
    )(code)

    outs = pl.pallas_call(
        lambda *refs: partial_kernel(groups, *refs),
        in_specs=[pl.BlockSpec()] + [anywhere] * 2,
        out_shape=[
            shape(rows_here, 3 * hidden_units, kind=F32),
            shape(rows_here, model_width),
            shape(rows_here, model_width),
            shape(2, owned, wide),
            shape(8, 128, kind=F32),
        ]
        + [shape(4, rows_here, owned)]
        + [shape(2, rows_here, owned)] * (groups - 2),
        scratch_shapes=[
            pltpu.VMEM((2, owned, hidden_units), BF16),
            pltpu.SemaphoreType.DMA((2, 3)),
        ],
        compiler_params=params(got, expert_weights, expert_weights),
    )(got, expert_weights, near)
    partial, rows, grads, near_pairs, token = outs[:5]
    slices = list(outs[5:])
    slices = slices[:1] + [swap(slices[b - 1], b) for b in range(1, groups)]

    arrived = pl.pallas_call(
        keep_kernel,
        in_specs=[anywhere] * (len(far) + 1),
        out_specs=[anywhere] * len(far),
        out_shape=[shape(*expert_weights.shape)] * len(far),
        input_output_aliases={at + 1: at for at in range(len(far))},
        compiler_params=params(),
        cost_estimate=cost(10**11, 10**8),
    )(token, *arriving)
    last = [swap(value, 1) for value in arrived]
    partial, far_pairs = pl.pallas_call(
        lambda *refs: far_kernel(groups, *refs),
        in_specs=[pl.BlockSpec()] * 3 + [anywhere] * len(far),
        out_shape=(shape(rows_here, 3 * hidden_units, kind=F32), shape(len(far), owned, wide)),
        scratch_shapes=[
            pltpu.VMEM((len(far), owned, hidden_units), BF16),
            pltpu.SemaphoreType.DMA((len(far), 3)),
        ],
        compiler_params=params(rows, grads, *arrived, *arrived),
    )(rows, grads, partial, *arrived)

    acts, back = pl.pallas_call(
        lambda *refs: back_kernel(groups, *refs),
        out_shape=(shape(rows_here, 3 * hidden_units), shape(window, padded, WIDE)),
        scratch_shapes=[pltpu.VMEM((rows_here, model_width), F32)],
        compiler_params=params(rows, grads, partial, near_pairs, far_pairs, *last),
        cost_estimate=cost(10**6, 10**5),
    )(rows, grads, partial, near_pairs, far_pairs, *last)
    returned = lax.all_to_all(back, "expert", split_axis=0, concat_axis=0, tiled=True)

    later = pl.pallas_call(
        token_kernel,
        out_shape=shape(16, 128, kind=F32),
        compiler_params=params(),
        cost_estimate=cost(10**11, 10**8),
    )()
    parts = pl.pallas_call(
        part_kernel,
        in_specs=[pl.BlockSpec()] + [anywhere] * groups,
        out_shape=[shape(rows_here, wide), shape(rows_here, hidden_units)],
        compiler_params=params(acts, acts),
        cost_estimate=cost(10**6, 10**5),
    )(acts, later, *slices[1:])
    every = slices + list(parts) + [swap(part, 1) for part in parts]
    for b in far:
        over = [swap(part, b) for part in parts]
        every += over + [swap(part, 1) for part in over]
    weight_grads = pl.pallas_call(
        lambda *refs: grads_kernel(groups, *refs),
        out_specs=anywhere,
        out_shape=shape(1, 3, owned, hidden_units, kind=F32),
        scratch_shapes=[
            pltpu.VMEM((3, owned, hidden_units), F32),
            pltpu.SemaphoreType.DMA((3,)),
        ],
        compiler_params=params(*every, expert_weights, expert_weights),
        cost_estimate=cost(6 * groups * rows_here * owned * hidden_units, 12 * owned * hidden_units),
    )(*every)

    token_grads = pl.pallas_call(
        combine_kernel,
        out_specs=anywhere,
        out_shape=shape(token_rows, model_width),
        scratch_shapes=[pltpu.VMEM((token_rows, model_width), BF16), pltpu.SemaphoreType.DMA((2,))],
        compiler_params=params(table, back, tokens),
    )(returned, table)
    return (token_grads, weight_grads)


def solution(mesh):
    lines = P(("dp", "expert"), None)
    slabs = P("expert", None, "dp", None)
    return jax.shard_map(
        on_device,
        mesh=mesh,
        in_specs=(lines, lines, lines, lines, slabs),
        out_specs=(lines, slabs),
        check_vma=False,
    )
```

```python
import jax
import jax.numpy as jnp
from jax import lax
from jax.experimental import pallas as pl
from jax.experimental.pallas import tpu as pltpu
from jax.sharding import PartitionSpec as P

SLOTS = 10
WIDE = 512
JOIN = 4
F32 = jnp.float32
BF16 = jnp.bfloat16


def dot(first_op, second_op):
    return jnp.dot(first_op, second_op, preferred_element_type=F32)


def dot_tn(first_op, second_op):
    return lax.dot_general(first_op, second_op, (((0,), (0,)), ((), ())), preferred_element_type=F32)


def dot_nt(first_op, second_op):
    return lax.dot_general(first_op, second_op, (((1,), (1,)), ((), ())), preferred_element_type=F32)


def swap(value, bits):
    return lax.ppermute(value, "dp", [(i, i ^ bits) for i in range(lax.axis_size("dp"))])


def piece_rows(chunks):
    return -(-chunks * SLOTS // 8) * 8


def params(*arrays):
    moved = sum(a.size * a.dtype.itemsize for a in arrays)
    return pltpu.CompilerParams(vmem_limit_bytes=min(56 * 2**20, 6 * 2**20 + 3 * moved // 2))


def cost(flops, moved):
    return pl.CostEstimate(flops=flops, bytes_accessed=moved, transcendentals=0)


def shape(*extent, kind=BF16):
    return jax.ShapeDtypeStruct(extent, kind)


def lower(value, by):
    return jnp.floor((value + 0.5) * (1.0 / by))


def sort_matrix(parts, chunks, transposed):
    padded = piece_rows(chunks)
    wide, tall = JOIN * parts * padded, parts * chunks * JOIN * SLOTS
    extent, axis = ((wide, tall), 0) if transposed else ((tall, wide), 1)
    line = (wide, 1) if transposed else (1, wide)
    place = lax.broadcasted_iota(jnp.int32, line, axis).astype(F32)
    block = lower(place, padded)
    inside = place - block * padded
    source = lower(block, parts)
    part = block - source * parts
    chunk = lower(inside, SLOTS)
    slot = inside - chunk * SLOTS
    target = ((part * chunks + chunk) * JOIN + source) * SLOTS + slot
    target = jnp.where(chunk < chunks, target, -1.0)
    spots = lax.broadcasted_iota(jnp.int32, extent, 1 - axis).astype(F32)
    return jnp.where(spots == target, 1.0, 0.0).astype(BF16)


def table_of(code, values, chunks, padded):
    window, token_rows = code.shape
    spots = lax.broadcasted_iota(jnp.int32, (padded, chunks * token_rows), 0).astype(F32)
    tables = []
    for expert in range(window):
        own = code[expert : expert + 1]
        hit = spots == jnp.concatenate([own + float(SLOTS * c) for c in range(chunks)], axis=1)
        row = []
        for value in values:
            if value is None:
                row.append(jnp.where(hit, 1.0, 0.0))
            else:
                gate = jnp.concatenate([value[expert : expert + 1]] * chunks, axis=1)
                row.append(jnp.where(hit, gate, 0.0))
        tables.append(row)
    return [jnp.concatenate([t[i] for t in tables], axis=0) for i in range(len(values))]


def token_kernel(token_ref):
    token_ref[...] = jnp.zeros_like(token_ref)


def pack_kernel(ids_ref, gates_ref, tokens_ref, grads_ref, _, sent_ref, code_ref):
    token_rows, model_width = tokens_ref.shape
    window = code_ref.shape[0]
    chunks = model_width // WIDE
    padded = piece_rows(chunks)
    above = lax.broadcasted_iota(jnp.int32, (token_rows, token_rows), 0)
    along = lax.broadcasted_iota(jnp.int32, (token_rows, token_rows), 1)
    earlier = jnp.where(above < along, 1.0, 0.0).astype(BF16)
    ids = ids_ref[...]
    gates = gates_ref[...].astype(F32)
    members, chosen = [], []
    for expert in range(window):
        hit = ids == expert
        members.append(jnp.sum(jnp.where(hit, 1.0, 0.0), axis=0, keepdims=True))
        chosen.append(jnp.sum(jnp.where(hit, gates, 0.0), axis=0, keepdims=True))
    members = jnp.concatenate(members, axis=0)
    chosen = jnp.concatenate(chosen, axis=0)
    code = jnp.where(members > 0.0, dot(members.astype(BF16), earlier), -1e6)
    code_ref[...] = code
    table, gated = table_of(code, [None, chosen], chunks, padded)

    def columns(ref):
        return jnp.concatenate([ref[:, c * WIDE : (c + 1) * WIDE] for c in range(chunks)], axis=0)

    rows = dot(table.astype(BF16), columns(tokens_ref))
    grads = dot(gated.astype(BF16), columns(grads_ref))
    for expert in range(window):
        lines = slice(expert * padded, (expert + 1) * padded)
        sent_ref[expert] = jnp.concatenate([rows[lines], grads[lines]], axis=0).astype(BF16)


def table_kernel(chunks, code_ref, table_ref):
    (table,) = table_of(code_ref[...], [None], chunks, piece_rows(chunks))
    table_ref[...] = table.T.astype(BF16)


def part_kernel(acts_ref, local_ref, *refs):
    pair_ref, hidden_ref, near_ref = refs[-3:]
    wide = pair_ref.shape[1]
    pair_ref[...] = acts_ref[:, :wide]
    hidden_ref[...] = acts_ref[:, wide:]
    near_ref[...] = local_ref[:2]


def keep_kernel(*refs):
    pass


def place(source, pair_ref, down_ref, sems, at):
    hidden_units = down_ref.shape[1]
    moves = [
        (source.at[0], pair_ref.at[:, pl.ds(0, hidden_units)]),
        (source.at[1], pair_ref.at[:, pl.ds(hidden_units, hidden_units)]),
        (source.at[2], down_ref),
    ]
    return [
        pltpu.make_async_copy(start, end, sems.at[at, which]) for which, (start, end) in enumerate(moves)
    ]


def partial_kernel(groups, got_ref, own_in, near_in, *refs):
    (out_ref, rows_ref, grads_ref, pair_ref, token_ref), refs = refs[:5], refs[5:]
    slices_refs, (down_ref, sems) = refs[: groups - 1], refs[groups - 1 :]
    copies = [
        copy
        for b, source in enumerate((own_in.at[0], near_in.at[0]))
        for copy in place(source, pair_ref.at[b], down_ref.at[b], sems, b)
    ]
    for copy in copies:
        copy.start()
    token_ref[...] = jnp.zeros_like(token_ref)
    sources, height, _ = got_ref.shape
    model_width = rows_ref.shape[1]
    chunks = model_width // WIDE
    owned = model_width // groups
    joined = sources // JOIN
    tall = JOIN * SLOTS
    blocks = jnp.concatenate(
        [got_ref[q * JOIN : (q + 1) * JOIN].reshape(JOIN * height, WIDE) for q in range(joined)],
        axis=1,
    )
    lines = dot(sort_matrix(2, chunks, False), blocks)

    def gathered(part):
        return jnp.concatenate(
            [
                jnp.concatenate(
                    [
                        lines[
                            (part * chunks + c) * tall : (part * chunks + c + 1) * tall,
                            q * WIDE : (q + 1) * WIDE,
                        ]
                        for c in range(chunks)
                    ],
                    axis=1,
                )
                for q in range(joined)
            ],
            axis=0,
        ).astype(BF16)

    rows_ref[...] = gathered(0)
    grads_ref[...] = gathered(1)
    me = lax.axis_index("dp")
    wide = pair_ref.shape[2]
    for copy in copies:
        copy.wait()
    pair_sum, down_sum = None, None
    for b in range(groups):
        lanes = pl.ds(pl.multiple_of((me ^ b) * owned, 128), owned)
        rows, grads = rows_ref[:, lanes], grads_ref[:, lanes]
        target, first = (slices_refs[0], 2) if b == 0 else (slices_refs[b - 1], 0)
        target[first] = rows
        target[first + 1] = grads
        if b < 2:
            term = dot(rows, pair_ref[b])
            pair_sum = term if pair_sum is None else pair_sum + term
            term = dot(grads, down_ref[b])
            down_sum = term if down_sum is None else down_sum + term
    out_ref[:, :wide] = pair_sum
    out_ref[:, wide:] = down_sum


def lanes_of(owner, owned):
    return pl.ds(pl.multiple_of(owner * owned, 128), owned)


def far_kernel(groups, rows_ref, grads_ref, partial_ref, *refs):
    far = range(2, groups, 2)
    weights_in, (out_ref, pair_ref, down_ref, sems) = refs[: len(far)], refs[len(far) :]
    copies = [
        place(source.at[0], pair_ref.at[at], down_ref.at[at], sems, at)
        for at, source in enumerate(weights_in)
    ]
    for some in copies:
        for copy in some:
            copy.start()
    me = lax.axis_index("dp")
    owned, wide = pair_ref.shape[1:]
    pair_sum, down_sum = partial_ref[:, :wide], partial_ref[:, wide:]
    for at, b in enumerate(far):
        for copy in copies[at]:
            copy.wait()
        lanes = lanes_of(me ^ b, owned)
        pair_sum = pair_sum + dot(rows_ref[:, lanes], pair_ref[at])
        down_sum = down_sum + dot(grads_ref[:, lanes], down_ref[at])
    out_ref[:, :wide] = pair_sum
    out_ref[:, wide:] = down_sum


def back_kernel(groups, rows_ref, grads_ref, partial_ref, near_ref, far_ref, *refs):
    last_refs, (acts_ref, out_ref, back_ref) = refs[:-3], refs[-3:]
    me = lax.axis_index("dp")
    model_width = grads_ref.shape[1]
    owned = model_width // groups
    chunks = model_width // WIDE
    hidden_units = partial_ref.shape[1] // 3
    wide = 2 * hidden_units

    def lanes(b):
        return lanes_of(me ^ b, owned)

    gate_act = partial_ref[:, :hidden_units]
    up_act = partial_ref[:, hidden_units:wide]
    grad_hidden = partial_ref[:, wide:]
    for at, ref in enumerate(last_refs):
        here = lanes(2 * at + 3)
        gate_act = gate_act + dot(rows_ref[:, here], ref[0, 0])
        up_act = up_act + dot(rows_ref[:, here], ref[0, 1])
        grad_hidden = grad_hidden + dot(grads_ref[:, here], ref[0, 2])
    logistic = jax.nn.sigmoid(gate_act)
    swish_out = gate_act * logistic
    hidden = (swish_out * up_act).astype(BF16)
    grad_up = (grad_hidden * swish_out).astype(BF16)
    grad_gate = (grad_hidden * up_act * logistic * (1.0 + gate_act * (1.0 - logistic))).astype(BF16)
    acts = jnp.concatenate([grad_gate, grad_up], axis=1)
    acts_ref[:, :wide] = acts
    acts_ref[:, wide:] = hidden
    for b in range(groups):
        if b < 2:
            term = dot_nt(acts, near_ref[b])
        elif b % 2 == 0:
            term = dot_nt(acts, far_ref[b // 2 - 1])
        else:
            ref = last_refs[b // 2 - 1]
            term = dot_nt(grad_gate, ref[0, 0]) + dot_nt(grad_up, ref[0, 1])
        back_ref[:, lanes(b)] = term
    tall = JOIN * SLOTS
    joined = grads_ref.shape[0] // tall
    lines = jnp.concatenate(
        [
            jnp.concatenate(
                [
                    back_ref[q * tall : (q + 1) * tall, c * WIDE : (c + 1) * WIDE]
                    for c in range(chunks)
                ],
                axis=0,
            )
            for q in range(joined)
        ],
        axis=1,
    ).astype(BF16)
    blocks = dot(sort_matrix(1, chunks, True), lines)
    height = piece_rows(chunks)
    for q in range(joined):
        for j in range(JOIN):
            part = blocks[j * height : (j + 1) * height, q * WIDE : (q + 1) * WIDE]
            out_ref[q * JOIN + j] = part.astype(BF16)


def combine_kernel(returned_ref, table_ref, out_ref, held_ref, sems):
    token_rows, model_width = held_ref.shape
    window, height, _ = returned_ref.shape
    lines = returned_ref[...].astype(F32).reshape(window * height, WIDE).astype(BF16)
    parts = sems.shape[0]
    chunks = model_width // WIDE // parts
    copies = []
    for part in range(parts):
        table = table_ref[part * chunks * token_rows : (part + 1) * chunks * token_rows]
        result = dot(table, lines).astype(BF16)
        for c in range(chunks):
            at = part * chunks + c
            held_ref[:, at * WIDE : (at + 1) * WIDE] = result[c * token_rows : (c + 1) * token_rows]
        lanes = pl.ds(part * chunks * WIDE, chunks * WIDE)
        copies.append(
            pltpu.make_async_copy(held_ref.at[:, lanes], out_ref.at[:, lanes], sems.at[part])
        )
        copies[-1].start()
    for copy in copies:
        copy.wait()


def grads_kernel(groups, *refs):
    slices_refs, acts_refs, (out_ref, held_ref, sems) = refs[:groups], refs[groups:-3], refs[-3:]
    hidden_units = out_ref.shape[3]
    copies = [pltpu.make_async_copy(held_ref.at[at], out_ref.at[0, at], sems.at[at]) for at in range(3)]
    rows_here = acts_refs[0].shape[0]
    step = max(1, min(groups, 640 // rows_here))
    for at in range(3):
        lanes = slice(at * hidden_units, (at + 1) * hidden_units)
        kind = 0 if at < 2 else 1
        places = [kind + 2 if b == 0 else kind for b in range(groups)]
        total = None
        for first in range(0, groups, step):
            some = range(first, first + step)
            rows = jnp.concatenate([slices_refs[b][places[b]] for b in some], axis=0)
            acts = jnp.concatenate(
                [
                    acts_refs[2 * b][:, lanes] if at < 2 else acts_refs[2 * b + 1][...]
                    for b in some
                ],
                axis=0,
            )
            term = dot_tn(rows, acts)
            total = term if total is None else total + term
        held_ref[at] = total
        copies[at].start()
    for copy in copies:
        copy.wait()


def on_device(tokens, out_grad, expert_ids, gates, expert_weights):
    window = lax.axis_size("expert")
    groups = lax.axis_size("dp")
    token_rows, model_width = tokens.shape
    hidden_units = expert_weights.shape[3]
    owned = model_width // groups
    chunks = model_width // WIDE
    padded = piece_rows(chunks)
    rows_here = window * SLOTS
    wide = 2 * hidden_units
    anywhere = pl.BlockSpec(memory_space=pl.ANY)

    far = list(range(2, groups, 2))
    token = pl.pallas_call(
        token_kernel,
        out_shape=shape(8, 128, kind=F32),
        compiler_params=params(),
        cost_estimate=cost(10**11, 10**8),
    )()
    arriving = [swap(expert_weights, b) for b in far]
    near = swap(expert_weights, 1)

    ids_t, gates_t = expert_ids.T, gates.T
    sent, code = pl.pallas_call(
        pack_kernel,
        out_shape=(
            shape(window, 2 * padded, WIDE),
            shape(window, token_rows, kind=F32),
        ),
        compiler_params=params(tokens, out_grad),
    )(ids_t, gates_t, tokens, out_grad, token)

    got = lax.all_to_all(sent, "expert", split_axis=0, concat_axis=0, tiled=True)
    table = pl.pallas_call(
        lambda *refs: table_kernel(chunks, *refs),
        out_shape=shape(chunks * token_rows, window * padded),
        compiler_params=params(),
        cost_estimate=cost(10**6, 10**5),
    )(code)

    outs = pl.pallas_call(
        lambda *refs: partial_kernel(groups, *refs),
        in_specs=[pl.BlockSpec()] + [anywhere] * 2,
        out_shape=[
            shape(rows_here, 3 * hidden_units, kind=F32),
            shape(rows_here, model_width),
            shape(rows_here, model_width),
            shape(2, owned, wide),
            shape(8, 128, kind=F32),
        ]
        + [shape(4, rows_here, owned)]
        + [shape(2, rows_here, owned)] * (groups - 2),
        scratch_shapes=[
            pltpu.VMEM((2, owned, hidden_units), BF16),
            pltpu.SemaphoreType.DMA((2, 3)),
        ],
        compiler_params=params(got, expert_weights, expert_weights),
    )(got, expert_weights, near)
    partial, rows, grads, near_pairs, token = outs[:5]
    slices = list(outs[5:])
    local, slices = slices[0], [swap(slices[b - 1], b) for b in range(2, groups)]

    arrived = pl.pallas_call(
        keep_kernel,
        in_specs=[anywhere] * (len(far) + 1),
        out_specs=[anywhere] * len(far),
        out_shape=[shape(*expert_weights.shape)] * len(far),
        input_output_aliases={at + 1: at for at in range(len(far))},
        compiler_params=params(),
        cost_estimate=cost(10**11, 10**8),
    )(token, *arriving)
    last = [swap(value, 1) for value in arrived]
    partial, far_pairs = pl.pallas_call(
        lambda *refs: far_kernel(groups, *refs),
        in_specs=[pl.BlockSpec()] * 3 + [anywhere] * len(far),
        out_shape=(shape(rows_here, 3 * hidden_units, kind=F32), shape(len(far), owned, wide)),
        scratch_shapes=[
            pltpu.VMEM((len(far), owned, hidden_units), BF16),
            pltpu.SemaphoreType.DMA((len(far), 3)),
        ],
        compiler_params=params(rows, grads, *arrived, *arrived),
    )(rows, grads, partial, *arrived)

    acts, back = pl.pallas_call(
        lambda *refs: back_kernel(groups, *refs),
        out_shape=(shape(rows_here, 3 * hidden_units), shape(window, padded, WIDE)),
        scratch_shapes=[pltpu.VMEM((rows_here, model_width), F32)],
        compiler_params=params(rows, grads, partial, near_pairs, far_pairs, *last),
        cost_estimate=cost(10**6, 10**5),
    )(rows, grads, partial, near_pairs, far_pairs, *last)
    returned = lax.all_to_all(back, "expert", split_axis=0, concat_axis=0, tiled=True)

    later = pl.pallas_call(
        token_kernel,
        out_shape=shape(16, 128, kind=F32),
        compiler_params=params(),
        cost_estimate=cost(10**11, 10**8),
    )()
    *parts, beside = pl.pallas_call(
        part_kernel,
        in_specs=[pl.BlockSpec()] * 2 + [anywhere] * (groups - 1),
        out_shape=[
            shape(rows_here, wide),
            shape(rows_here, hidden_units),
            shape(2, rows_here, owned),
        ],
        compiler_params=params(acts, acts, local),
        cost_estimate=cost(10**6, 10**5),
    )(acts, local, later, *slices)
    every = [local, swap(beside, 1)] + slices + parts + [swap(part, 1) for part in parts]
    for b in far:
        over = [swap(part, b) for part in parts]
        every += over + [swap(part, 1) for part in over]
    weight_grads = pl.pallas_call(
        lambda *refs: grads_kernel(groups, *refs),
        out_specs=anywhere,
        out_shape=shape(1, 3, owned, hidden_units, kind=F32),
        scratch_shapes=[
            pltpu.VMEM((3, owned, hidden_units), F32),
            pltpu.SemaphoreType.DMA((3,)),
        ],
        compiler_params=params(*every, expert_weights, expert_weights),
        cost_estimate=cost(6 * groups * rows_here * owned * hidden_units, 12 * owned * hidden_units),
    )(*every)

    token_grads = pl.pallas_call(
        combine_kernel,
        out_specs=anywhere,
        out_shape=shape(token_rows, model_width),
        scratch_shapes=[pltpu.VMEM((token_rows, model_width), BF16), pltpu.SemaphoreType.DMA((2,))],
        compiler_params=params(table, back, tokens),
    )(returned, table)
    return (token_grads, weight_grads)


def solution(mesh):
    lines = P(("dp", "expert"), None)
    slabs = P("expert", None, "dp", None)
    return jax.shard_map(
        on_device,
        mesh=mesh,
        in_specs=(lines, lines, lines, lines, slabs),
        out_specs=(lines, slabs),
        check_vma=False,
    )
```

```python
import jax
import jax.numpy as jnp
from jax import lax
from jax.experimental import pallas as pl
from jax.experimental.pallas import tpu as pltpu
from jax.sharding import PartitionSpec as P

SLOTS = 10
WIDE = 512
JOIN = 4
F32 = jnp.float32
BF16 = jnp.bfloat16


def dot(first_op, second_op):
    return jnp.dot(first_op, second_op, preferred_element_type=F32)


def dot_tn(first_op, second_op):
    return lax.dot_general(first_op, second_op, (((0,), (0,)), ((), ())), preferred_element_type=F32)


def dot_nt(first_op, second_op):
    return lax.dot_general(first_op, second_op, (((1,), (1,)), ((), ())), preferred_element_type=F32)


def swap(value, bits):
    return lax.ppermute(value, "dp", [(i, i ^ bits) for i in range(lax.axis_size("dp"))])


def piece_rows(chunks):
    return -(-chunks * SLOTS // 8) * 8


def params(*arrays):
    moved = sum(a.size * a.dtype.itemsize for a in arrays)
    return pltpu.CompilerParams(vmem_limit_bytes=min(56 * 2**20, 6 * 2**20 + 3 * moved // 2))


def cost(flops, moved):
    return pl.CostEstimate(flops=flops, bytes_accessed=moved, transcendentals=0)


def shape(*extent, kind=BF16):
    return jax.ShapeDtypeStruct(extent, kind)


def lower(value, by):
    return jnp.floor((value + 0.5) * (1.0 / by))


def sort_matrix(parts, chunks, transposed):
    padded = piece_rows(chunks)
    wide, tall = JOIN * parts * padded, parts * chunks * JOIN * SLOTS
    extent, axis = ((wide, tall), 0) if transposed else ((tall, wide), 1)
    line = (wide, 1) if transposed else (1, wide)
    place = lax.broadcasted_iota(jnp.int32, line, axis).astype(F32)
    block = lower(place, padded)
    inside = place - block * padded
    source = lower(block, parts)
    part = block - source * parts
    chunk = lower(inside, SLOTS)
    slot = inside - chunk * SLOTS
    target = ((part * chunks + chunk) * JOIN + source) * SLOTS + slot
    target = jnp.where(chunk < chunks, target, -1.0)
    spots = lax.broadcasted_iota(jnp.int32, extent, 1 - axis).astype(F32)
    return jnp.where(spots == target, 1.0, 0.0).astype(BF16)


def table_of(code, values, chunks, padded):
    window, token_rows = code.shape
    spots = lax.broadcasted_iota(jnp.int32, (padded, chunks * token_rows), 0).astype(F32)
    tables = []
    for expert in range(window):
        own = code[expert : expert + 1]
        hit = spots == jnp.concatenate([own + float(SLOTS * c) for c in range(chunks)], axis=1)
        row = []
        for value in values:
            if value is None:
                row.append(jnp.where(hit, 1.0, 0.0))
            else:
                gate = jnp.concatenate([value[expert : expert + 1]] * chunks, axis=1)
                row.append(jnp.where(hit, gate, 0.0))
        tables.append(row)
    return [jnp.concatenate([t[i] for t in tables], axis=0) for i in range(len(values))]


def token_kernel(token_ref):
    token_ref[...] = jnp.zeros_like(token_ref)


def pack_kernel(ids_ref, gates_ref, tokens_ref, grads_ref, _, sent_ref, code_ref):
    token_rows, model_width = tokens_ref.shape
    window = code_ref.shape[0]
    chunks = model_width // WIDE
    padded = piece_rows(chunks)
    above = lax.broadcasted_iota(jnp.int32, (token_rows, token_rows), 0)
    along = lax.broadcasted_iota(jnp.int32, (token_rows, token_rows), 1)
    earlier = jnp.where(above < along, 1.0, 0.0).astype(BF16)
    ids = ids_ref[...]
    gates = gates_ref[...].astype(F32)
    members, chosen = [], []
    for expert in range(window):
        hit = ids == expert
        members.append(jnp.sum(jnp.where(hit, 1.0, 0.0), axis=0, keepdims=True))
        chosen.append(jnp.sum(jnp.where(hit, gates, 0.0), axis=0, keepdims=True))
    members = jnp.concatenate(members, axis=0)
    chosen = jnp.concatenate(chosen, axis=0)
    code = jnp.where(members > 0.0, dot(members.astype(BF16), earlier), -1e6)
    code_ref[...] = code
    table, gated = table_of(code, [None, chosen], chunks, padded)

    def columns(ref):
        return jnp.concatenate([ref[:, c * WIDE : (c + 1) * WIDE] for c in range(chunks)], axis=0)

    rows = dot(table.astype(BF16), columns(tokens_ref))
    grads = dot(gated.astype(BF16), columns(grads_ref))
    for expert in range(window):
        lines = slice(expert * padded, (expert + 1) * padded)
        sent_ref[expert] = jnp.concatenate([rows[lines], grads[lines]], axis=0).astype(BF16)


def table_kernel(chunks, code_ref, table_ref):
    (table,) = table_of(code_ref[...], [None], chunks, piece_rows(chunks))
    table_ref[...] = table.T.astype(BF16)


def part_kernel(acts_ref, local_ref, *refs):
    pair_ref, hidden_ref, near_ref = refs[-3:]
    wide = pair_ref.shape[1]
    pair_ref[...] = acts_ref[:, :wide]
    hidden_ref[...] = acts_ref[:, wide:]
    near_ref[...] = local_ref[:2]


def keep_kernel(*refs):
    pass


def place(source, pair_ref, down_ref, sems, at):
    hidden_units = down_ref.shape[1]
    moves = [
        (source.at[0], pair_ref.at[:, pl.ds(0, hidden_units)]),
        (source.at[1], pair_ref.at[:, pl.ds(hidden_units, hidden_units)]),
        (source.at[2], down_ref),
    ]
    return [
        pltpu.make_async_copy(start, end, sems.at[at, which]) for which, (start, end) in enumerate(moves)
    ]


def partial_kernel(groups, got_ref, own_in, near_in, *refs):
    (out_ref, rows_ref, grads_ref, pair_ref, token_ref), refs = refs[:5], refs[5:]
    slices_refs, (down_ref, sems) = refs[: groups - 1], refs[groups - 1 :]
    copies = [
        copy
        for b, source in enumerate((own_in.at[0], near_in.at[0]))
        for copy in place(source, pair_ref.at[b], down_ref.at[b], sems, b)
    ]
    for copy in copies:
        copy.start()
    token_ref[...] = jnp.zeros_like(token_ref)
    sources, height, _ = got_ref.shape
    model_width = rows_ref.shape[1]
    chunks = model_width // WIDE
    owned = model_width // groups
    joined = sources // JOIN
    tall = JOIN * SLOTS
    blocks = jnp.concatenate(
        [got_ref[q * JOIN : (q + 1) * JOIN].reshape(JOIN * height, WIDE) for q in range(joined)],
        axis=1,
    )
    lines = dot(sort_matrix(2, chunks, False), blocks)

    def gathered(part):
        return jnp.concatenate(
            [
                jnp.concatenate(
                    [
                        lines[
                            (part * chunks + c) * tall : (part * chunks + c + 1) * tall,
                            q * WIDE : (q + 1) * WIDE,
                        ]
                        for c in range(chunks)
                    ],
                    axis=1,
                )
                for q in range(joined)
            ],
            axis=0,
        ).astype(BF16)

    rows_ref[...] = gathered(0)
    grads_ref[...] = gathered(1)
    me = lax.axis_index("dp")
    wide = pair_ref.shape[2]
    for copy in copies:
        copy.wait()
    pair_sum, down_sum = None, None
    for b in range(groups):
        lanes = pl.ds(pl.multiple_of((me ^ b) * owned, 128), owned)
        rows, grads = rows_ref[:, lanes], grads_ref[:, lanes]
        target, first = (slices_refs[0], 2) if b == 0 else (slices_refs[b - 1], 0)
        target[first] = rows
        target[first + 1] = grads
        if b < 2:
            term = dot(rows, pair_ref[b])
            pair_sum = term if pair_sum is None else pair_sum + term
            term = dot(grads, down_ref[b])
            down_sum = term if down_sum is None else down_sum + term
    out_ref[:, :wide] = pair_sum
    out_ref[:, wide:] = down_sum


def lanes_of(owner, owned):
    return pl.ds(pl.multiple_of(owner * owned, 128), owned)


def far_kernel(groups, rows_ref, grads_ref, partial_ref, *refs):
    far = range(2, groups, 2)
    weights_in, (out_ref, pair_ref, down_ref, sems) = refs[: len(far)], refs[len(far) :]
    copies = [
        place(source.at[0], pair_ref.at[at], down_ref.at[at], sems, at)
        for at, source in enumerate(weights_in)
    ]
    for some in copies:
        for copy in some:
            copy.start()
    me = lax.axis_index("dp")
    owned, wide = pair_ref.shape[1:]
    pair_sum, down_sum = partial_ref[:, :wide], partial_ref[:, wide:]
    for at, b in enumerate(far):
        for copy in copies[at]:
            copy.wait()
        lanes = lanes_of(me ^ b, owned)
        pair_sum = pair_sum + dot(rows_ref[:, lanes], pair_ref[at])
        down_sum = down_sum + dot(grads_ref[:, lanes], down_ref[at])
    out_ref[:, :wide] = pair_sum
    out_ref[:, wide:] = down_sum


def back_kernel(groups, rows_ref, grads_ref, partial_ref, near_ref, far_ref, *refs):
    last_refs, (acts_ref, out_ref, back_ref) = refs[:-3], refs[-3:]
    me = lax.axis_index("dp")
    model_width = grads_ref.shape[1]
    owned = model_width // groups
    chunks = model_width // WIDE
    hidden_units = partial_ref.shape[1] // 3
    wide = 2 * hidden_units

    def lanes(b):
        return lanes_of(me ^ b, owned)

    gate_act = partial_ref[:, :hidden_units]
    up_act = partial_ref[:, hidden_units:wide]
    grad_hidden = partial_ref[:, wide:]
    for at, ref in enumerate(last_refs):
        here = lanes(2 * at + 3)
        gate_act = gate_act + dot(rows_ref[:, here], ref[0, 0])
        up_act = up_act + dot(rows_ref[:, here], ref[0, 1])
        grad_hidden = grad_hidden + dot(grads_ref[:, here], ref[0, 2])
    logistic = jax.nn.sigmoid(gate_act)
    swish_out = gate_act * logistic
    hidden = (swish_out * up_act).astype(BF16)
    grad_up = (grad_hidden * swish_out).astype(BF16)
    grad_gate = (grad_hidden * up_act * logistic * (1.0 + gate_act * (1.0 - logistic))).astype(BF16)
    acts = jnp.concatenate([grad_gate, grad_up], axis=1)
    acts_ref[:, :wide] = acts
    acts_ref[:, wide:] = hidden
    for b in range(groups):
        if b < 2:
            term = dot_nt(acts, near_ref[b])
        elif b % 2 == 0:
            term = dot_nt(acts, far_ref[b // 2 - 1])
        else:
            ref = last_refs[b // 2 - 1]
            term = dot_nt(grad_gate, ref[0, 0]) + dot_nt(grad_up, ref[0, 1])
        back_ref[:, lanes(b)] = term
    tall = JOIN * SLOTS
    joined = grads_ref.shape[0] // tall
    lines = jnp.concatenate(
        [
            jnp.concatenate(
                [
                    back_ref[q * tall : (q + 1) * tall, c * WIDE : (c + 1) * WIDE]
                    for c in range(chunks)
                ],
                axis=0,
            )
            for q in range(joined)
        ],
        axis=1,
    ).astype(BF16)
    blocks = dot(sort_matrix(1, chunks, True), lines)
    height = piece_rows(chunks)
    for q in range(joined):
        for j in range(JOIN):
            part = blocks[j * height : (j + 1) * height, q * WIDE : (q + 1) * WIDE]
            out_ref[q * JOIN + j] = part.astype(BF16)


def combine_kernel(returned_ref, table_ref, out_ref, held_ref, sems):
    token_rows, model_width = held_ref.shape
    lines = returned_ref[...]
    parts = sems.shape[0]
    chunks = model_width // WIDE // parts
    copies = []
    for part in range(parts):
        table = table_ref[part * chunks * token_rows : (part + 1) * chunks * token_rows]
        result = dot(table, lines).astype(BF16)
        for c in range(chunks):
            at = part * chunks + c
            held_ref[:, at * WIDE : (at + 1) * WIDE] = result[c * token_rows : (c + 1) * token_rows]
        lanes = pl.ds(part * chunks * WIDE, chunks * WIDE)
        copies.append(
            pltpu.make_async_copy(held_ref.at[:, lanes], out_ref.at[:, lanes], sems.at[part])
        )
        copies[-1].start()
    for copy in copies:
        copy.wait()


def grads_kernel(groups, *refs):
    slices_refs, acts_refs, (out_ref, held_ref, sems) = refs[:groups], refs[groups:-3], refs[-3:]
    hidden_units = out_ref.shape[3]
    copies = [pltpu.make_async_copy(held_ref.at[at], out_ref.at[0, at], sems.at[at]) for at in range(3)]
    rows_here = acts_refs[0].shape[0]
    step = max(1, min(groups, 640 // rows_here))
    for at in range(3):
        lanes = slice(at * hidden_units, (at + 1) * hidden_units)
        kind = 0 if at < 2 else 1
        places = [kind + 2 if b == 0 else kind for b in range(groups)]
        total = None
        for first in range(0, groups, step):
            some = range(first, first + step)
            rows = jnp.concatenate([slices_refs[b][places[b]] for b in some], axis=0)
            acts = jnp.concatenate(
                [
                    acts_refs[2 * b][:, lanes] if at < 2 else acts_refs[2 * b + 1][...]
                    for b in some
                ],
                axis=0,
            )
            term = dot_tn(rows, acts)
            total = term if total is None else total + term
        held_ref[at] = total
        copies[at].start()
    for copy in copies:
        copy.wait()


def on_device(tokens, out_grad, expert_ids, gates, expert_weights):
    window = lax.axis_size("expert")
    groups = lax.axis_size("dp")
    token_rows, model_width = tokens.shape
    hidden_units = expert_weights.shape[3]
    owned = model_width // groups
    chunks = model_width // WIDE
    padded = piece_rows(chunks)
    rows_here = window * SLOTS
    wide = 2 * hidden_units
    anywhere = pl.BlockSpec(memory_space=pl.ANY)

    far = list(range(2, groups, 2))
    token = pl.pallas_call(
        token_kernel,
        out_shape=shape(8, 128, kind=F32),
        compiler_params=params(),
        cost_estimate=cost(10**11, 10**8),
    )()
    arriving = [swap(expert_weights, b) for b in far]
    near = swap(expert_weights, 1)

    ids_t, gates_t = expert_ids.T, gates.T
    sent, code = pl.pallas_call(
        pack_kernel,
        out_shape=(
            shape(window, 2 * padded, WIDE),
            shape(window, token_rows, kind=F32),
        ),
        compiler_params=params(tokens, out_grad),
    )(ids_t, gates_t, tokens, out_grad, token)

    got = lax.all_to_all(sent, "expert", split_axis=0, concat_axis=0, tiled=True)
    table = pl.pallas_call(
        lambda *refs: table_kernel(chunks, *refs),
        out_shape=shape(chunks * token_rows, window * padded),
        compiler_params=params(),
        cost_estimate=cost(10**6, 10**5),
    )(code)

    outs = pl.pallas_call(
        lambda *refs: partial_kernel(groups, *refs),
        in_specs=[pl.BlockSpec()] + [anywhere] * 2,
        out_shape=[
            shape(rows_here, 3 * hidden_units, kind=F32),
            shape(rows_here, model_width),
            shape(rows_here, model_width),
            shape(2, owned, wide),
            shape(8, 128, kind=F32),
        ]
        + [shape(4, rows_here, owned)]
        + [shape(2, rows_here, owned)] * (groups - 2),
        scratch_shapes=[
            pltpu.VMEM((2, owned, hidden_units), BF16),
            pltpu.SemaphoreType.DMA((2, 3)),
        ],
        compiler_params=params(got, expert_weights, expert_weights),
    )(got, expert_weights, near)
    partial, rows, grads, near_pairs, token = outs[:5]
    slices = list(outs[5:])
    local, slices = slices[0], [swap(slices[b - 1], b) for b in range(2, groups)]

    arrived = pl.pallas_call(
        keep_kernel,
        in_specs=[anywhere] * (len(far) + 1),
        out_specs=[anywhere] * len(far),
        out_shape=[shape(*expert_weights.shape)] * len(far),
        input_output_aliases={at + 1: at for at in range(len(far))},
        compiler_params=params(),
        cost_estimate=cost(10**11, 10**8),
    )(token, *arriving)
    last = [swap(value, 1) for value in arrived]
    partial, far_pairs = pl.pallas_call(
        lambda *refs: far_kernel(groups, *refs),
        in_specs=[pl.BlockSpec()] * 3 + [anywhere] * len(far),
        out_shape=(shape(rows_here, 3 * hidden_units, kind=F32), shape(len(far), owned, wide)),
        scratch_shapes=[
            pltpu.VMEM((len(far), owned, hidden_units), BF16),
            pltpu.SemaphoreType.DMA((len(far), 3)),
        ],
        compiler_params=params(rows, grads, *arrived, *arrived),
    )(rows, grads, partial, *arrived)

    acts, back = pl.pallas_call(
        lambda *refs: back_kernel(groups, *refs),
        out_shape=(shape(rows_here, 3 * hidden_units), shape(window, padded, WIDE)),
        scratch_shapes=[pltpu.VMEM((rows_here, model_width), F32)],
        compiler_params=params(rows, grads, partial, near_pairs, far_pairs, *last),
        cost_estimate=cost(10**6, 10**5),
    )(rows, grads, partial, near_pairs, far_pairs, *last)
    returned = lax.all_to_all(back, "expert", split_axis=0, concat_axis=0, tiled=True)

    later = pl.pallas_call(
        token_kernel,
        out_shape=shape(16, 128, kind=F32),
        compiler_params=params(),
        cost_estimate=cost(10**11, 10**8),
    )()
    *parts, beside = pl.pallas_call(
        part_kernel,
        in_specs=[pl.BlockSpec()] * 2 + [anywhere] * (groups - 1),
        out_shape=[
            shape(rows_here, wide),
            shape(rows_here, hidden_units),
            shape(2, rows_here, owned),
        ],
        compiler_params=params(acts, acts, local),
        cost_estimate=cost(10**6, 10**5),
    )(acts, local, later, *slices)
    every = [local, swap(beside, 1)] + slices + parts + [swap(part, 1) for part in parts]
    for b in far:
        over = [swap(part, b) for part in parts]
        every += over + [swap(part, 1) for part in over]
    weight_grads = pl.pallas_call(
        lambda *refs: grads_kernel(groups, *refs),
        out_specs=anywhere,
        out_shape=shape(1, 3, owned, hidden_units, kind=F32),
        scratch_shapes=[
            pltpu.VMEM((3, owned, hidden_units), F32),
            pltpu.SemaphoreType.DMA((3,)),
        ],
        compiler_params=params(*every, expert_weights, expert_weights),
        cost_estimate=cost(6 * groups * rows_here * owned * hidden_units, 12 * owned * hidden_units),
    )(*every)

    token_grads = pl.pallas_call(
        combine_kernel,
        out_specs=anywhere,
        out_shape=shape(token_rows, model_width),
        scratch_shapes=[pltpu.VMEM((token_rows, model_width), BF16), pltpu.SemaphoreType.DMA((2,))],
        compiler_params=params(table, back, tokens),
    )(returned.reshape(window * padded, WIDE), table)
    return (token_grads, weight_grads)


def solution(mesh):
    lines = P(("dp", "expert"), None)
    slabs = P("expert", None, "dp", None)
    return jax.shard_map(
        on_device,
        mesh=mesh,
        in_specs=(lines, lines, lines, lines, slabs),
        out_specs=(lines, slabs),
        check_vma=False,
    )
```

```python
import jax
import jax.numpy as jnp
from jax import lax
from jax.experimental import pallas as pl
from jax.experimental.pallas import tpu as pltpu
from jax.sharding import PartitionSpec as P

SLOTS = 10
WIDE = 512
JOIN = 4
F32 = jnp.float32
BF16 = jnp.bfloat16


def dot(first_op, second_op):
    return jnp.dot(first_op, second_op, preferred_element_type=F32)


def dot_tn(first_op, second_op):
    return lax.dot_general(first_op, second_op, (((0,), (0,)), ((), ())), preferred_element_type=F32)


def dot_nt(first_op, second_op):
    return lax.dot_general(first_op, second_op, (((1,), (1,)), ((), ())), preferred_element_type=F32)


def swap(value, bits):
    return lax.ppermute(value, "dp", [(i, i ^ bits) for i in range(lax.axis_size("dp"))])


def piece_rows(chunks):
    return -(-chunks * SLOTS // 8) * 8


def params(*arrays):
    moved = sum(a.size * a.dtype.itemsize for a in arrays)
    return pltpu.CompilerParams(vmem_limit_bytes=min(56 * 2**20, 6 * 2**20 + 3 * moved // 2))


def cost(flops, moved):
    return pl.CostEstimate(flops=flops, bytes_accessed=moved, transcendentals=0)


def shape(*extent, kind=BF16):
    return jax.ShapeDtypeStruct(extent, kind)


def lower(value, by):
    return jnp.floor((value + 0.5) * (1.0 / by))


def sort_matrix(parts, chunks, transposed):
    padded = piece_rows(chunks)
    wide, tall = JOIN * parts * padded, parts * chunks * JOIN * SLOTS
    extent, axis = ((wide, tall), 0) if transposed else ((tall, wide), 1)
    line = (wide, 1) if transposed else (1, wide)
    place = lax.broadcasted_iota(jnp.int32, line, axis).astype(F32)
    block = lower(place, padded)
    inside = place - block * padded
    source = lower(block, parts)
    part = block - source * parts
    chunk = lower(inside, SLOTS)
    slot = inside - chunk * SLOTS
    target = ((part * chunks + chunk) * JOIN + source) * SLOTS + slot
    target = jnp.where(chunk < chunks, target, -1.0)
    spots = lax.broadcasted_iota(jnp.int32, extent, 1 - axis).astype(F32)
    return jnp.where(spots == target, 1.0, 0.0).astype(BF16)


def table_of(code, values, chunks, padded):
    window, token_rows = code.shape
    spots = lax.broadcasted_iota(jnp.int32, (padded, chunks * token_rows), 0).astype(F32)
    tables = []
    for expert in range(window):
        own = code[expert : expert + 1]
        hit = spots == jnp.concatenate([own + float(SLOTS * c) for c in range(chunks)], axis=1)
        row = []
        for value in values:
            if value is None:
                row.append(jnp.where(hit, 1.0, 0.0))
            else:
                gate = jnp.concatenate([value[expert : expert + 1]] * chunks, axis=1)
                row.append(jnp.where(hit, gate, 0.0))
        tables.append(row)
    return [jnp.concatenate([t[i] for t in tables], axis=0) for i in range(len(values))]


def token_kernel(token_ref):
    token_ref[...] = jnp.zeros_like(token_ref)


def pack_kernel(ids_ref, gates_ref, tokens_ref, grads_ref, _, sent_ref, code_ref):
    token_rows, model_width = tokens_ref.shape
    window = code_ref.shape[0]
    chunks = model_width // WIDE
    padded = piece_rows(chunks)
    above = lax.broadcasted_iota(jnp.int32, (token_rows, token_rows), 0)
    along = lax.broadcasted_iota(jnp.int32, (token_rows, token_rows), 1)
    earlier = jnp.where(above < along, 1.0, 0.0).astype(BF16)
    ids = ids_ref[...]
    gates = gates_ref[...].astype(F32)
    members, chosen = [], []
    for expert in range(window):
        hit = ids == expert
        members.append(jnp.sum(jnp.where(hit, 1.0, 0.0), axis=0, keepdims=True))
        chosen.append(jnp.sum(jnp.where(hit, gates, 0.0), axis=0, keepdims=True))
    members = jnp.concatenate(members, axis=0)
    chosen = jnp.concatenate(chosen, axis=0)
    code = jnp.where(members > 0.0, dot(members.astype(BF16), earlier), -1e6)
    code_ref[...] = code
    table, gated = table_of(code, [None, chosen], chunks, padded)

    def columns(ref):
        return jnp.concatenate([ref[:, c * WIDE : (c + 1) * WIDE] for c in range(chunks)], axis=0)

    rows = dot(table.astype(BF16), columns(tokens_ref))
    grads = dot(gated.astype(BF16), columns(grads_ref))
    for expert in range(window):
        lines = slice(expert * padded, (expert + 1) * padded)
        sent_ref[expert] = jnp.concatenate([rows[lines], grads[lines]], axis=0).astype(BF16)


def table_kernel(chunks, code_ref, table_ref):
    (table,) = table_of(code_ref[...], [None], chunks, piece_rows(chunks))
    table_ref[...] = table.T.astype(BF16)


def part_kernel(acts_ref, local_ref, *refs):
    pair_ref, hidden_ref, near_ref = refs[-3:]
    wide = pair_ref.shape[1]
    pair_ref[...] = acts_ref[:, :wide]
    hidden_ref[...] = acts_ref[:, wide:]
    near_ref[...] = local_ref[:2]


def keep_kernel(*refs):
    pass


def place(source, pair_ref, down_ref, sems, at):
    hidden_units = down_ref.shape[1]
    moves = [
        (source.at[0], pair_ref.at[:, pl.ds(0, hidden_units)]),
        (source.at[1], pair_ref.at[:, pl.ds(hidden_units, hidden_units)]),
        (source.at[2], down_ref),
    ]
    return [
        pltpu.make_async_copy(start, end, sems.at[at, which]) for which, (start, end) in enumerate(moves)
    ]


def partial_kernel(groups, got_ref, own_in, near_in, *refs):
    (out_ref, rows_ref, grads_ref, pair_ref, token_ref), refs = refs[:5], refs[5:]
    slices_refs, (down_ref, sems) = refs[: groups - 1], refs[groups - 1 :]
    copies = [
        copy
        for b, source in enumerate((own_in.at[0], near_in.at[0]))
        for copy in place(source, pair_ref.at[b], down_ref.at[b], sems, b)
    ]
    for copy in copies:
        copy.start()
    token_ref[...] = jnp.zeros_like(token_ref)
    sources, height, _ = got_ref.shape
    model_width = rows_ref.shape[1]
    chunks = model_width // WIDE
    owned = model_width // groups
    joined = sources // JOIN
    tall = JOIN * SLOTS
    blocks = jnp.concatenate(
        [got_ref[q * JOIN : (q + 1) * JOIN].reshape(JOIN * height, WIDE) for q in range(joined)],
        axis=1,
    )
    lines = dot(sort_matrix(2, chunks, False), blocks)

    def gathered(part):
        return jnp.concatenate(
            [
                jnp.concatenate(
                    [
                        lines[
                            (part * chunks + c) * tall : (part * chunks + c + 1) * tall,
                            q * WIDE : (q + 1) * WIDE,
                        ]
                        for c in range(chunks)
                    ],
                    axis=1,
                )
                for q in range(joined)
            ],
            axis=0,
        ).astype(BF16)

    rows_ref[...] = gathered(0)
    grads_ref[...] = gathered(1)
    me = lax.axis_index("dp")
    wide = pair_ref.shape[2]
    for copy in copies:
        copy.wait()
    pair_sum, down_sum = None, None
    for b in range(groups):
        lanes = pl.ds(pl.multiple_of((me ^ b) * owned, 128), owned)
        rows, grads = rows_ref[:, lanes], grads_ref[:, lanes]
        target, first = (slices_refs[0], 2) if b == 0 else (slices_refs[b - 1], 0)
        target[first] = rows
        target[first + 1] = grads
        if b < 2:
            term = dot(rows, pair_ref[b])
            pair_sum = term if pair_sum is None else pair_sum + term
            term = dot(grads, down_ref[b])
            down_sum = term if down_sum is None else down_sum + term
    out_ref[:, :wide] = pair_sum
    out_ref[:, wide:] = down_sum


def lanes_of(owner, owned):
    return pl.ds(pl.multiple_of(owner * owned, 128), owned)


def far_kernel(groups, rows_ref, grads_ref, partial_ref, *refs):
    far = range(2, groups, 2)
    weights_in, (out_ref, pair_ref, down_ref, sems) = refs[: len(far)], refs[len(far) :]
    copies = [
        place(source.at[0], pair_ref.at[at], down_ref.at[at], sems, at)
        for at, source in enumerate(weights_in)
    ]
    for some in copies:
        for copy in some:
            copy.start()
    me = lax.axis_index("dp")
    owned, wide = pair_ref.shape[1:]
    pair_sum, down_sum = partial_ref[:, :wide], partial_ref[:, wide:]
    for at, b in enumerate(far):
        for copy in copies[at]:
            copy.wait()
        lanes = lanes_of(me ^ b, owned)
        pair_sum = pair_sum + dot(rows_ref[:, lanes], pair_ref[at])
        down_sum = down_sum + dot(grads_ref[:, lanes], down_ref[at])
    out_ref[:, :wide] = pair_sum
    out_ref[:, wide:] = down_sum


def back_kernel(groups, rows_ref, grads_ref, partial_ref, near_ref, far_ref, *refs):
    last_refs, (acts_ref, out_ref, back_ref) = refs[:-3], refs[-3:]
    me = lax.axis_index("dp")
    model_width = grads_ref.shape[1]
    owned = model_width // groups
    chunks = model_width // WIDE
    hidden_units = partial_ref.shape[1] // 3
    wide = 2 * hidden_units

    def lanes(b):
        return lanes_of(me ^ b, owned)

    gate_act = partial_ref[:, :hidden_units]
    up_act = partial_ref[:, hidden_units:wide]
    grad_hidden = partial_ref[:, wide:]
    for at, ref in enumerate(last_refs):
        here = lanes(2 * at + 3)
        gate_act = gate_act + dot(rows_ref[:, here], ref[0, 0])
        up_act = up_act + dot(rows_ref[:, here], ref[0, 1])
        grad_hidden = grad_hidden + dot(grads_ref[:, here], ref[0, 2])
    logistic = jax.nn.sigmoid(gate_act)
    swish_out = gate_act * logistic
    hidden = (swish_out * up_act).astype(BF16)
    grad_up = (grad_hidden * swish_out).astype(BF16)
    grad_gate = (grad_hidden * up_act * logistic * (1.0 + gate_act * (1.0 - logistic))).astype(BF16)
    acts = jnp.concatenate([grad_gate, grad_up], axis=1)
    acts_ref[:, :wide] = acts
    acts_ref[:, wide:] = hidden
    for b in range(groups):
        if b < 2:
            term = dot_nt(acts, near_ref[b])
        elif b % 2 == 0:
            term = dot_nt(acts, far_ref[b // 2 - 1])
        else:
            ref = last_refs[b // 2 - 1]
            term = dot_nt(grad_gate, ref[0, 0]) + dot_nt(grad_up, ref[0, 1])
        back_ref[:, lanes(b)] = term
    tall = JOIN * SLOTS
    joined = grads_ref.shape[0] // tall
    lines = jnp.concatenate(
        [
            jnp.concatenate(
                [
                    back_ref[q * tall : (q + 1) * tall, c * WIDE : (c + 1) * WIDE]
                    for c in range(chunks)
                ],
                axis=0,
            )
            for q in range(joined)
        ],
        axis=1,
    ).astype(BF16)
    blocks = dot(sort_matrix(1, chunks, True), lines)
    height = piece_rows(chunks)
    for q in range(joined):
        for j in range(JOIN):
            part = blocks[j * height : (j + 1) * height, q * WIDE : (q + 1) * WIDE]
            out_ref[q * JOIN + j] = part.astype(BF16)


def combine_kernel(returned_ref, table_ref, out_ref, held_ref, sems):
    token_rows, model_width = held_ref.shape
    window, height, _ = returned_ref.shape
    lines = returned_ref[...].astype(F32).reshape(window * height, WIDE).astype(BF16)
    parts = sems.shape[0]
    chunks = model_width // WIDE // parts
    copies = []
    for part in range(parts):
        table = table_ref[part * chunks * token_rows : (part + 1) * chunks * token_rows]
        result = dot(table, lines).astype(BF16)
        for c in range(chunks):
            at = part * chunks + c
            held_ref[:, at * WIDE : (at + 1) * WIDE] = result[c * token_rows : (c + 1) * token_rows]
        lanes = pl.ds(part * chunks * WIDE, chunks * WIDE)
        copies.append(
            pltpu.make_async_copy(held_ref.at[:, lanes], out_ref.at[:, lanes], sems.at[part])
        )
        copies[-1].start()
    for copy in copies:
        copy.wait()


def grads_kernel(groups, *refs):
    slices_refs, acts_refs, (out_ref, held_ref, sems) = refs[:groups], refs[groups:-3], refs[-3:]
    hidden_units = out_ref.shape[3]
    copies = [pltpu.make_async_copy(held_ref.at[at], out_ref.at[0, at], sems.at[at]) for at in range(3)]
    rows_here = acts_refs[0].shape[0]
    step = max(1, min(groups, 640 // rows_here))
    for at in range(3):
        lanes = slice(at * hidden_units, (at + 1) * hidden_units)
        kind = 0 if at < 2 else 1
        places = [kind + 2 if b == 0 else kind for b in range(groups)]
        total = None
        for first in range(0, groups, step):
            some = range(first, first + step)
            rows = jnp.concatenate([slices_refs[b][places[b]] for b in some], axis=0)
            acts = jnp.concatenate(
                [
                    acts_refs[2 * b][:, lanes] if at < 2 else acts_refs[2 * b + 1][...]
                    for b in some
                ],
                axis=0,
            )
            term = dot_tn(rows, acts)
            total = term if total is None else total + term
        held_ref[at] = total
        copies[at].start()
    for copy in copies:
        copy.wait()


def on_device(tokens, out_grad, expert_ids, gates, expert_weights):
    window = lax.axis_size("expert")
    groups = lax.axis_size("dp")
    token_rows, model_width = tokens.shape
    hidden_units = expert_weights.shape[3]
    owned = model_width // groups
    chunks = model_width // WIDE
    padded = piece_rows(chunks)
    rows_here = window * SLOTS
    wide = 2 * hidden_units
    anywhere = pl.BlockSpec(memory_space=pl.ANY)

    far = list(range(2, groups, 2))
    token = pl.pallas_call(
        token_kernel,
        out_shape=shape(8, 128, kind=F32),
        compiler_params=params(),
        cost_estimate=cost(10**11, 10**8),
    )()
    arriving = [swap(expert_weights, b) for b in far]
    near = swap(expert_weights, 1)

    ids_t, gates_t = expert_ids.T, gates.T
    sent, code = pl.pallas_call(
        pack_kernel,
        out_shape=(
            shape(window, 2 * padded, WIDE),
            shape(window, token_rows, kind=F32),
        ),
        compiler_params=params(tokens, out_grad),
    )(ids_t, gates_t, tokens, out_grad, token)

    got = lax.all_to_all(sent, "expert", split_axis=0, concat_axis=0, tiled=True)
    table = pl.pallas_call(
        lambda *refs: table_kernel(chunks, *refs),
        out_shape=shape(chunks * token_rows, window * padded),
        compiler_params=params(),
        cost_estimate=cost(10**6, 10**5),
    )(code)

    outs = pl.pallas_call(
        lambda *refs: partial_kernel(groups, *refs),
        in_specs=[pl.BlockSpec()] + [anywhere] * 2,
        out_shape=[
            shape(rows_here, 3 * hidden_units, kind=F32),
            shape(rows_here, model_width),
            shape(rows_here, model_width),
            shape(2, owned, wide),
            shape(8, 128, kind=F32),
        ]
        + [shape(4, rows_here, owned)]
        + [shape(2, rows_here, owned)] * (groups - 2),
        scratch_shapes=[
            pltpu.VMEM((2, owned, hidden_units), BF16),
            pltpu.SemaphoreType.DMA((2, 3)),
        ],
        compiler_params=params(got, expert_weights, expert_weights),
    )(got, expert_weights, near)
    partial, rows, grads, near_pairs, token = outs[:5]
    slices = list(outs[5:])
    local, slices = slices[0], [swap(slices[b - 1], b) for b in range(2, groups)]

    arrived = pl.pallas_call(
        keep_kernel,
        in_specs=[anywhere] * (len(far) + 1),
        out_specs=[anywhere] * len(far),
        out_shape=[shape(*expert_weights.shape)] * len(far),
        input_output_aliases={at + 1: at for at in range(len(far))},
        compiler_params=params(),
        cost_estimate=cost(10**11, 10**8),
    )(token, *arriving)
    last = [swap(value, 1) for value in arrived]
    partial, far_pairs = pl.pallas_call(
        lambda *refs: far_kernel(groups, *refs),
        in_specs=[pl.BlockSpec()] * 3 + [anywhere] * len(far),
        out_shape=(shape(rows_here, 3 * hidden_units, kind=F32), shape(len(far), owned, wide)),
        scratch_shapes=[
            pltpu.VMEM((len(far), owned, hidden_units), BF16),
            pltpu.SemaphoreType.DMA((len(far), 3)),
        ],
        compiler_params=params(rows, grads, *arrived, *arrived),
    )(rows, grads, partial, *arrived)

    acts, back = pl.pallas_call(
        lambda *refs: back_kernel(groups, *refs),
        out_shape=(shape(rows_here, 3 * hidden_units), shape(window, padded, WIDE)),
        scratch_shapes=[pltpu.VMEM((rows_here, model_width), F32)],
        compiler_params=params(rows, grads, partial, near_pairs, far_pairs, *last),
        cost_estimate=cost(10**6, 10**5),
    )(rows, grads, partial, near_pairs, far_pairs, *last)
    returned = lax.all_to_all(back, "expert", split_axis=0, concat_axis=0, tiled=True)

    later = pl.pallas_call(
        token_kernel,
        out_shape=shape(16, 128, kind=F32),
        compiler_params=params(),
        cost_estimate=cost(10**11, 10**8),
    )()
    *parts, beside = pl.pallas_call(
        part_kernel,
        in_specs=[pl.BlockSpec()] * 2 + [anywhere] * (groups - 1),
        out_shape=[
            shape(rows_here, wide),
            shape(rows_here, hidden_units),
            shape(2, rows_here, owned),
        ],
        compiler_params=params(acts, acts, local),
        cost_estimate=cost(10**6, 10**5),
    )(acts, local, later, *slices)
    every = [local, swap(beside, 1)] + slices + parts + [swap(part, 1) for part in parts]
    for b in far:
        over = [swap(part, b) for part in parts]
        every += over + [swap(part, 1) for part in over]
    weight_grads = pl.pallas_call(
        lambda *refs: grads_kernel(groups, *refs),
        out_specs=anywhere,
        out_shape=shape(1, 3, owned, hidden_units, kind=F32),
        scratch_shapes=[
            pltpu.VMEM((3, owned, hidden_units), F32),
            pltpu.SemaphoreType.DMA((3,)),
        ],
        compiler_params=params(*every, expert_weights, expert_weights),
        cost_estimate=cost(6 * groups * rows_here * owned * hidden_units, 12 * owned * hidden_units),
    )(*every)

    token_grads = pl.pallas_call(
        combine_kernel,
        out_specs=anywhere,
        out_shape=shape(token_rows, model_width),
        scratch_shapes=[pltpu.VMEM((token_rows, model_width), BF16), pltpu.SemaphoreType.DMA((4,))],
        compiler_params=params(table, back, tokens),
    )(returned, table)
    return (token_grads, weight_grads)


def solution(mesh):
    lines = P(("dp", "expert"), None)
    slabs = P("expert", None, "dp", None)
    return jax.shard_map(
        on_device,
        mesh=mesh,
        in_specs=(lines, lines, lines, lines, slabs),
        out_specs=(lines, slabs),
        check_vma=False,
    )
```
